32 devices in a mesh: req: 8 (over y, x, core), row: 4 (over z).
Axes of the slice: x: 2, y: 2, z: 4, core: 2. Of those that a mesh axis runs over, the one named last changes fastest.
Arguments:
- hidden_in: bfloat16 [8, 512, 2304], P('req', 'row'), may hold values from -30 to 30
- cache_len: int32 [8], P('req'), may hold values from 64 to 512, as said below
- new_count: int32 [8], P('req'), may hold values from 128 to 512, as said below
- key_cache: bfloat16 [8, 512, 2304], P('req', 'row'), may hold values from -150 to 150
- value_cache: bfloat16 [8, 512, 2304], P('req', 'row'), may hold values from -6 to 6
- attn_gain: float32 [2304], replicated, may hold values from 0.1 to 1.9
- w_query: bfloat16 [2304, 2304], P('req', 'row'), may hold values from -0.125 to 0.125
- w_key: bfloat16 [2304, 2304], P('req', 'row'), may hold values from -0.125 to 0.125
- w_value: bfloat16 [2304, 2304], P('req', 'row'), may hold values from -0.125 to 0.125
- w_out: bfloat16 [2304, 2304], P('row', 'req'), may hold values from -0.125 to 0.125
- final_gain: float32 [2304], replicated, may hold values from 0.1 to 1.9
- head_weight: bfloat16 [2304, 122880], P(None, ('req', 'row')), may hold values from -60 to 60
Outputs:
- layer_out: bfloat16 [8, 512, 2304], P('req', 'row')
- logprobs: float32 [8, 122880], P(None, ('req', 'row'))
The draws below stay inside these ranges and needn't reach their ends.
Inputs may be any that keep to these rules, and one draw needn't show every extreme that they name: `cache_len`: exactly 1 request, chosen at random, hold between 448 and 512 cached tokens, one of them exactly 512; every other request holds between 64 and 128. `new_count`: one request brings exactly 512 live tokens.
All inputs are finite; a program needn't handle non-finite values.
Results may differ from the reference program's by a relative error of at most 0.0075.
Values may be sent and summed in bfloat16 or wider, within the bound.
No kernel may reach another device: no remote copies, remote signals or barrier semaphores. Data moves between devices by JAX's collectives and lax.ppermute only.
A program may use at most 128 MiB of HBM per device.

```python
import jax
import jax.numpy as jnp
from jax import lax

D = 2304
HEADS = 36
HEAD_DIM = 64
VOCAB = 122880
SPAN = 512
CAP = 512
REQS = 8
LONG = 1


def draw_hidden_in(key, part):
    key_values, key_scale = jax.random.split(jax.random.fold_in(key, 3))
    row_scale = jnp.exp(jax.random.uniform(key_scale, (REQS, SPAN, 1), jnp.float32, jnp.log(0.3), jnp.log(3.0)))
    base_values = jax.random.normal(key_values, (REQS, SPAN, D), jnp.float32)
    return (base_values * row_scale).astype(jnp.bfloat16)


def draw_cache_len(key, part):
    key_order, key_long, key_short = jax.random.split(jax.random.fold_in(key, 5), 3)
    ranking = jax.random.permutation(key_order, REQS)
    long_lengths = jax.random.randint(key_long, (REQS,), CAP - CAP // 8, CAP + 1)
    short_lengths = jax.random.randint(key_short, (REQS,), CAP // 8, CAP // 4 + 1)
    lengths = jnp.where(ranking < LONG, long_lengths, short_lengths)
    return jnp.where(ranking == 0, CAP, lengths).astype(jnp.int32)


def draw_new_count(key, part):
    key_order, key_count = jax.random.split(jax.random.fold_in(key, 7))
    ranking = jax.random.permutation(key_order, REQS)
    counts = jax.random.randint(key_count, (REQS,), SPAN // 4, SPAN + 1)
    return jnp.where(ranking == 0, SPAN, counts).astype(jnp.int32)


def draw_key_cache(key, part):
    key_base = jax.random.fold_in(jax.random.fold_in(key, 11), 0)
    paired = jax.random.normal(key_base, (REQS, CAP // 2, 2, D), jnp.float32)
    return paired.reshape(REQS, CAP, D).astype(jnp.bfloat16)


def draw_head_weight(key, part):
    key_base = jax.random.fold_in(jax.random.fold_in(key, 13), 0)
    key_scale = jax.random.fold_in(jax.random.fold_in(key, 13), 2)
    column = jnp.arange(VOCAB // 2).astype(jnp.float32)
    rising = 1.0 + 0.8 * column / (VOCAB // 2)
    column_scale = jnp.exp(jax.random.uniform(key_scale, (1, VOCAB // 2, 1), jnp.float32, jnp.log(0.5), jnp.log(1.5)))
    column_scale = column_scale * rising[None, :, None] * (3.0 / D ** 0.5)
    paired = jax.random.normal(key_base, (D, VOCAB // 2, 2), jnp.float32) * column_scale
    return paired.reshape(D, VOCAB).astype(jnp.bfloat16)


def steps_of(rng, extent, cuts, low, high):
    loudness = 1.0
    for axis_at, shards_of in cuts:
        draws = jax.random.uniform(jax.random.fold_in(jax.random.fold_in(rng, 6), axis_at), (shards_of,), jnp.float32, low / len(cuts), high / len(cuts))
        loudness = loudness * jnp.repeat(jnp.exp(draws), extent[axis_at] // shards_of).reshape((-1,) + (1,) * (len(extent) - 1 - axis_at))
    return loudness


def noise(stream_key, shape, deviation, bound, pieces=(), kind=jnp.bfloat16):
    factor_of = steps_of(stream_key, shape, pieces, -0.22, 0.18) if pieces else 1.0
    drawn = jax.random.normal(stream_key, shape, jnp.float32) * deviation * factor_of
    return jnp.minimum(jnp.maximum(drawn, -bound), bound).astype(kind)


def setup_inputs(seed: int = 0) -> dict:
    arg_keys = jax.random.split(jax.random.key(seed), 13)
    hidden_in = draw_hidden_in(jax.random.fold_in(arg_keys[12], 71), 0)
    cache_len = draw_cache_len(jax.random.fold_in(arg_keys[12], 71), 0)
    new_count = draw_new_count(jax.random.fold_in(arg_keys[12], 71), 0)
    key_cache = draw_key_cache(jax.random.fold_in(arg_keys[12], 71), 0)
    value_cache = noise(arg_keys[4], (REQS, CAP, D), 1.0, 6.0, ((0, 8), (1, 4)))
    attn_gain = jnp.clip(1.0 + 0.18 * jax.random.normal(arg_keys[5], (D,), jnp.float32), 0.1, 1.9)
    w_query = noise(arg_keys[6], (D, D), D ** -0.5, 0.125, ((0, 8), (1, 4)))
    w_key = noise(arg_keys[7], (D, D), D ** -0.5, 0.125, ((0, 8), (1, 4)))
    w_value = noise(arg_keys[8], (D, D), D ** -0.5, 0.125, ((0, 8), (1, 4)))
    w_out = noise(arg_keys[9], (D, D), D ** -0.5, 0.125, ((0, 4), (1, 8)))
    final_gain = jnp.clip(1.0 + 0.18 * jax.random.normal(arg_keys[10], (D,), jnp.float32), 0.1, 1.9)
    head_weight = draw_head_weight(jax.random.fold_in(arg_keys[12], 71), 0)
    return dict(hidden_in=hidden_in, cache_len=cache_len, new_count=new_count, key_cache=key_cache, value_cache=value_cache, attn_gain=attn_gain, w_query=w_query, w_key=w_key, w_value=w_value, w_out=w_out, final_gain=final_gain, head_weight=head_weight)


EPSILON = 1e-05

def rms_scale(values, gain_vec):
    return values * lax.rsqrt(lax.optimization_barrier(jnp.mean(values * values, axis=-1, keepdims=True)) + EPSILON) * gain_vec

def rotate(vectors, places):
    half_dim = vectors.shape[-1] // 2
    frequency = 10000.0 ** (-jnp.arange(half_dim).astype(jnp.float32) / half_dim)
    angles = places.astype(jnp.float32)[:, None] * frequency[None, :]
    cosine = jnp.cos(angles)[:, None, :]
    sine_part = jnp.sin(angles)[:, None, :]
    first_half = vectors[..., :half_dim]
    second_half = vectors[..., half_dim:]
    return jnp.concatenate([first_half * cosine - second_half * sine_part, second_half * cosine + first_half * sine_part], axis=-1)

def reference(hidden_in, cache_len, new_count, key_cache, value_cache, attn_gain, w_query, w_key, w_value, w_out, final_gain, head_weight):
    scale_factor = HEAD_DIM ** (-0.5)

    def request(operands):
        inputs, length, fresh_count, keys_old, values_old = operands
        normed = rms_scale(inputs.astype(jnp.float32), attn_gain).astype(jnp.bfloat16)
        places = length + jnp.arange(SPAN, dtype=jnp.int32)
        queries = rotate(jnp.dot(normed, w_query, preferred_element_type=jnp.float32).reshape(SPAN, HEADS, HEAD_DIM), places).astype(jnp.bfloat16)
        fresh_keys = rotate(jnp.dot(normed, w_key, preferred_element_type=jnp.float32).reshape(SPAN, HEADS, HEAD_DIM), places).astype(jnp.bfloat16)
        fresh_values = jnp.dot(normed, w_value, preferred_element_type=jnp.float32).astype(jnp.bfloat16).reshape(SPAN, HEADS, HEAD_DIM)
        all_keys = jnp.concatenate([keys_old.reshape(CAP, HEADS, HEAD_DIM), fresh_keys], axis=0)
        all_values = jnp.concatenate([values_old.reshape(CAP, HEADS, HEAD_DIM), fresh_values], axis=0)
        query_pos = jnp.arange(SPAN)[:, None]
        cache_ok = jnp.broadcast_to(jnp.arange(CAP)[None, :] < length, (SPAN, CAP))
        span_cols = jnp.arange(SPAN)[None, :]
        span_ok = (span_cols <= query_pos) & (span_cols < fresh_count)
        allowed = jnp.concatenate([cache_ok, span_ok], axis=1)
        scores = jnp.einsum('chd,khd->hck', queries.astype(jnp.float32), all_keys.astype(jnp.float32)) * scale_factor
        scores = jnp.where(allowed[None], scores, -jnp.inf)
        row_max = lax.optimization_barrier(jnp.max(scores, axis=-1, keepdims=True))
        exp_scores = jnp.exp(scores - row_max)
        row_total = lax.optimization_barrier(jnp.sum(exp_scores, axis=-1))
        weights = lax.optimization_barrier(exp_scores.astype(jnp.bfloat16)).astype(jnp.float32)
        summed = jnp.einsum('hck,khd->hcd', weights, all_values.astype(jnp.float32))
        attended = (summed / row_total[..., None]).astype(jnp.bfloat16)
        attended = jnp.transpose(attended, (1, 0, 2)).reshape(SPAN, HEADS * HEAD_DIM)
        mixed_rows = jnp.dot(attended, w_out, preferred_element_type=jnp.float32) + inputs.astype(jnp.float32)
        return mixed_rows.astype(jnp.bfloat16)
    layer_out = lax.map(request, (hidden_in, cache_len, new_count, key_cache, value_cache))
    last_index = (new_count - 1).astype(jnp.int32)
    last_rows = layer_out[jnp.arange(REQS, dtype=jnp.int32), last_index]
    final_rows = rms_scale(last_rows.astype(jnp.float32), final_gain).astype(jnp.bfloat16)
    logits = jnp.dot(final_rows, head_weight, preferred_element_type=jnp.float32)
    row_max = lax.optimization_barrier(jnp.max(logits, axis=1, keepdims=True))
    log_total = jnp.log(lax.optimization_barrier(jnp.sum(jnp.exp(logits - row_max), axis=1, keepdims=True)))
    logprobs = logits - row_max - log_total
    return (layer_out, logprobs)
```

```python
import functools

import jax
import jax.numpy as jnp
from jax import lax
from jax.experimental import pallas as pl
from jax.experimental.pallas import tpu as pltpu
from jax.sharding import PartitionSpec as P

HEAD_DIM = 64
EPSILON = 1e-05
VMEM_LIMIT = 56 * 1024 * 1024
ANY = pl.BlockSpec(memory_space=pl.ANY)
SMEM = pl.BlockSpec(memory_space=pltpu.SMEM)
VMEM = pl.BlockSpec(memory_space=pltpu.VMEM)


def rms_scale(values, gain_vec):
    return (
        values * lax.rsqrt(jnp.mean(values * values, axis=-1, keepdims=True) + EPSILON) * gain_vec
    )


def rotary_tables(places):
    half_dim = HEAD_DIM // 2
    frequency = 10000.0 ** (-jnp.arange(half_dim).astype(jnp.float32) / half_dim)
    angles = places.astype(jnp.float32)[:, None] * frequency[None, :]
    cosine, sine = jnp.cos(angles), jnp.sin(angles)
    return (
        jnp.concatenate([cosine] * 4, axis=1),
        jnp.concatenate([-sine, sine, -sine, sine], axis=1),
    )


def up_pairs(size, hop, first=0):
    return [(i, i + hop) for i in range(first, size - hop)]


def down_pairs(size, hop, last=None):
    last = size - 1 if last is None else last
    return [(i, i - hop) for i in range(hop, last + 1)]


def xor_pairs(size, bit):
    return [(i, i ^ bit) for i in range(size)]


def gather_line(block, size):
    ups, downs = [], []
    up, down = block, block
    for step in range(1, size):
        up = lax.ppermute(up, "row", up_pairs(size, 1, step - 1))
        down = lax.ppermute(down, "row", down_pairs(size, 1, size - step))
        ups.append(up)
        downs.append(down)
    return ups, downs


def exchange_line(pieces_for, size):
    me = lax.axis_index("row")
    ups, downs = [], []
    for hop in range(1, size):
        up = pieces_for(jnp.minimum(me + hop, size - 1))
        down = pieces_for(jnp.maximum(me - hop, 0))
        ups.append(lax.ppermute(up, "row", up_pairs(size, hop)))
        downs.append(lax.ppermute(down, "row", down_pairs(size, hop)))
    return ups, downs


def gather_weights(block, size):
    rows = block.shape[0]
    if size != 8:
        whole = lax.all_gather(block, "req", axis=0, tiled=True)
        return [(whole, None, 0, rows * size)]
    half = rows // 2
    from_x = lax.ppermute(block, "req", xor_pairs(size, 2))
    from_y = lax.ppermute(block, "req", xor_pairs(size, 4))
    from_c = lax.ppermute(block, "req", xor_pairs(size, 1))
    diag_a = lax.ppermute(from_y[:half], "req", xor_pairs(size, 2))
    diag_b = lax.ppermute(from_x[half:], "req", xor_pairs(size, 4))
    pieces = [
        (block, 0, 0, rows),
        (from_x, 2, 0, rows),
        (from_y, 4, 0, rows),
        (diag_a, 6, 0, half),
        (diag_b, 6, half, half),
        (from_c, 1, 0, rows),
    ]
    for array, mask, first, count in pieces[1:5]:
        pieces.append((lax.ppermute(array, "req", xor_pairs(size, 1)), mask ^ 1, first, count))
    return pieces


def weight_copies(refs, layout, target, sems, me_req, block_rows):
    copies = []
    for index, (ref, (mask, first, count)) in enumerate(zip(refs, layout)):
        if mask is None:
            start = 0
        else:
            start = pl.multiple_of(jnp.bitwise_xor(me_req, mask) * block_rows + first, 16)
        copies.append(pltpu.make_async_copy(ref, target.at[pl.ds(start, count), :], sems.at[index]))
    return copies


def start_line_copies(own, ups, downs, target, sems, me_row, rows):
    size = len(ups) + 1
    waits = []
    own_copy = pltpu.make_async_copy(own, target.at[pl.ds(me_row * rows, rows), :], sems.at[0])
    own_copy.start()
    waits.append(own_copy)
    for hop in range(1, size):
        index = lax.rem(me_row - hop + size, size)
        place = target.at[pl.ds(pl.multiple_of(index * rows, rows), rows), :]
        below = pltpu.make_async_copy(ups[hop - 1], place, sems.at[hop])
        above = pltpu.make_async_copy(downs[size - hop - 1], place, sems.at[hop])

        @pl.when(me_row >= hop)
        def _(below=below):
            below.start()

        @pl.when(me_row < hop)
        def _(above=above):
            above.start()

        waits.append(below)
    return waits


def qkv_kernel(size, layout, block_rows, scalars, *refs):
    pieces = len(layout)
    own, ups, downs = refs[0], refs[1:size], refs[size : 2 * size - 1]
    weights = refs[2 * size - 1 : 2 * size - 1 + pieces]
    cos_ref, sin_ref, qk_ref, v_ref, x_scr, w_scr, x_sems, w_sems = refs[2 * size - 1 + pieces :]
    rows = own.shape[0]
    copies = weight_copies(weights, layout, w_scr, w_sems, scalars[1], block_rows)
    for copy in copies:
        copy.start()
    waits = start_line_copies(own, ups, downs, x_scr, x_sems, scalars[0], rows)
    for copy in waits + copies:
        copy.wait()
    span = x_scr.shape[0]
    width = v_ref.shape[1]
    lane = lax.broadcasted_iota(jnp.int32, (span, 128), 1)
    first_half = lax.rem(lane, HEAD_DIM) < HEAD_DIM // 2
    cosine, sine = cos_ref[...], sin_ref[...]
    x = x_scr[...]
    for tile in range(0, 2 * width, 256):
        stop = min(tile + 256, 2 * width)
        raw = jnp.dot(x, w_scr[:, tile:stop], preferred_element_type=jnp.float32)
        for at in range(tile, stop, 128):
            part = raw[:, at - tile : at - tile + 128]
            half = HEAD_DIM // 2
            swapped = jnp.where(
                first_half, pltpu.roll(part, 128 - half, 1), pltpu.roll(part, half, 1)
            )
            turned = part * cosine + swapped * sine
            if at + 128 <= width:
                turned = turned * (HEAD_DIM**-0.5)
            elif at < width:
                turned = jnp.where(lane < width - at, turned * (HEAD_DIM**-0.5), turned)
            qk_ref[:, at : at + 128] = turned.astype(jnp.bfloat16)
    for tile in range(0, width, 256):
        stop = min(tile + 256, width)
        v_ref[:, tile:stop] = jnp.dot(
            x, w_scr[:, 2 * width + tile : 2 * width + stop], preferred_element_type=jnp.float32
        ).astype(jnp.bfloat16)


def attend_block(q, k_new, v_new, k_old, v_old, limit_new, length):
    nt = (((1,), (1,)), ((), ()))
    s_new = lax.dot_general(q, k_new, nt, preferred_element_type=jnp.float32)
    s_old = lax.dot_general(q, k_old, nt, preferred_element_type=jnp.float32)
    pos_new = lax.broadcasted_iota(jnp.int32, s_new.shape, 1)
    pos_old = lax.broadcasted_iota(jnp.int32, s_old.shape, 1)
    s_new = jnp.where(pos_new < limit_new, s_new, -jnp.inf)
    s_old = jnp.where(pos_old < length, s_old, -jnp.inf)
    top = jnp.maximum(
        jnp.max(s_new, axis=1, keepdims=True), jnp.max(s_old, axis=1, keepdims=True)
    )
    e_new = jnp.exp(s_new - top)
    e_old = jnp.exp(s_old - top)
    total = jnp.sum(e_new, axis=1, keepdims=True) + jnp.sum(e_old, axis=1, keepdims=True)
    summed = jnp.dot(e_new.astype(jnp.bfloat16), v_new, preferred_element_type=jnp.float32)
    summed += jnp.dot(e_old.astype(jnp.bfloat16), v_old, preferred_element_type=jnp.float32)
    return summed / total


def attention_kernel(size, layout, block_rows, scalars, *refs):
    pieces = len(layout)
    own, ups, downs = refs[0], refs[1:size], refs[size : 2 * size - 1]
    weights = refs[2 * size - 1 : 2 * size - 1 + pieces]
    qk_ref, v_ref, out_ref, old_scr, w_scr, att_scr, x_sems, w_sems = refs[2 * size - 1 + pieces :]
    rows = own.shape[0]
    half_rows = rows // 2
    copies = weight_copies(weights, layout, w_scr, w_sems, scalars[1], block_rows)
    waits = start_line_copies(own, ups, downs, old_scr, x_sems, scalars[0], rows)
    for copy in copies:
        copy.start()
    for copy in waits:
        copy.wait()
    span, width = v_ref.shape
    length, count = scalars[2], scalars[3]
    heads = width // HEAD_DIM
    block = min(256, span)

    def attend(live):
        lane = lax.broadcasted_iota(jnp.int32, (block, 128), 1)
        left = lane < HEAD_DIM
        for at in range(0, heads, 2):
            lo = at * HEAD_DIM
            hi = min(lo + 128, width)
            k_at = width + HEAD_DIM + lo if hi - lo == 128 else width
            k_old = jnp.concatenate(
                [old_scr[i * rows : i * rows + half_rows, lo:hi] for i in range(live)], axis=0
            )
            v_old = jnp.concatenate(
                [old_scr[i * rows + half_rows : (i + 1) * rows, lo:hi] for i in range(live)], axis=0
            )
            for begin in range(0, span, block):
                q = qk_ref[begin : begin + block, lo:hi]
                k_new = qk_ref[0 : begin + block, k_at : k_at + hi - lo]
                v_new = v_ref[0 : begin + block, lo:hi]
                row = begin + lax.broadcasted_iota(jnp.int32, (block, 1), 0)
                limit = jnp.minimum(row + 1, count)
                if hi - lo == 128:
                    zero = jnp.zeros_like(q)
                    even = attend_block(
                        jnp.where(left, q, zero), k_new, v_new, k_old, v_old, limit, length
                    )
                    odd = attend_block(
                        jnp.where(left, zero, q), k_new, v_new, k_old, v_old, limit, length
                    )
                    both = jnp.where(left, even, odd)
                else:
                    both = attend_block(q, k_new, v_new, k_old, v_old, limit, length)
                att_scr[begin : begin + block, lo:hi] = both.astype(jnp.bfloat16)

    @pl.when(length <= half_rows)
    def _():
        attend(1)

    @pl.when(length > half_rows)
    def _():
        attend(size)

    for copy in copies:
        copy.wait()
    attended = att_scr[...]
    for tile in range(0, out_ref.shape[1], 256):
        out_ref[:, tile : tile + 256] = lax.dot_general(
            attended,
            w_scr[tile : tile + 256, :],
            (((1,), (1,)), ((), ())),
            preferred_element_type=jnp.float32,
        ).astype(jnp.bfloat16)


def scatter_line(chunks, size):
    me = lax.axis_index("row")

    def own_part(index):
        return lax.dynamic_index_in_dim(chunks, jnp.clip(index, 0, size - 1), 0, keepdims=False)

    up, down = own_part(me + size - 1), own_part(me - size + 1)
    for step in range(1, size):
        up = lax.ppermute(up, "row", [(i, i + 1) for i in range(step)])
        down = lax.ppermute(down, "row", [(i, i - 1) for i in range(size - step, size)])
        if step < size - 1:
            up = (
                up.astype(jnp.float32) + own_part(me + size - 1 - step).astype(jnp.float32)
            ).astype(jnp.bfloat16)
            down = (
                down.astype(jnp.float32) + own_part(me - size + 1 + step).astype(jnp.float32)
            ).astype(jnp.bfloat16)
    return up.astype(jnp.float32) + down.astype(jnp.float32) + own_part(me).astype(jnp.float32)


def butterfly(value, axis, size, combine):
    bit = 1
    while bit < size:
        value = combine(value, lax.ppermute(value, axis, xor_pairs(size, bit)))
        bit *= 2
    return value


def merge_stats(one, other):
    top = jnp.maximum(one[0], other[0])
    total = one[1] * jnp.exp(one[0] - top) + other[1] * jnp.exp(other[0] - top)
    return jnp.stack([top, total])


def on_device(
    n_req,
    n_row,
    hidden_in,
    cache_len,
    new_count,
    key_cache,
    value_cache,
    attn_gain,
    w_query,
    w_key,
    w_value,
    w_out,
    final_gain,
    head_weight,
):
    me_row = lax.axis_index("row")
    me_req = lax.axis_index("req")
    inputs = hidden_in[0]
    rows, model = inputs.shape
    span = rows * n_row
    block_rows, width = w_query.shape
    length, count = cache_len[0], new_count[0]
    scalars = jnp.stack([me_row, me_req, length, count]).astype(jnp.int32)
    params = pltpu.CompilerParams(vmem_limit_bytes=VMEM_LIMIT)

    normed = rms_scale(inputs.astype(jnp.float32), attn_gain).astype(jnp.bfloat16)
    last = width - width % 128
    joined = jnp.concatenate([w_query, w_key[:, last:], w_key[:, :last], w_value], axis=1)
    x_ups, x_downs = gather_line(normed, n_row)
    w_pieces = gather_weights(joined, n_req)
    out_pieces = gather_weights(w_out.T, n_req)

    def cache_for(owner):
        return jnp.concatenate(
            [
                lax.dynamic_slice_in_dim(key_cache[0], owner * width, width, 1),
                lax.dynamic_slice_in_dim(value_cache[0], owner * width, width, 1),
            ],
            axis=0,
        )

    old_ups, old_downs = exchange_line(cache_for, n_row)
    cosine, sine = rotary_tables(length + jnp.arange(span, dtype=jnp.int32))

    w_layout = tuple(piece[1:] for piece in w_pieces)
    queries_keys, values = pl.pallas_call(
        functools.partial(qkv_kernel, n_row, w_layout, block_rows),
        out_shape=(
            jax.ShapeDtypeStruct((span, 2 * width), jnp.bfloat16),
            jax.ShapeDtypeStruct((span, width), jnp.bfloat16),
        ),
        in_specs=[SMEM] + [ANY] * (2 * n_row - 1 + len(w_pieces)) + [VMEM] * 2,
        out_specs=(VMEM, VMEM),
        scratch_shapes=[
            pltpu.VMEM((span, model), jnp.bfloat16),
            pltpu.VMEM((model, 3 * width), jnp.bfloat16),
            pltpu.SemaphoreType.DMA((n_row,)),
            pltpu.SemaphoreType.DMA((len(w_pieces),)),
        ],
        compiler_params=params,
        cost_estimate=pl.CostEstimate(
            flops=6 * span * model * width, bytes_accessed=14 * 2**20, transcendentals=0
        ),
        name="qkv",
    )(scalars, normed, *x_ups, *x_downs, *[piece[0] for piece in w_pieces], cosine, sine)

    out_layout = tuple(piece[1:] for piece in out_pieces)
    partial = pl.pallas_call(
        functools.partial(attention_kernel, n_row, out_layout, block_rows),
        out_shape=jax.ShapeDtypeStruct((span, model), jnp.bfloat16),
        in_specs=[SMEM] + [ANY] * (2 * n_row - 1 + len(out_pieces)) + [VMEM] * 2,
        out_specs=VMEM,
        scratch_shapes=[
            pltpu.VMEM((2 * key_cache.shape[1] * n_row, width), jnp.bfloat16),
            pltpu.VMEM((model, width), jnp.bfloat16),
            pltpu.VMEM((span, width), jnp.bfloat16),
            pltpu.SemaphoreType.DMA((n_row,)),
            pltpu.SemaphoreType.DMA((len(out_pieces),)),
        ],
        compiler_params=params,
        cost_estimate=pl.CostEstimate(
            flops=8 * span * model * width, bytes_accessed=14 * 2**20, transcendentals=0
        ),
        name="attention",
    )(
        scalars,
        cache_for(me_row),
        *old_ups,
        *old_downs,
        *[piece[0] for piece in out_pieces],
        queries_keys,
        values,
    )

    local_index = count - 1 - me_row * rows
    is_owner = (local_index >= 0) & (local_index < rows)
    residual = lax.dynamic_slice_in_dim(inputs, jnp.clip(local_index, 0, rows - 1), 1, 0)
    last_row = lax.dynamic_slice_in_dim(partial, count - 1, 1, 0).astype(jnp.float32)
    last_row += jnp.where(is_owner, residual.astype(jnp.float32), 0.0)
    last_row = butterfly(last_row, "row", n_row, jnp.add).astype(jnp.bfloat16)
    final_row = rms_scale(last_row.astype(jnp.float32), final_gain).astype(jnp.bfloat16)
    table = jnp.where(jnp.arange(n_req)[:, None] == me_req, final_row, jnp.zeros_like(final_row))
    table = butterfly(table, "req", n_req, jnp.add)
    logits = jnp.dot(table, head_weight, preferred_element_type=jnp.float32)
    top = jnp.max(logits, axis=1)
    stats = jnp.stack([top, jnp.sum(jnp.exp(logits - top[:, None]), axis=1)])
    stats = butterfly(stats, "req", n_req, merge_stats)
    stats = butterfly(stats, "row", n_row, merge_stats)
    logprobs = logits - stats[0][:, None] - jnp.log(stats[1])[:, None]

    own_rows = scatter_line(partial.reshape(n_row, rows, model), n_row)
    layer_rows = (own_rows + inputs.astype(jnp.float32)).astype(jnp.bfloat16)
    return (layer_rows[None], logprobs)


def solution(mesh):
    placed = (
        P("req", "row", None),
        P("req"),
        P("req"),
        P("req", "row", None),
        P("req", "row", None),
        P(),
        P("req", "row"),
        P("req", "row"),
        P("req", "row"),
        P("row", "req"),
        P(),
        P(None, ("req", "row")),
    )
    return jax.shard_map(
        functools.partial(on_device, mesh.shape["req"], mesh.shape["row"]),
        mesh=mesh,
        in_specs=placed,
        out_specs=(P("req", "row", None), P(None, ("req", "row"))),
        check_vma=False,
    )
```

```python
import functools

import jax
import jax.numpy as jnp
from jax import lax
from jax.experimental import pallas as pl
from jax.experimental.pallas import tpu as pltpu
from jax.sharding import PartitionSpec as P

HEAD_DIM = 64
EPSILON = 1e-05
ANY = pl.BlockSpec(memory_space=pl.ANY)
SMEM = pl.BlockSpec(memory_space=pltpu.SMEM)
VMEM = pl.BlockSpec(memory_space=pltpu.VMEM)


def rms_scale(values, gain_vec):
    return (
        values * lax.rsqrt(jnp.mean(values * values, axis=-1, keepdims=True) + EPSILON) * gain_vec
    )


def rotary_tables(places):
    half_dim = HEAD_DIM // 2
    frequency = 10000.0 ** (-jnp.arange(half_dim).astype(jnp.float32) / half_dim)
    angles = places.astype(jnp.float32)[:, None] * frequency[None, :]
    cosine, sine = jnp.cos(angles), jnp.sin(angles)
    return (
        jnp.concatenate([cosine] * 4, axis=1),
        jnp.concatenate([-sine, sine, -sine, sine], axis=1),
    )


def up_pairs(size, hop, first=0):
    return [(i, i + hop) for i in range(first, size - hop)]


def down_pairs(size, hop, last=None):
    last = size - 1 if last is None else last
    return [(i, i - hop) for i in range(hop, last + 1)]


def xor_pairs(size, bit):
    return [(i, i ^ bit) for i in range(size)]


def after(value, *earlier):
    return lax.optimization_barrier((value, *earlier))[0]


def gather_line(block, size):
    ups, downs = [], []
    up, down = block, block
    for step in range(1, size):
        up = lax.ppermute(up, "row", up_pairs(size, 1, step - 1))
        down = lax.ppermute(down, "row", down_pairs(size, 1, size - step))
        up, down = lax.optimization_barrier((up, down))
        ups.append(up)
        downs.append(down)
    return ups, downs


def gather_weights(block, size, *earlier):
    rows = block.shape[0]
    if size != 8:
        whole = lax.all_gather(block, "req", axis=0, tiled=True)
        return [(whole, None, 0, rows * size)]
    half = rows // 2
    from_x = lax.ppermute(block, "req", xor_pairs(size, 2))
    from_y = lax.ppermute(block, "req", xor_pairs(size, 4))
    block, from_x, from_y, *_ = lax.optimization_barrier((block, from_x, from_y, *earlier))
    from_c = lax.ppermute(block, "req", xor_pairs(size, 1))
    half_x, half_y = lax.optimization_barrier((from_x[half:], from_y[:half]))
    diag_a = lax.ppermute(half_y, "req", xor_pairs(size, 2))
    diag_b = lax.ppermute(half_x, "req", xor_pairs(size, 4))
    pieces = [
        (block, 0, 0, rows),
        (from_x, 2, 0, rows),
        (from_y, 4, 0, rows),
        (diag_a, 6, 0, half),
        (diag_b, 6, half, half),
        (from_c, 1, 0, rows),
    ]
    for array, mask, first, count in pieces[1:5]:
        pieces.append((lax.ppermute(array, "req", xor_pairs(size, 1)), mask ^ 1, first, count))
    return pieces


def weight_copies(refs, layout, target, sems, me_req, block_rows):
    copies = []
    for index, (ref, (mask, first, count)) in enumerate(zip(refs, layout)):
        if mask is None:
            start = 0
        else:
            start = pl.multiple_of(jnp.bitwise_xor(me_req, mask) * block_rows + first, 16)
        copies.append(pltpu.make_async_copy(ref, target.at[pl.ds(start, count), :], sems.at[index]))
    return copies


def start_line_copies(own, ups, downs, target, sems, me_row, rows):
    size = len(ups) + 1
    waits = []
    own_copy = pltpu.make_async_copy(own, target.at[pl.ds(me_row * rows, rows), :], sems.at[0])
    own_copy.start()
    waits.append(own_copy)
    for hop in range(1, size):
        index = lax.rem(me_row - hop + size, size)
        place = target.at[pl.ds(pl.multiple_of(index * rows, rows), rows), :]
        below = pltpu.make_async_copy(ups[hop - 1], place, sems.at[hop])
        above = pltpu.make_async_copy(downs[size - hop - 1], place, sems.at[hop])

        @pl.when(me_row >= hop)
        def _(below=below):
            below.start()

        @pl.when(me_row < hop)
        def _(above=above):
            above.start()

        waits.append(below)
    return waits


def qkv_kernel(size, layout, block_rows, scalars, *refs):
    pieces = len(layout)
    own, ups, downs = refs[0], refs[1:size], refs[size : 2 * size - 1]
    weights = refs[2 * size - 1 : 2 * size - 1 + pieces]
    cos_ref, sin_ref, out_ref, x_scr, w_scr, x_sems, w_sems = refs[2 * size - 1 + pieces :]
    rows = own.shape[0]
    copies = weight_copies(weights, layout, w_scr, w_sems, scalars[1], block_rows)
    for copy in copies:
        copy.start()
    waits = start_line_copies(own, ups, downs, x_scr, x_sems, scalars[0], rows)
    for copy in waits + copies:
        copy.wait()
    span = x_scr.shape[0]
    total = out_ref.shape[1]
    width = total // 3
    half = HEAD_DIM // 2
    lane = lax.broadcasted_iota(jnp.int32, (span, 128), 1)
    first_half = lax.rem(lane, HEAD_DIM) < half
    cosine, sine = cos_ref[...], sin_ref[...]
    x = x_scr[...]
    for tile in range(0, total, 256):
        end = min(tile + 256, total)
        raw = jnp.dot(x, w_scr[:, tile:end], preferred_element_type=jnp.float32)
        for at in range(tile, end, 128):
            stop = min(at + 128, end)
            part = raw[:, at - tile : stop - tile]
            if at < 2 * width:
                swapped = jnp.where(
                    first_half, pltpu.roll(part, 128 - half, 1), pltpu.roll(part, half, 1)
                )
                part = part * cosine + swapped * sine
                if stop <= width:
                    part = part * (HEAD_DIM**-0.5)
                elif at < width:
                    part = jnp.where(lane < width - at, part * (HEAD_DIM**-0.5), part)
            out_ref[:, at:stop] = part.astype(jnp.bfloat16)


def attend_block(q, k_new, v_new, k_old, v_old, limit_new, length):
    nt = (((1,), (1,)), ((), ()))
    s_new = lax.dot_general(q, k_new, nt, preferred_element_type=jnp.float32)
    s_old = lax.dot_general(q, k_old, nt, preferred_element_type=jnp.float32)
    pos_new = lax.broadcasted_iota(jnp.int32, s_new.shape, 1)
    pos_old = lax.broadcasted_iota(jnp.int32, s_old.shape, 1)
    s_new = jnp.where(pos_new < limit_new, s_new, -jnp.inf)
    s_old = jnp.where(pos_old < length, s_old, -jnp.inf)
    top = jnp.maximum(
        jnp.max(s_new, axis=1, keepdims=True), jnp.max(s_old, axis=1, keepdims=True)
    )
    e_new = jnp.exp(s_new - top)
    e_old = jnp.exp(s_old - top)
    total = jnp.sum(e_new, axis=1, keepdims=True) + jnp.sum(e_old, axis=1, keepdims=True)
    summed = jnp.dot(e_new.astype(jnp.bfloat16), v_new, preferred_element_type=jnp.float32)
    summed += jnp.dot(e_old.astype(jnp.bfloat16), v_old, preferred_element_type=jnp.float32)
    return summed / total


def attention_kernel(size, scalars, *refs):
    blocks = refs[:size]
    qkv_ref, keep_ref, send_ref, last_ref, old_scr, att_scr, sems = refs[size:]
    rows = blocks[0].shape[0]
    half_rows = rows // 2
    me_row, length, count = scalars[0], scalars[2], scalars[3]
    waits = []
    for mask in range(size):
        index = jnp.bitwise_xor(me_row, mask)
        place = old_scr.at[pl.ds(pl.multiple_of(index * rows, rows), rows), :]
        waits.append(pltpu.make_async_copy(blocks[mask], place, sems.at[mask]))
        waits[-1].start()
    for copy in waits:
        copy.wait()
    span, total = qkv_ref.shape
    width = total // 3
    last = width - HEAD_DIM
    block = min(256, span)

    def attend(live):
        lane = lax.broadcasted_iota(jnp.int32, (block, 128), 1)
        left = lane < HEAD_DIM

        def old(part, lo, hi):
            at = part * half_rows
            return jnp.concatenate(
                [old_scr[i * rows + at : i * rows + at + half_rows, lo:hi] for i in range(live)],
                axis=0,
            )

        for lo in range(0, width, 128):
            pair = lo < last
            hi = lo + 128 if pair else width
            k_at = width + HEAD_DIM + lo if pair else width
            k_old, v_old = old(0, lo, hi), old(1, lo, hi)
            for begin in range(0, span, block):
                stop = begin + block
                q = qkv_ref[begin:stop, lo:hi]
                k_new = qkv_ref[0:stop, k_at : k_at + hi - lo]
                v_new = qkv_ref[0:stop, 2 * width + lo : 2 * width + hi]
                row = begin + lax.broadcasted_iota(jnp.int32, (block, 1), 0)
                limit = jnp.minimum(row + 1, count)
                if pair:
                    zero = jnp.zeros_like(q)
                    even = attend_block(
                        jnp.where(left, q, zero), k_new, v_new, k_old, v_old, limit, length
                    )
                    odd = attend_block(
                        jnp.where(left, zero, q), k_new, v_new, k_old, v_old, limit, length
                    )
                    both = jnp.where(left, even, odd)
                else:
                    both = attend_block(q, k_new, v_new, k_old, v_old, limit, length)
                att_scr[begin:stop, lo:hi] = both.astype(jnp.bfloat16)

    @pl.when(length <= half_rows)
    def _():
        attend(1)

    @pl.when(length > half_rows)
    def _():
        attend(size)

    chunk = span // size
    for slot, ref in ((0, keep_ref), (1, send_ref), (2, keep_ref), (3, send_ref)):
        start = pl.multiple_of(jnp.bitwise_xor(me_row, slot) * chunk, chunk)
        at = slot // 2 * chunk
        ref[at : at + chunk, :] = att_scr[pl.ds(start, chunk), :]
    group = lax.div(count - 1, 16)
    rows16 = att_scr[pl.ds(pl.multiple_of(group * 16, 16), 16), :].astype(jnp.float32)
    at16 = lax.broadcasted_iota(jnp.int32, rows16.shape, 0) == count - 1 - group * 16
    row = jnp.sum(jnp.where(at16, rows16, 0.0), axis=0, keepdims=True)
    last_ref[...] = jnp.broadcast_to(row, last_ref.shape).astype(jnp.bfloat16)


NT = (((1,), (1,)), ((), ()))


def last_row_kernel(layout, block_rows, scalars, *refs):
    pieces = len(layout)
    weights = refs[:pieces]
    last_ref, out_ref, w_scr, sems = refs[pieces:]
    columns = w_scr.shape[1]
    weights = [ref.at[:, 0:columns] for ref in weights]
    copies = weight_copies(weights, layout, w_scr, sems, scalars[1], block_rows)
    for copy in copies:
        copy.start()
    for copy in copies:
        copy.wait()
    width = last_ref.shape[1]
    for tile in range(0, out_ref.shape[1], 256):
        out_ref[:, tile : tile + 256] = lax.dot_general(
            last_ref[...],
            w_scr[tile : tile + 256, 0:width],
            NT,
            preferred_element_type=jnp.float32,
        )


def project_kernel(layout, block_rows, scalars, *refs):
    pieces = len(layout)
    keep_ref, got_ref, in_ref, own_ref, mate_ref, w_scr, sems = refs[pieces:]
    copies = weight_copies(refs[:pieces], layout, w_scr, sems, scalars[1], block_rows)
    for copy in copies:
        copy.start()
    attended = jnp.concatenate([keep_ref[...], got_ref[...]], axis=1)
    for copy in copies:
        copy.wait()
    chunk = own_ref.shape[0]
    for tile in range(0, own_ref.shape[1], 256):
        to = tile + 256
        total = lax.dot_general(
            attended, w_scr[tile:to, :], NT, preferred_element_type=jnp.float32
        )
        own_ref[:, tile:to] = total[:chunk] + in_ref[:, tile:to].astype(jnp.float32)
        mate_ref[:, tile:to] = total[chunk:].astype(jnp.bfloat16)


def sum_line(value, size):
    total = value
    for mask in range(1, size):
        total = total + lax.ppermute(value, "row", xor_pairs(size, mask))
    return total


def butterfly(value, axis, size, combine):
    bit = 1
    while bit < size:
        value = combine(value, lax.ppermute(value, axis, xor_pairs(size, bit)))
        bit *= 2
    return value


def merge_stats(one, other):
    top = jnp.maximum(one[0], other[0])
    total = one[1] * jnp.exp(one[0] - top) + other[1] * jnp.exp(other[0] - top)
    return jnp.stack([top, total])


def on_device(
    n_req,
    n_row,
    hidden_in,
    cache_len,
    new_count,
    key_cache,
    value_cache,
    attn_gain,
    w_query,
    w_key,
    w_value,
    w_out,
    final_gain,
    head_weight,
):
    me_row = lax.axis_index("row")
    me_req = lax.axis_index("req")
    inputs = hidden_in[0]
    rows, model = inputs.shape
    span = rows * n_row
    block_rows, width = w_query.shape
    length, count = cache_len[0], new_count[0]
    scalars = jnp.stack([me_row, me_req, length, count]).astype(jnp.int32)

    def params(mib):
        return pltpu.CompilerParams(vmem_limit_bytes=mib * 1024 * 1024)


    normed = rms_scale(inputs.astype(jnp.float32), attn_gain).astype(jnp.bfloat16)
    last = width - HEAD_DIM
    joined = jnp.concatenate([w_query, w_key[:, last:], w_key[:, :last], w_value], axis=1)
    x_ups, x_downs = gather_line(normed, n_row)
    joined = after(joined, normed)
    pieces = gather_weights(joined, n_req)
    layout = tuple(piece[1:] for piece in pieces)

    out_own = w_out.T
    out_next = lax.ppermute(out_own, "row", xor_pairs(n_row, 1))
    out_both = jnp.concatenate([out_own, out_next], axis=1)
    out_both = after(out_both, *[piece[0] for piece in pieces[1:]], x_ups[-1], x_downs[-1])

    def cache_for(owner):
        return jnp.concatenate(
            [
                lax.dynamic_slice_in_dim(key_cache[0], owner * width, width, 1),
                lax.dynamic_slice_in_dim(value_cache[0], owner * width, width, 1),
            ],
            axis=0,
        )

    cached_rows = key_cache.shape[1]
    old_blocks = []
    for mask in range(1, n_row):
        block = after(cache_for(jnp.bitwise_xor(me_row, mask)), x_ups[-1], x_downs[-1])
        old_blocks.append(lax.ppermute(block, "row", xor_pairs(n_row, mask)))
    cosine, sine = rotary_tables(length + jnp.arange(span, dtype=jnp.int32))

    qkv = pl.pallas_call(
        functools.partial(qkv_kernel, n_row, layout, block_rows),
        out_shape=jax.ShapeDtypeStruct((span, 3 * width), jnp.bfloat16),
        in_specs=[SMEM] + [ANY] * (2 * n_row - 1 + len(pieces)) + [VMEM] * 2,
        out_specs=VMEM,
        scratch_shapes=[
            pltpu.VMEM((span, model), jnp.bfloat16),
            pltpu.VMEM((model, 3 * width), jnp.bfloat16),
            pltpu.SemaphoreType.DMA((n_row,)),
            pltpu.SemaphoreType.DMA((len(pieces),)),
        ],
        compiler_params=params(24),
        cost_estimate=pl.CostEstimate(
            flops=6 * span * model * width, bytes_accessed=14 * 2**20, transcendentals=0
        ),
        name="qkv",
    )(scalars, normed, *x_ups, *x_downs, *[piece[0] for piece in pieces], cosine, sine)

    out_pieces = gather_weights(out_both, n_req, qkv)

    chunk = span // n_row
    keep, send, last_attended = pl.pallas_call(
        functools.partial(attention_kernel, n_row),
        out_shape=(
            jax.ShapeDtypeStruct((2 * chunk, width), jnp.bfloat16),
            jax.ShapeDtypeStruct((2 * chunk, width), jnp.bfloat16),
            jax.ShapeDtypeStruct((16, width), jnp.bfloat16),
        ),
        in_specs=[SMEM] + [ANY] * n_row + [VMEM],
        out_specs=(VMEM, VMEM, VMEM),
        scratch_shapes=[
            pltpu.VMEM((2 * cached_rows * n_row, width), jnp.bfloat16),
            pltpu.VMEM((span, width), jnp.bfloat16),
            pltpu.SemaphoreType.DMA((n_row,)),
        ],
        compiler_params=params(24),
        cost_estimate=pl.CostEstimate(
            flops=6 * span * span * width, bytes_accessed=4 * 2**20, transcendentals=0
        ),
        name="attention",
    )(scalars, cache_for(me_row), *old_blocks, qkv)

    out_layout = tuple(piece[1:] for piece in out_pieces)
    out_weights = [piece[0] for piece in out_pieces]
    own_columns = -(-width // 128) * 128
    own_part = pl.pallas_call(
        functools.partial(last_row_kernel, out_layout, block_rows),
        out_shape=jax.ShapeDtypeStruct((16, model), jnp.float32),
        in_specs=[SMEM] + [ANY] * len(out_weights) + [VMEM],
        out_specs=VMEM,
        scratch_shapes=[
            pltpu.VMEM((model, own_columns), jnp.bfloat16),
            pltpu.SemaphoreType.DMA((len(out_weights),)),
        ],
        compiler_params=params(8),
        cost_estimate=pl.CostEstimate(
            flops=32 * model * width, bytes_accessed=4 * 2**20, transcendentals=0
        ),
        name="last_row",
    )(scalars, *out_weights, last_attended)[:1]

    local_index = count - 1 - me_row * rows
    is_owner = (local_index >= 0) & (local_index < rows)
    residual = lax.dynamic_slice_in_dim(inputs, jnp.clip(local_index, 0, rows - 1), 1, 0)
    own_part += jnp.where(is_owner, residual.astype(jnp.float32), 0.0)
    last_row = sum_line(own_part, n_row)

    got = lax.ppermute(send, "row", xor_pairs(n_row, 1))
    got = after(got, last_row)
    own_sum, mate_part = pl.pallas_call(
        functools.partial(project_kernel, out_layout, block_rows),
        out_shape=(
            jax.ShapeDtypeStruct((chunk, model), jnp.float32),
            jax.ShapeDtypeStruct((chunk, model), jnp.bfloat16),
        ),
        in_specs=[SMEM] + [ANY] * len(out_weights) + [VMEM] * 3,
        out_specs=(VMEM, VMEM),
        scratch_shapes=[
            pltpu.VMEM((model, 2 * width), jnp.bfloat16),
            pltpu.SemaphoreType.DMA((len(out_weights),)),
        ],
        compiler_params=params(16),
        cost_estimate=pl.CostEstimate(
            flops=2 * span * model * width, bytes_accessed=8 * 2**20, transcendentals=0
        ),
        name="project",
    )(scalars, *out_weights, keep, got, inputs)
    others = lax.ppermute(mate_part, "row", xor_pairs(n_row, 2))
    layer_rows = (own_sum + others.astype(jnp.float32)).astype(jnp.bfloat16)

    final_row = rms_scale(
        last_row.astype(jnp.bfloat16).astype(jnp.float32), final_gain
    ).astype(jnp.bfloat16)
    final_row = after(final_row, mate_part)
    table = jnp.where(jnp.arange(n_req)[:, None] == me_req, final_row, jnp.zeros_like(final_row))
    table = butterfly(table, "req", n_req, jnp.add)
    logits = jnp.dot(table, head_weight, preferred_element_type=jnp.float32)
    top = jnp.max(logits, axis=1)
    stats = jnp.stack([top, jnp.sum(jnp.exp(logits - top[:, None]), axis=1)])
    stats = after(stats, others)
    stats = butterfly(stats, "req", n_req, merge_stats)
    stats = butterfly(stats, "row", n_row, merge_stats)
    logprobs = logits - stats[0][:, None] - jnp.log(stats[1])[:, None]
    return (layer_rows[None], logprobs)


def solution(mesh):
    placed = (
        P("req", "row", None),
        P("req"),
        P("req"),
        P("req", "row", None),
        P("req", "row", None),
        P(),
        P("req", "row"),
        P("req", "row"),
        P("req", "row"),
        P("row", "req"),
        P(),
        P(None, ("req", "row")),
    )
    return jax.shard_map(
        functools.partial(on_device, mesh.shape["req"], mesh.shape["row"]),
        mesh=mesh,
        in_specs=placed,
        out_specs=(P("req", "row", None), P(None, ("req", "row"))),
        check_vma=False,
    )
```

```python
import functools

import jax
import jax.numpy as jnp
from jax import lax
from jax.experimental import pallas as pl
from jax.experimental.pallas import tpu as pltpu
from jax.sharding import PartitionSpec as P

HEAD_DIM = 64
EPSILON = 1e-05
HBM = pl.BlockSpec(memory_space=pltpu.HBM)
SMEM = pl.BlockSpec(memory_space=pltpu.SMEM)
VMEM = pl.BlockSpec(memory_space=pltpu.VMEM)


def rms_scale(values, gain_vec):
    return (
        values * lax.rsqrt(jnp.mean(values * values, axis=-1, keepdims=True) + EPSILON) * gain_vec
    )


def rotary_tables(places):
    half_dim = HEAD_DIM // 2
    frequency = 10000.0 ** (-jnp.arange(half_dim).astype(jnp.float32) / half_dim)
    angles = places.astype(jnp.float32)[:, None] * frequency[None, :]
    cosine, sine = jnp.cos(angles), jnp.sin(angles)
    return (
        jnp.concatenate([cosine] * 4, axis=1),
        jnp.concatenate([-sine, sine, -sine, sine], axis=1),
    )


def up_pairs(size, hop, first=0):
    return [(i, i + hop) for i in range(first, size - hop)]


def down_pairs(size, hop, last=None):
    last = size - 1 if last is None else last
    return [(i, i - hop) for i in range(hop, last + 1)]


def xor_pairs(size, bit):
    return [(i, i ^ bit) for i in range(size)]


def after(value, *earlier):
    return lax.optimization_barrier((value, *earlier))[0]


class Rows:
    def __init__(self, block, size):
        self.block, self.size, self.rows = block, size, block.shape[0]
        self.half = self.rows // 2

    def send(self, array, mask):
        return lax.ppermute(array, "req", xor_pairs(self.size, mask))

    def neighbours(self):
        if self.size != 8:
            return [lax.all_gather(self.block, "req", axis=0, tiled=True)]
        return [self.send(self.block, 2), self.send(self.block, 4)]

    def diagonal(self, got):
        if self.size != 8:
            return []
        half_x, half_y = lax.optimization_barrier((got[0][self.half :], got[1][: self.half]))
        return [self.send(half_y, 2), self.send(half_x, 4)]

    def cores(self, arrays):
        return [self.send(array, 1) for array in arrays] if self.size == 8 else []

    def pieces(self, got, diagonal, others):
        if self.size != 8:
            return [(got[0], None, 0, self.rows * self.size)]
        places = [
            (0, 0, self.rows),
            (2, 0, self.rows),
            (4, 0, self.rows),
            (6, 0, self.half),
            (6, self.half, self.half),
        ]
        pieces = []
        for here, there, (mask, at, count) in zip(
            [self.block, *got, *diagonal], others, places, strict=True
        ):
            pieces += [(here, mask, at, count), (there, mask ^ 1, at, count)]
        return pieces


def gather_line(block, size, *ready):
    ups, downs = [], []
    up, down = block, block
    for step in range(1, size):
        up = lax.ppermute(up, "row", up_pairs(size, 1, step - 1))
        down = lax.ppermute(down, "row", down_pairs(size, 1, size - step))
        if step == size - 2:
            up, down, *ready = lax.optimization_barrier((up, down, *ready))
        else:
            up, down = lax.optimization_barrier((up, down))
        ups.append(up)
        downs.append(down)
    return ups, downs, *ready


def together(*groups):
    flat = lax.optimization_barrier(tuple(array for group in groups for array in group))
    result, at = [], 0
    for group in groups:
        result.append(list(flat[at : at + len(group)]))
        at += len(group)
    return result


def weight_copies(refs, layout, target, sems, me_req, block_rows):
    copies = []
    for index, (ref, (mask, first, count)) in enumerate(zip(refs, layout)):
        if mask is None:
            start = 0
        else:
            start = pl.multiple_of(jnp.bitwise_xor(me_req, mask) * block_rows + first, 16)
        copies.append(pltpu.make_async_copy(ref, target.at[pl.ds(start, count), :], sems.at[index]))
    return copies


def start_line_copies(own, ups, downs, target, sems, me_row, rows):
    size = len(ups) + 1
    waits = []
    own_copy = pltpu.make_async_copy(own, target.at[pl.ds(me_row * rows, rows), :], sems.at[0])
    own_copy.start()
    waits.append(own_copy)
    for hop in range(1, size):
        index = lax.rem(me_row - hop + size, size)
        place = target.at[pl.ds(pl.multiple_of(index * rows, rows), rows), :]
        below = pltpu.make_async_copy(ups[hop - 1], place, sems.at[hop])
        above = pltpu.make_async_copy(downs[size - hop - 1], place, sems.at[hop])

        @pl.when(me_row >= hop)
        def _(below=below):
            below.start()

        @pl.when(me_row < hop)
        def _(above=above):
            above.start()

        waits.append(below)
    return waits


def qkv_kernel(size, layout, block_rows, scalars, *refs):
    pieces = len(layout)
    own, ups, downs = refs[0], refs[1:size], refs[size : 2 * size - 1]
    weights = refs[2 * size - 1 : 2 * size - 1 + pieces]
    cos_ref, sin_ref, out_ref, x_scr, w_scr, x_sems, w_sems = refs[2 * size - 1 + pieces :]
    rows = own.shape[0]
    total = out_ref.shape[1]
    copies = weight_copies(weights, layout, w_scr, w_sems, scalars[1], block_rows)
    for copy in copies:
        copy.start()
    waits = start_line_copies(own, ups, downs, x_scr, x_sems, scalars[0], rows)
    for copy in waits + copies:
        copy.wait()
    span = x_scr.shape[0]
    width = total // 3
    half = HEAD_DIM // 2
    lane = lax.broadcasted_iota(jnp.int32, (span, 128), 1)
    first_half = lax.rem(lane, HEAD_DIM) < half
    cosine, sine = cos_ref[...], sin_ref[...]
    for tile in range(0, total, 256):
        end = min(tile + 256, total)
        raw = jnp.dot(x_scr[...], w_scr[:, tile:end], preferred_element_type=jnp.float32)
        for at in range(tile, end, 128):
            stop = min(at + 128, end)
            part = raw[:, at - tile : stop - tile]
            if at < 2 * width:
                swapped = jnp.where(
                    first_half, pltpu.roll(part, 128 - half, 1), pltpu.roll(part, half, 1)
                )
                part = part * cosine + swapped * sine
                if stop <= width:
                    part = part * (HEAD_DIM**-0.5)
                elif at < width:
                    part = jnp.where(lane < width - at, part * (HEAD_DIM**-0.5), part)
            out_ref[:, at:stop] = part.astype(jnp.bfloat16)


def attend_block(q, k_new, v_new, k_old, v_old, limit_new, length):
    nt = (((1,), (1,)), ((), ()))
    s_new = lax.dot_general(q, k_new, nt, preferred_element_type=jnp.float32)
    s_old = lax.dot_general(q, k_old, nt, preferred_element_type=jnp.float32)
    pos_new = lax.broadcasted_iota(jnp.int32, s_new.shape, 1)
    pos_old = lax.broadcasted_iota(jnp.int32, s_old.shape, 1)
    s_new = jnp.where(pos_new < limit_new, s_new, -jnp.inf)
    s_old = jnp.where(pos_old < length, s_old, -jnp.inf)
    top = jnp.maximum(
        jnp.max(s_new, axis=1, keepdims=True), jnp.max(s_old, axis=1, keepdims=True)
    )
    e_new = jnp.exp(s_new - top)
    e_old = jnp.exp(s_old - top)
    total = jnp.sum(e_new, axis=1, keepdims=True) + jnp.sum(e_old, axis=1, keepdims=True)
    summed = jnp.dot(e_new.astype(jnp.bfloat16), v_new, preferred_element_type=jnp.float32)
    summed += jnp.dot(e_old.astype(jnp.bfloat16), v_old, preferred_element_type=jnp.float32)
    return summed / total


def attention_kernel(size, scalars, *refs):
    blocks = refs[:size]
    qkv_ref, keep_ref, send_ref, last_ref, k_old, v_old, att_scr, sems = refs[size:]
    rows = blocks[0].shape[0] // 2
    me_row, length, count = scalars[0], scalars[2], scalars[3]
    waits = []
    for mask in range(size):
        index = jnp.bitwise_xor(me_row, mask)
        for part, target in enumerate((k_old, v_old)):
            copy = pltpu.make_async_copy(
                blocks[mask].at[pl.ds(part * rows, rows), :],
                target.at[pl.ds(pl.multiple_of(index * rows, rows), rows), :],
                sems.at[part, mask],
            )
            copy.start()
            waits.append(copy)
    for copy in waits:
        copy.wait()
    span, total = qkv_ref.shape
    width = total // 3
    last = width - HEAD_DIM
    block = min(256, span)

    def attend(live):
        lane = lax.broadcasted_iota(jnp.int32, (block, 128), 1)
        left = lane < HEAD_DIM

        def heads(q_at, k_at, v_at, lo, wide):
            old_k, old_v = k_old[0:live, pl.ds(lo, wide)], v_old[0:live, pl.ds(lo, wide)]
            for begin in range(0, span, block):
                stop = begin + block
                q = qkv_ref[begin:stop, pl.ds(q_at, wide)]
                k_new = qkv_ref[0:stop, pl.ds(k_at, wide)]
                v_new = qkv_ref[0:stop, pl.ds(v_at, wide)]
                row = begin + lax.broadcasted_iota(jnp.int32, (block, 1), 0)
                limit = jnp.minimum(row + 1, count)
                if wide == 128:
                    zero = jnp.zeros_like(q)
                    both = jnp.where(
                        left,
                        attend_block(
                            jnp.where(left, q, zero), k_new, v_new, old_k, old_v, limit, length
                        ),
                        attend_block(
                            jnp.where(left, zero, q), k_new, v_new, old_k, old_v, limit, length
                        ),
                    )
                else:
                    both = attend_block(q, k_new, v_new, old_k, old_v, limit, length)
                att_scr[begin:stop, pl.ds(lo, wide)] = both.astype(jnp.bfloat16)

        @pl.loop(0, last // 128)
        def _(pair):
            lo = pl.multiple_of(pair * 128, 128)
            heads(lo, lo + width + HEAD_DIM, lo + 2 * width, lo, 128)

        heads(last, width, 2 * width + last, last, HEAD_DIM)

    @pl.when(length <= rows)
    def _():
        attend(rows)

    @pl.when(length > rows)
    def _():
        attend(size * rows)

    chunk = span // size
    for slot, ref in ((0, keep_ref), (1, send_ref), (2, keep_ref), (3, send_ref)):
        start = pl.multiple_of(jnp.bitwise_xor(me_row, slot) * chunk, chunk)
        at = slot // 2 * chunk
        ref[at : at + chunk, :] = att_scr[pl.ds(start, chunk), :]
    group = lax.div(count - 1, 16)
    rows16 = att_scr[pl.ds(pl.multiple_of(group * 16, 16), 16), :].astype(jnp.float32)
    at16 = lax.broadcasted_iota(jnp.int32, rows16.shape, 0) == count - 1 - group * 16
    row = jnp.sum(jnp.where(at16, rows16, 0.0), axis=0, keepdims=True)
    last_ref[...] = jnp.broadcast_to(row, last_ref.shape).astype(jnp.bfloat16)


NT = (((1,), (1,)), ((), ()))


def last_row_kernel(layout, block_rows, scalars, *refs):
    pieces = len(layout)
    weights = refs[:pieces]
    last_ref, out_ref, w_scr, sems = refs[pieces:]
    columns = w_scr.shape[1]
    weights = [ref.at[:, 0:columns] for ref in weights]
    copies = weight_copies(weights, layout, w_scr, sems, scalars[1], block_rows)
    for copy in copies:
        copy.start()
    for copy in copies:
        copy.wait()
    width = last_ref.shape[1]
    for tile in range(0, out_ref.shape[1], 256):
        out_ref[:, tile : tile + 256] = lax.dot_general(
            last_ref[...],
            w_scr[tile : tile + 256, 0:width],
            NT,
            preferred_element_type=jnp.float32,
        )


def project_kernel(layout, block_rows, scalars, *refs):
    pieces = len(layout)
    keep_ref, got_ref, in_ref, own_ref, mate_ref, w_scr, sems = refs[pieces:]
    copies = weight_copies(refs[:pieces], layout, w_scr, sems, scalars[1], block_rows)
    for copy in copies:
        copy.start()
    attended = jnp.concatenate([keep_ref[...], got_ref[...]], axis=1)
    for copy in copies:
        copy.wait()
    chunk = own_ref.shape[0]
    for tile in range(0, own_ref.shape[1], 256):
        to = tile + 256
        total = lax.dot_general(
            attended, w_scr[tile:to, :], NT, preferred_element_type=jnp.float32
        )
        own_ref[:, tile:to] = total[:chunk] + in_ref[:, tile:to].astype(jnp.float32)
        mate_ref[:, tile:to] = total[chunk:].astype(jnp.bfloat16)


def head_kernel(table_ref, *refs):
    weights, (logits_ref, stats_ref) = refs[:-2], refs[-2:]
    step = pl.program_id(0)
    wide = weights[0].shape[1]
    for index, ref in enumerate(weights):
        start = pl.multiple_of((step * len(weights) + index) * wide, 128)
        logits_ref[:, pl.ds(start, wide)] = jnp.dot(
            table_ref[...], ref[...], preferred_element_type=jnp.float32
        )

    @pl.when(step == pl.num_programs(0) - 1)
    def _():
        logits = logits_ref[...]
        top = jnp.max(logits, axis=1, keepdims=True)
        stats_ref[:, 0:1] = top
        stats_ref[:, 1:2] = jnp.sum(jnp.exp(logits - top), axis=1, keepdims=True)


def sum_line(value, size):
    total = value
    for mask in range(1, size):
        total = total + lax.ppermute(value, "row", xor_pairs(size, mask))
    return total


def combine_all(value, axis, size, combine, width=4):
    bit = 1
    while bit < size:
        count = min(width, size // bit)
        others = [
            lax.ppermute(value, axis, xor_pairs(size, bit * index)) for index in range(1, count)
        ]
        value = combine(value, *others)
        bit *= count
    return value


def add_all(*tables):
    return functools.reduce(jnp.add, tables)


def merge_stats(*stats):
    top = functools.reduce(jnp.maximum, [one[:, :1] for one in stats])
    total = add_all(*[one[:, 1:] * jnp.exp(one[:, :1] - top) for one in stats])
    return jnp.concatenate([top, total], axis=1)


def on_device(
    n_req,
    n_row,
    hidden_in,
    cache_len,
    new_count,
    key_cache,
    value_cache,
    attn_gain,
    w_query,
    w_key,
    w_value,
    w_out,
    final_gain,
    head_weight,
):
    me_row = lax.axis_index("row")
    me_req = lax.axis_index("req")
    inputs = hidden_in[0]
    rows, model = inputs.shape
    span = rows * n_row
    block_rows, width = w_query.shape
    length, count = cache_len[0], new_count[0]
    scalars = jnp.stack([me_row, me_req, length, count]).astype(jnp.int32)

    def params(mib):
        return pltpu.CompilerParams(vmem_limit_bytes=mib * 1024 * 1024)


    normed = rms_scale(inputs.astype(jnp.float32), attn_gain).astype(jnp.bfloat16)
    last = width - HEAD_DIM
    joined = jnp.concatenate([w_query, w_key[:, last:], w_key[:, :last], w_value], axis=1)

    def cache_for(owner):
        return jnp.concatenate(
            [
                lax.dynamic_slice_in_dim(key_cache[0], owner * width, width, 1),
                lax.dynamic_slice_in_dim(value_cache[0], owner * width, width, 1),
            ],
            axis=0,
        )

    cached_rows = key_cache.shape[1]

    joined = after(joined, normed)
    out_own = w_out.T
    weights = Rows(joined, n_req)
    got = weights.neighbours()
    cosine, sine = rotary_tables(length + jnp.arange(span, dtype=jnp.int32))
    x_ups, x_downs, scalars, cosine, sine = gather_line(normed, n_row, scalars, cosine, sine)
    got, own = together(got, [joined])
    diagonal = weights.diagonal(got)
    others = weights.cores([*own, *got, *diagonal])
    pieces = weights.pieces(got, diagonal, others)
    layout = tuple(piece[1:] for piece in pieces)

    out_next = lax.ppermute(out_own, "row", xor_pairs(n_row, 1))
    old_blocks = [
        lax.ppermute(
            after(cache_for(jnp.bitwise_xor(me_row, mask)), x_ups[-1], x_downs[-1]),
            "row",
            xor_pairs(n_row, mask),
        )
        for mask in range(1, n_row)
    ]
    out_rows = Rows(
        after(jnp.concatenate([out_own, out_next], axis=1), x_ups[-1], x_downs[-1], *others), n_req
    )
    out_got = out_rows.neighbours()

    qkv = pl.pallas_call(
        functools.partial(qkv_kernel, n_row, layout, block_rows),
        out_shape=jax.ShapeDtypeStruct((span, 3 * width), jnp.bfloat16),
        in_specs=[SMEM] + [HBM] * (2 * n_row - 1 + len(pieces)) + [VMEM] * 2,
        out_specs=VMEM,
        scratch_shapes=[
            pltpu.VMEM((span, model), jnp.bfloat16),
            pltpu.VMEM((model, 3 * width), jnp.bfloat16),
            pltpu.SemaphoreType.DMA((n_row,)),
            pltpu.SemaphoreType.DMA((len(pieces),)),
        ],
        compiler_params=params(24),
        cost_estimate=pl.CostEstimate(
            flops=6 * span * model * width, bytes_accessed=14 * 2**20, transcendentals=0
        ),
        name="qkv",
    )(scalars, normed, *x_ups, *x_downs, *[piece[0] for piece in pieces], cosine, sine)

    out_block, *out_got = lax.optimization_barrier((out_rows.block, *out_got, qkv))[:-1]
    out_diagonal = out_rows.diagonal(out_got)
    out_others = out_rows.cores([out_block, *out_got])

    chunk = span // n_row
    keep, send, last_attended = pl.pallas_call(
        functools.partial(attention_kernel, n_row),
        out_shape=(
            jax.ShapeDtypeStruct((2 * chunk, width), jnp.bfloat16),
            jax.ShapeDtypeStruct((2 * chunk, width), jnp.bfloat16),
            jax.ShapeDtypeStruct((16, width), jnp.bfloat16),
        ),
        in_specs=[SMEM] + [HBM] * (1 + len(old_blocks)) + [VMEM],
        out_specs=(VMEM, VMEM, VMEM),
        scratch_shapes=[
            pltpu.VMEM((cached_rows * n_row, width), jnp.bfloat16),
            pltpu.VMEM((cached_rows * n_row, width), jnp.bfloat16),
            pltpu.VMEM((span, width), jnp.bfloat16),
            pltpu.SemaphoreType.DMA((2, n_row)),
        ],
        compiler_params=params(24),
        cost_estimate=pl.CostEstimate(
            flops=6 * span * span * width, bytes_accessed=4 * 2**20, transcendentals=0
        ),
        name="attention",
    )(scalars, cache_for(me_row), *old_blocks, qkv)

    out_others += out_rows.cores(out_diagonal)
    out_pieces = out_rows.pieces(out_got, out_diagonal, out_others)
    out_layout = tuple(piece[1:] for piece in out_pieces)
    out_weights = [piece[0] for piece in out_pieces]
    own_columns = -(-width // 128) * 128
    own_part = pl.pallas_call(
        functools.partial(last_row_kernel, out_layout, block_rows),
        out_shape=jax.ShapeDtypeStruct((16, model), jnp.float32),
        in_specs=[SMEM] + [HBM] * len(out_weights) + [VMEM],
        out_specs=VMEM,
        scratch_shapes=[
            pltpu.VMEM((model, own_columns), jnp.bfloat16),
            pltpu.SemaphoreType.DMA((len(out_weights),)),
        ],
        compiler_params=params(8),
        cost_estimate=pl.CostEstimate(
            flops=32 * model * width, bytes_accessed=4 * 2**20, transcendentals=0
        ),
        name="last_row",
    )(scalars, *out_weights, last_attended)[:1]

    local_index = count - 1 - me_row * rows
    is_owner = (local_index >= 0) & (local_index < rows)
    residual = lax.dynamic_slice_in_dim(inputs, jnp.clip(local_index, 0, rows - 1), 1, 0)
    own_part += jnp.where(is_owner, residual.astype(jnp.float32), 0.0)
    last_row = sum_line(own_part, n_row)

    got = after(lax.ppermute(send, "row", xor_pairs(n_row, 1)), last_row)
    own_sum, mate_part = pl.pallas_call(
        functools.partial(project_kernel, out_layout, block_rows),
        out_shape=(
            jax.ShapeDtypeStruct((chunk, model), jnp.float32),
            jax.ShapeDtypeStruct((chunk, model), jnp.bfloat16),
        ),
        in_specs=[SMEM] + [HBM] * len(out_weights) + [VMEM] * 3,
        out_specs=(VMEM, VMEM),
        scratch_shapes=[
            pltpu.VMEM((model, 2 * width), jnp.bfloat16),
            pltpu.SemaphoreType.DMA((len(out_weights),)),
        ],
        compiler_params=params(16),
        cost_estimate=pl.CostEstimate(
            flops=2 * span * model * width, bytes_accessed=8 * 2**20, transcendentals=0
        ),
        name="project",
    )(scalars, *out_weights, keep, got, inputs)
    others = lax.ppermute(mate_part, "row", xor_pairs(n_row, 2))
    layer_rows = (own_sum + others.astype(jnp.float32)).astype(jnp.bfloat16)

    final_row = rms_scale(
        last_row.astype(jnp.bfloat16).astype(jnp.float32), final_gain
    ).astype(jnp.bfloat16)
    table = jnp.where(jnp.arange(n_req)[:, None] == me_req, final_row, jnp.zeros_like(final_row))
    table = combine_all(table, "req", n_req, add_all, 2)
    table = after(table, mate_part)
    vocab = head_weight.shape[1]
    wide, streams = 256, 3

    def columns(index):
        return pl.BlockSpec((model, wide), lambda step: (0, step * streams + index))

    logits, stats = pl.pallas_call(
        head_kernel,
        grid=(vocab // (wide * streams),),
        out_shape=(
            jax.ShapeDtypeStruct((n_req, vocab), jnp.float32),
            jax.ShapeDtypeStruct((n_req, 2), jnp.float32),
        ),
        in_specs=[
            pl.BlockSpec((n_req, model), lambda step: (0, 0)),
            *[columns(index) for index in range(streams)],
        ],
        out_specs=(
            pl.BlockSpec((n_req, vocab), lambda step: (0, 0)),
            pl.BlockSpec((n_req, 2), lambda step: (0, 0)),
        ),
        compiler_params=params(48),
        cost_estimate=pl.CostEstimate(flops=0, bytes_accessed=0, transcendentals=0),
        name="head",
    )(table, *[head_weight] * streams)
    stats = combine_all(stats, "req", n_req, merge_stats, 8)
    stats = after(stats, others)
    stats = combine_all(stats, "row", n_row, merge_stats)
    logprobs = logits - stats[:, :1] - jnp.log(stats[:, 1:])
    return (layer_rows[None], logprobs)


def solution(mesh):
    placed = (
        P("req", "row", None),
        P("req"),
        P("req"),
        P("req", "row", None),
        P("req", "row", None),
        P(),
        P("req", "row"),
        P("req", "row"),
        P("req", "row"),
        P("row", "req"),
        P(),
        P(None, ("req", "row")),
    )
    return jax.shard_map(
        functools.partial(on_device, mesh.shape["req"], mesh.shape["row"]),
        mesh=mesh,
        in_specs=placed,
        out_specs=(P("req", "row", None), P(None, ("req", "row"))),
        check_vma=False,
    )
```

```python
import functools

import jax
import jax.numpy as jnp
from jax import lax
from jax.experimental import pallas as pl
from jax.experimental.pallas import tpu as pltpu
from jax.sharding import PartitionSpec as P

HEAD_DIM = 64
EPSILON = 1e-05
HBM = pl.BlockSpec(memory_space=pltpu.HBM)
SMEM = pl.BlockSpec(memory_space=pltpu.SMEM)
VMEM = pl.BlockSpec(memory_space=pltpu.VMEM)
FREE = pl.CostEstimate(flops=0, bytes_accessed=0, transcendentals=0)


def rms_scale(values, gain_vec):
    return (
        values * lax.rsqrt(jnp.mean(values * values, axis=-1, keepdims=True) + EPSILON) * gain_vec
    )


def rotary_tables(places):
    half_dim = HEAD_DIM // 2
    frequency = 10000.0 ** (-jnp.arange(half_dim).astype(jnp.float32) / half_dim)
    angles = places.astype(jnp.float32)[:, None] * frequency[None, :]
    cosine, sine = jnp.cos(angles), jnp.sin(angles)
    return (
        jnp.concatenate([cosine] * 4, axis=1),
        jnp.concatenate([-sine, sine, -sine, sine], axis=1),
    )


def up_pairs(size, hop, first=0):
    return [(i, i + hop) for i in range(first, size - hop)]


def down_pairs(size, hop, last=None):
    last = size - 1 if last is None else last
    return [(i, i - hop) for i in range(hop, last + 1)]


def xor_pairs(size, bit):
    return [(i, i ^ bit) for i in range(size)]


def after(value, *earlier):
    return lax.optimization_barrier((value, *earlier))[0]


class Rows:
    def __init__(self, block, size):
        self.block, self.size, self.rows = block, size, block.shape[0]
        self.half = self.rows // 2

    def send(self, array, mask):
        return lax.ppermute(array, "req", xor_pairs(self.size, mask))

    def neighbours(self):
        if self.size != 8:
            return [lax.all_gather(self.block, "req", axis=0, tiled=True)]
        return [self.send(self.block, 2), self.send(self.block, 4)]

    def diagonal(self, got):
        if self.size != 8:
            return []
        half_x, half_y = lax.optimization_barrier((got[0][self.half :], got[1][: self.half]))
        return [self.send(half_y, 2), self.send(half_x, 4)]

    def cores(self, arrays):
        return [self.send(array, 1) for array in arrays] if self.size == 8 else []

    def pieces(self, got, diagonal, others):
        if self.size != 8:
            return [(got[0], None, 0, self.rows * self.size)]
        places = [
            (0, 0, self.rows),
            (2, 0, self.rows),
            (4, 0, self.rows),
            (6, 0, self.half),
            (6, self.half, self.half),
        ]
        pieces = []
        for here, there, (mask, at, count) in zip(
            [self.block, *got, *diagonal], others, places, strict=True
        ):
            pieces += [(here, mask, at, count), (there, mask ^ 1, at, count)]
        return pieces


def after_all(values, *earlier):
    return list(lax.optimization_barrier((*values, *earlier)))[: len(values)]


def gather_line(block, size, *ready):
    ups, downs = [], []
    up, down = block, block
    for step in range(1, size):
        up = lax.ppermute(up, "row", up_pairs(size, 1, step - 1))
        down = lax.ppermute(down, "row", down_pairs(size, 1, size - step))
        if step == size - 2:
            up, down, *ready = lax.optimization_barrier((up, down, *ready))
        else:
            up, down = lax.optimization_barrier((up, down))
        ups.append(up)
        downs.append(down)
    return ups, downs, *ready


def together(*groups):
    flat = lax.optimization_barrier(tuple(array for group in groups for array in group))
    result, at = [], 0
    for group in groups:
        result.append(list(flat[at : at + len(group)]))
        at += len(group)
    return result


def weight_copies(refs, layout, target, sems, me_req, block_rows):
    copies = []
    for index, (ref, (mask, first, count)) in enumerate(zip(refs, layout)):
        if mask is None:
            start = 0
        else:
            start = pl.multiple_of(jnp.bitwise_xor(me_req, mask) * block_rows + first, 16)
        copies.append(pltpu.make_async_copy(ref, target.at[pl.ds(start, count), :], sems.at[index]))
    return copies


def start_line_copies(own, ups, downs, target, sems, me_row, rows):
    size = len(ups) + 1
    waits = []
    own_copy = pltpu.make_async_copy(own, target.at[pl.ds(me_row * rows, rows), :], sems.at[0])
    own_copy.start()
    waits.append(own_copy)
    for hop in range(1, size):
        index = lax.rem(me_row - hop + size, size)
        place = target.at[pl.ds(pl.multiple_of(index * rows, rows), rows), :]
        below = pltpu.make_async_copy(ups[hop - 1], place, sems.at[hop])
        above = pltpu.make_async_copy(downs[size - hop - 1], place, sems.at[hop])

        @pl.when(me_row >= hop)
        def _(below=below):
            below.start()

        @pl.when(me_row < hop)
        def _(above=above):
            above.start()

        waits.append(below)
    return waits


def qkv_kernel(size, layout, block_rows, scalars, *refs):
    pieces = len(layout)
    own, ups, downs = refs[0], refs[1:size], refs[size : 2 * size - 1]
    weights = refs[2 * size - 1 : 2 * size - 1 + pieces]
    cos_ref, sin_ref, out_ref, x_scr, w_scr, x_sems, w_sems = refs[2 * size - 1 + pieces :]
    rows = own.shape[0]
    total = out_ref.shape[1]
    copies = weight_copies(weights, layout, w_scr, w_sems, scalars[1], block_rows)
    for copy in copies:
        copy.start()
    waits = start_line_copies(own, ups, downs, x_scr, x_sems, scalars[0], rows)
    for copy in waits + copies:
        copy.wait()
    span = x_scr.shape[0]
    width = total // 3
    half = HEAD_DIM // 2
    lane = lax.broadcasted_iota(jnp.int32, (span, 128), 1)
    first_half = lax.rem(lane, HEAD_DIM) < half
    cosine, sine = cos_ref[...], sin_ref[...]
    for tile in range(0, total, 256):
        end = min(tile + 256, total)
        raw = jnp.dot(x_scr[...], w_scr[:, tile:end], preferred_element_type=jnp.float32)
        for at in range(tile, end, 128):
            stop = min(at + 128, end)
            part = raw[:, at - tile : stop - tile]
            if at < 2 * width:
                swapped = jnp.where(
                    first_half, pltpu.roll(part, 128 - half, 1), pltpu.roll(part, half, 1)
                )
                part = part * cosine + swapped * sine
                if stop <= width:
                    part = part * (HEAD_DIM**-0.5)
                elif at < width:
                    part = jnp.where(lane < width - at, part * (HEAD_DIM**-0.5), part)
            out_ref[:, at:stop] = part.astype(jnp.bfloat16)


def attend_block(q, k_new, v_new, k_old, v_old, limit_new, length):
    nt = (((1,), (1,)), ((), ()))
    s_new = lax.dot_general(q, k_new, nt, preferred_element_type=jnp.float32)
    s_old = lax.dot_general(q, k_old, nt, preferred_element_type=jnp.float32)
    pos_new = lax.broadcasted_iota(jnp.int32, s_new.shape, 1)
    pos_old = lax.broadcasted_iota(jnp.int32, s_old.shape, 1)
    s_new = jnp.where(pos_new < limit_new, s_new, -jnp.inf)
    s_old = jnp.where(pos_old < length, s_old, -jnp.inf)
    top = jnp.maximum(
        jnp.max(s_new, axis=1, keepdims=True), jnp.max(s_old, axis=1, keepdims=True)
    )
    e_new = jnp.exp(s_new - top)
    e_old = jnp.exp(s_old - top)
    total = jnp.sum(e_new, axis=1, keepdims=True) + jnp.sum(e_old, axis=1, keepdims=True)
    summed = jnp.dot(e_new.astype(jnp.bfloat16), v_new, preferred_element_type=jnp.float32)
    summed += jnp.dot(e_old.astype(jnp.bfloat16), v_old, preferred_element_type=jnp.float32)
    return summed / total


def attention_kernel(size, scalars, *refs):
    blocks = refs[:size]
    qkv_ref, keep_ref, send_ref, last_ref, k_old, v_old, att_scr, sems = refs[size:]
    rows = blocks[0].shape[0] // 2
    me_row, length, count = scalars[0], scalars[2], scalars[3]
    waits = []
    for mask in range(size):
        index = jnp.bitwise_xor(me_row, mask)
        for part, target in enumerate((k_old, v_old)):
            copy = pltpu.make_async_copy(
                blocks[mask].at[pl.ds(part * rows, rows), :],
                target.at[pl.ds(pl.multiple_of(index * rows, rows), rows), :],
                sems.at[part, mask],
            )
            copy.start()
            waits.append(copy)
    for copy in waits:
        copy.wait()
    span, total = qkv_ref.shape
    width = total // 3
    last = width - HEAD_DIM
    block = min(256, span)

    def attend(live):
        lane = lax.broadcasted_iota(jnp.int32, (block, 128), 1)
        left = lane < HEAD_DIM

        def heads(q_at, k_at, v_at, lo, wide):
            old_k, old_v = k_old[0:live, pl.ds(lo, wide)], v_old[0:live, pl.ds(lo, wide)]
            for begin in range(0, span, block):
                stop = begin + block
                q = qkv_ref[begin:stop, pl.ds(q_at, wide)]
                k_new = qkv_ref[0:stop, pl.ds(k_at, wide)]
                v_new = qkv_ref[0:stop, pl.ds(v_at, wide)]
                row = begin + lax.broadcasted_iota(jnp.int32, (block, 1), 0)
                limit = jnp.minimum(row + 1, count)
                if wide == 128:
                    zero = jnp.zeros_like(q)
                    both = jnp.where(
                        left,
                        attend_block(
                            jnp.where(left, q, zero), k_new, v_new, old_k, old_v, limit, length
                        ),
                        attend_block(
                            jnp.where(left, zero, q), k_new, v_new, old_k, old_v, limit, length
                        ),
                    )
                else:
                    both = attend_block(q, k_new, v_new, old_k, old_v, limit, length)
                att_scr[begin:stop, pl.ds(lo, wide)] = both.astype(jnp.bfloat16)

        @pl.loop(0, last // 128)
        def _(pair):
            lo = pl.multiple_of(pair * 128, 128)
            heads(lo, lo + width + HEAD_DIM, lo + 2 * width, lo, 128)

        heads(last, width, 2 * width + last, last, HEAD_DIM)

    @pl.when(length <= rows)
    def _():
        attend(rows)

    @pl.when(length > rows)
    def _():
        attend(size * rows)

    chunk = span // size
    for slot, ref in ((0, keep_ref), (1, send_ref), (2, keep_ref), (3, send_ref)):
        start = pl.multiple_of(jnp.bitwise_xor(me_row, slot) * chunk, chunk)
        at = slot // 2 * chunk
        ref[at : at + chunk, :] = att_scr[pl.ds(start, chunk), :]
    group = lax.div(count - 1, 16)
    rows16 = att_scr[pl.ds(pl.multiple_of(group * 16, 16), 16), :].astype(jnp.float32)
    at16 = lax.broadcasted_iota(jnp.int32, rows16.shape, 0) == count - 1 - group * 16
    row = jnp.sum(jnp.where(at16, rows16, 0.0), axis=0, keepdims=True)
    last_ref[...] = jnp.broadcast_to(row, last_ref.shape).astype(jnp.bfloat16)


NT = (((1,), (1,)), ((), ()))


def last_row_kernel(layout, block_rows, scalars, *refs):
    pieces = len(layout)
    weights = refs[:pieces]
    last_ref, in_ref, out_ref, w_scr, sems = refs[pieces:]
    columns = w_scr.shape[1]
    weights = [ref.at[:, 0:columns] for ref in weights]
    copies = weight_copies(weights, layout, w_scr, sems, scalars[1], block_rows)
    for copy in copies:
        copy.start()
    rows = in_ref.shape[0]
    local = scalars[3] - 1 - scalars[0] * rows
    group = jnp.clip(lax.div(local, 16), 0, rows // 16 - 1)
    rows16 = in_ref[pl.ds(pl.multiple_of(group * 16, 16), 16), :].astype(jnp.float32)
    at16 = lax.broadcasted_iota(jnp.int32, rows16.shape, 0) == local - group * 16
    residual = jnp.sum(jnp.where(at16, rows16, 0.0), axis=0, keepdims=True)
    for copy in copies:
        copy.wait()
    width = last_ref.shape[1]
    for tile in range(0, out_ref.shape[1], 256):
        share = lax.dot_general(
            last_ref[...],
            w_scr[tile : tile + 256, 0:width],
            NT,
            preferred_element_type=jnp.float32,
        )
        out_ref[:, tile : tile + 256] = share[0:1] + residual[:, tile : tile + 256]


def final_row_kernel(scalars, *refs):
    shares, (gain_ref, table_ref) = refs[:-2], refs[-2:]
    row = add_all(*[ref[...] for ref in shares]).astype(jnp.bfloat16).astype(jnp.float32)
    row = rms_scale(row, gain_ref[...]).astype(jnp.bfloat16).astype(jnp.float32)
    at = lax.broadcasted_iota(jnp.int32, table_ref.shape, 0) == scalars[1]
    table_ref[...] = jnp.where(at, row, 0.0).astype(jnp.bfloat16)


def merge_kernel(*refs):
    stats, out_ref = refs[:-1], refs[-1]
    out_ref[...] = merge_stats(*[ref[...] for ref in stats])


def logprobs_kernel(logits_ref, *refs):
    stats, out_ref = refs[:-1], refs[-1]
    merged = merge_stats(*[ref[...] for ref in stats])
    out_ref[...] = logits_ref[...] - merged[:, :1] - jnp.log(merged[:, 1:])


def project_kernel(layout, block_rows, scalars, *refs):
    pieces = len(layout)
    keep_ref, got_ref, in_ref, own_ref, mate_ref, w_scr, sems = refs[pieces:]
    copies = weight_copies(refs[:pieces], layout, w_scr, sems, scalars[1], block_rows)
    for copy in copies:
        copy.start()
    attended = jnp.concatenate([keep_ref[...], got_ref[...]], axis=1)
    for copy in copies:
        copy.wait()
    chunk = own_ref.shape[0]
    for tile in range(0, own_ref.shape[1], 256):
        to = tile + 256
        total = lax.dot_general(
            attended, w_scr[tile:to, :], NT, preferred_element_type=jnp.float32
        )
        own_ref[:, tile:to] = total[:chunk] + in_ref[:, tile:to].astype(jnp.float32)
        mate_ref[:, tile:to] = total[chunk:].astype(jnp.bfloat16)


def head_kernel(table_ref, *refs):
    weights, (logits_ref, stats_ref) = refs[:-2], refs[-2:]
    step = pl.program_id(0)
    wide = weights[0].shape[1]
    for index, ref in enumerate(weights):
        start = pl.multiple_of((step * len(weights) + index) * wide, 128)
        logits_ref[:, pl.ds(start, wide)] = jnp.dot(
            table_ref[...], ref[...], preferred_element_type=jnp.float32
        )

    @pl.when(step == pl.num_programs(0) - 1)
    def _():
        logits = logits_ref[...]
        top = jnp.max(logits, axis=1, keepdims=True)
        stats_ref[:, 0:1] = top
        stats_ref[:, 1:2] = jnp.sum(jnp.exp(logits - top), axis=1, keepdims=True)


def combine_all(value, axis, size, combine, width=4):
    bit = 1
    while bit < size:
        count = min(width, size // bit)
        others = [
            lax.ppermute(value, axis, xor_pairs(size, bit * index)) for index in range(1, count)
        ]
        value = combine(value, *others)
        bit *= count
    return value


def add_all(*tables):
    return functools.reduce(jnp.add, tables)


def merge_stats(*stats):
    top = functools.reduce(jnp.maximum, [one[:, :1] for one in stats])
    total = add_all(*[one[:, 1:] * jnp.exp(one[:, :1] - top) for one in stats])
    return jnp.concatenate([top, total], axis=1)


def merge(*stats):
    return pl.pallas_call(
        merge_kernel,
        out_shape=jax.ShapeDtypeStruct(stats[0].shape, jnp.float32),
        cost_estimate=FREE,
        name="merge",
    )(*stats)


def on_device(
    n_req,
    n_row,
    hidden_in,
    cache_len,
    new_count,
    key_cache,
    value_cache,
    attn_gain,
    w_query,
    w_key,
    w_value,
    w_out,
    final_gain,
    head_weight,
):
    me_row = lax.axis_index("row")
    me_req = lax.axis_index("req")
    inputs = hidden_in[0]
    rows, model = inputs.shape
    span = rows * n_row
    block_rows, width = w_query.shape
    length, count = cache_len[0], new_count[0]
    scalars = jnp.stack([me_row, me_req, length, count]).astype(jnp.int32)

    def params(mib):
        return pltpu.CompilerParams(vmem_limit_bytes=mib * 1024 * 1024)


    normed = rms_scale(inputs.astype(jnp.float32), attn_gain).astype(jnp.bfloat16)
    last = width - HEAD_DIM
    joined = jnp.concatenate([w_query, w_key[:, last:], w_key[:, :last], w_value], axis=1)

    def cache_for(owner):
        return jnp.concatenate(
            [
                lax.dynamic_slice_in_dim(key_cache[0], owner * width, width, 1),
                lax.dynamic_slice_in_dim(value_cache[0], owner * width, width, 1),
            ],
            axis=0,
        )

    cached_rows = key_cache.shape[1]

    joined = after(joined, normed)
    out_own = w_out.T
    weights = Rows(joined, n_req)
    got = weights.neighbours()
    cosine, sine = rotary_tables(length + jnp.arange(span, dtype=jnp.int32))
    out_next = lax.ppermute(out_own, "row", xor_pairs(n_row, 1))
    out_both = jnp.concatenate([out_own, out_next], axis=1)
    cached = [cache_for(jnp.bitwise_xor(me_row, mask)) for mask in range(n_row)]
    x_ups, x_downs, scalars, cosine, sine, out_both, own_block, *cached = gather_line(
        normed, n_row, scalars, cosine, sine, out_both, *cached
    )
    got, own = together(got, [joined])
    diagonal = weights.diagonal(got)
    others = weights.cores([*own, *got, *diagonal])
    pieces = weights.pieces(got, diagonal, others)
    layout = tuple(piece[1:] for piece in pieces)

    across = lax.ppermute(cached[1], "row", xor_pairs(n_row, 2))
    beside, behind = after_all([cached[0], cached[2]], across, x_ups[-1], x_downs[-1])
    old_blocks = [
        lax.ppermute(beside, "row", xor_pairs(n_row, 1)),
        across,
        lax.ppermute(behind, "row", xor_pairs(n_row, 3)),
    ]
    out_rows = Rows(after(out_both, *diagonal), n_req)
    out_got = out_rows.neighbours()
    out_got, out_block = together(out_got, [out_rows.block])
    out_diagonal = out_rows.diagonal(out_got)
    qkv = pl.pallas_call(
        functools.partial(qkv_kernel, n_row, layout, block_rows),
        out_shape=jax.ShapeDtypeStruct((span, 3 * width), jnp.bfloat16),
        in_specs=[SMEM] + [HBM] * (2 * n_row - 1 + len(pieces)) + [VMEM] * 2,
        out_specs=VMEM,
        scratch_shapes=[
            pltpu.VMEM((span, model), jnp.bfloat16),
            pltpu.VMEM((model, 3 * width), jnp.bfloat16),
            pltpu.SemaphoreType.DMA((n_row,)),
            pltpu.SemaphoreType.DMA((len(pieces),)),
        ],
        compiler_params=params(17),
        cost_estimate=pl.CostEstimate(
            flops=6 * span * model * width, bytes_accessed=14 * 2**20, transcendentals=0
        ),
        name="qkv",
    )(scalars, normed, *x_ups, *x_downs, *[piece[0] for piece in pieces], cosine, sine)

    out_here, _ = together([*out_block, *out_got, *out_diagonal], [qkv])
    out_others = out_rows.cores(out_here)
    out_pieces = out_rows.pieces(out_got, out_diagonal, out_others)

    chunk = span // n_row
    keep, send, last_attended = pl.pallas_call(
        functools.partial(attention_kernel, n_row),
        out_shape=(
            jax.ShapeDtypeStruct((2 * chunk, width), jnp.bfloat16),
            jax.ShapeDtypeStruct((2 * chunk, width), jnp.bfloat16),
            jax.ShapeDtypeStruct((16, width), jnp.bfloat16),
        ),
        in_specs=[SMEM] + [HBM] * (1 + len(old_blocks)) + [VMEM],
        out_specs=(VMEM, VMEM, VMEM),
        scratch_shapes=[
            pltpu.VMEM((cached_rows * n_row, width), jnp.bfloat16),
            pltpu.VMEM((cached_rows * n_row, width), jnp.bfloat16),
            pltpu.VMEM((span, width), jnp.bfloat16),
            pltpu.SemaphoreType.DMA((2, n_row)),
        ],
        compiler_params=params(11),
        cost_estimate=pl.CostEstimate(
            flops=6 * span * span * width, bytes_accessed=4 * 2**20, transcendentals=0
        ),
        name="attention",
    )(scalars, own_block, *old_blocks, qkv)

    out_layout = tuple(piece[1:] for piece in out_pieces)
    out_weights = [piece[0] for piece in out_pieces]
    own_columns = -(-width // 128) * 128
    share = pl.pallas_call(
        functools.partial(last_row_kernel, out_layout, block_rows),
        out_shape=jax.ShapeDtypeStruct((1, model), jnp.float32),
        in_specs=[SMEM] + [HBM] * len(out_weights) + [VMEM] * 2,
        out_specs=VMEM,
        scratch_shapes=[
            pltpu.VMEM((model, own_columns), jnp.bfloat16),
            pltpu.SemaphoreType.DMA((len(out_weights),)),
        ],
        compiler_params=params(7),
        cost_estimate=FREE,
        name="last_row",
    )(scalars, *out_weights, last_attended, inputs)

    shares = [share] + [
        lax.ppermute(share, "row", xor_pairs(n_row, mask)) for mask in range(1, n_row)
    ]

    got = after(lax.ppermute(send, "row", xor_pairs(n_row, 1)), share)
    own_sum, mate_part = pl.pallas_call(
        functools.partial(project_kernel, out_layout, block_rows),
        out_shape=(
            jax.ShapeDtypeStruct((chunk, model), jnp.float32),
            jax.ShapeDtypeStruct((chunk, model), jnp.bfloat16),
        ),
        in_specs=[SMEM] + [HBM] * len(out_weights) + [VMEM] * 3,
        out_specs=(VMEM, VMEM),
        scratch_shapes=[
            pltpu.VMEM((model, 2 * width), jnp.bfloat16),
            pltpu.SemaphoreType.DMA((len(out_weights),)),
        ],
        compiler_params=params(11),
        cost_estimate=pl.CostEstimate(
            flops=2 * span * model * width, bytes_accessed=8 * 2**20, transcendentals=0
        ),
        name="project",
    )(scalars, *out_weights, keep, got, inputs)
    mate_part, *shares = lax.optimization_barrier((mate_part, *shares))
    others = lax.ppermute(mate_part, "row", xor_pairs(n_row, 2))
    layer_rows = (own_sum + others.astype(jnp.float32)).astype(jnp.bfloat16)

    table = pl.pallas_call(
        final_row_kernel,
        out_shape=jax.ShapeDtypeStruct((n_req, model), jnp.bfloat16),
        in_specs=[SMEM] + [VMEM] * (n_row + 1),
        out_specs=VMEM,
        cost_estimate=FREE,
        name="final_row",
    )(scalars, *shares, final_gain[None])
    table = combine_all(table, "req", n_req, add_all, 2)
    vocab = head_weight.shape[1]
    wide, streams = 256, 5

    def columns(index):
        return pl.BlockSpec((model, wide), lambda step: (0, step * streams + index))

    logits, stats = pl.pallas_call(
        head_kernel,
        grid=(vocab // (wide * streams),),
        out_shape=(
            jax.ShapeDtypeStruct((n_req, vocab), jnp.float32),
            jax.ShapeDtypeStruct((n_req, 2), jnp.float32),
        ),
        in_specs=[
            pl.BlockSpec((n_req, model), lambda step: (0, 0)),
            *[columns(index) for index in range(streams)],
        ],
        out_specs=(
            pl.BlockSpec((n_req, vocab), lambda step: (0, 0)),
            pl.BlockSpec((n_req, 2), lambda step: (0, 0)),
        ),
        compiler_params=params(48),
        cost_estimate=FREE,
        name="head",
    )(table, *[head_weight] * streams)
    stats = combine_all(stats, "req", n_req, merge, 8)
    stats = after(stats, others)
    stats = [stats] + [
        lax.ppermute(stats, "row", xor_pairs(n_row, mask)) for mask in range(1, n_row)
    ]
    logprobs = pl.pallas_call(
        logprobs_kernel,
        out_shape=jax.ShapeDtypeStruct(logits.shape, jnp.float32),
        cost_estimate=FREE,
        name="logprobs",
    )(logits, *stats)
    return (layer_rows[None], logprobs)


def solution(mesh):
    placed = (
        P("req", "row", None),
        P("req"),
        P("req"),
        P("req", "row", None),
        P("req", "row", None),
        P(),
        P("req", "row"),
        P("req", "row"),
        P("req", "row"),
        P("row", "req"),
        P(),
        P(None, ("req", "row")),
    )
    return jax.shard_map(
        functools.partial(on_device, mesh.shape["req"], mesh.shape["row"]),
        mesh=mesh,
        in_specs=placed,
        out_specs=(P("req", "row", None), P(None, ("req", "row"))),
        check_vma=False,
    )
```

```python
import functools

import jax
import jax.numpy as jnp
from jax import lax
from jax.experimental import pallas as pl
from jax.experimental.pallas import tpu as pltpu
from jax.sharding import PartitionSpec as P

HEAD_DIM = 64
EPSILON = 1e-05
HBM = pl.BlockSpec(memory_space=pltpu.HBM)
SMEM = pl.BlockSpec(memory_space=pltpu.SMEM)
VMEM = pl.BlockSpec(memory_space=pltpu.VMEM)


def params(mib):
    return pltpu.CompilerParams(vmem_limit_bytes=mib * 1024 * 1024)


FREE = pl.CostEstimate(flops=0, bytes_accessed=0, transcendentals=0)


def rms_scale(values, gain_vec):
    return (
        values * lax.rsqrt(jnp.mean(values * values, axis=-1, keepdims=True) + EPSILON) * gain_vec
    )


def rotary_tables(places):
    half_dim = HEAD_DIM // 2
    frequency = 10000.0 ** (-jnp.arange(half_dim).astype(jnp.float32) / half_dim)
    angles = places.astype(jnp.float32)[:, None] * frequency[None, :]
    cosine, sine = jnp.cos(angles), jnp.sin(angles)
    return (
        jnp.concatenate([cosine] * 4, axis=1),
        jnp.concatenate([-sine, sine, -sine, sine], axis=1),
    )


def up_pairs(size, hop, first=0):
    return [(i, i + hop) for i in range(first, size - hop)]


def down_pairs(size, hop, last=None):
    last = size - 1 if last is None else last
    return [(i, i - hop) for i in range(hop, last + 1)]


def xor_pairs(size, bit):
    return [(i, i ^ bit) for i in range(size)]


def after(value, *earlier):
    return lax.optimization_barrier((value, *earlier))[0]


class Rows:
    def __init__(self, block, size):
        self.block, self.size, self.rows = block, size, block.shape[0]
        self.half = self.rows // 2

    def send(self, array, mask):
        return lax.ppermute(array, "req", xor_pairs(self.size, mask))

    def neighbours(self):
        if self.size != 8:
            return [lax.all_gather(self.block, "req", axis=0, tiled=True)]
        return [self.send(self.block, 2), self.send(self.block, 4)]

    def diagonal(self, got):
        if self.size != 8:
            return []
        half_x, half_y = lax.optimization_barrier((got[0][self.half :], got[1][: self.half]))
        return [self.send(half_y, 2), self.send(half_x, 4)]

    def cores(self, arrays):
        return [self.send(array, 1) for array in arrays] if self.size == 8 else []

    def pieces(self, got, diagonal, others):
        if self.size != 8:
            return [(got[0], None, 0, self.rows * self.size)]
        places = [
            (0, 0, self.rows),
            (2, 0, self.rows),
            (4, 0, self.rows),
            (6, 0, self.half),
            (6, self.half, self.half),
        ]
        pieces = []
        for here, there, (mask, at, count) in zip(
            [self.block, *got, *diagonal], others, places, strict=True
        ):
            pieces += [(here, mask, at, count), (there, mask ^ 1, at, count)]
        return pieces


def after_all(values, *earlier):
    return list(lax.optimization_barrier((*values, *earlier)))[: len(values)]


def gather_line(block, size, *ready):
    ups, downs = [], []
    up, down = block, block
    for step in range(1, size):
        up = lax.ppermute(up, "row", up_pairs(size, 1, step - 1))
        down = lax.ppermute(down, "row", down_pairs(size, 1, size - step))
        if step == size - 2:
            up, down, *ready = lax.optimization_barrier((up, down, *ready))
        else:
            up, down = lax.optimization_barrier((up, down))
        ups.append(up)
        downs.append(down)
    return ups, downs, *ready


def together(*groups):
    flat = lax.optimization_barrier(tuple(array for group in groups for array in group))
    result, at = [], 0
    for group in groups:
        result.append(list(flat[at : at + len(group)]))
        at += len(group)
    return result


def weight_copies(refs, layout, target, sems, me_req, block_rows):
    copies = []
    for index, (ref, (mask, first, count)) in enumerate(zip(refs, layout)):
        if mask is None:
            start = 0
        else:
            start = pl.multiple_of(jnp.bitwise_xor(me_req, mask) * block_rows + first, 16)
        copies.append(pltpu.make_async_copy(ref, target.at[pl.ds(start, count), :], sems.at[index]))
    return copies


def start_line_copies(own, ups, downs, target, sems, me_row, rows):
    size = len(ups) + 1
    waits = []
    own_copy = pltpu.make_async_copy(own, target.at[pl.ds(me_row * rows, rows), :], sems.at[0])
    own_copy.start()
    waits.append(own_copy)
    for hop in range(1, size):
        index = lax.rem(me_row - hop + size, size)
        place = target.at[pl.ds(pl.multiple_of(index * rows, rows), rows), :]
        below = pltpu.make_async_copy(ups[hop - 1], place, sems.at[hop])
        above = pltpu.make_async_copy(downs[size - hop - 1], place, sems.at[hop])

        @pl.when(me_row >= hop)
        def _(below=below):
            below.start()

        @pl.when(me_row < hop)
        def _(above=above):
            above.start()

        waits.append(below)
    return waits


def qkv_kernel(size, layout, block_rows, scalars, *refs):
    pieces = len(layout)
    own, ups, downs = refs[0], refs[1:size], refs[size : 2 * size - 1]
    weights = refs[2 * size - 1 : 2 * size - 1 + pieces]
    cos_ref, sin_ref, out_ref, x_scr, w_scr, x_sems, w_sems = refs[2 * size - 1 + pieces :]
    rows = own.shape[0]
    total = out_ref.shape[1]
    copies = weight_copies(weights, layout, w_scr, w_sems, scalars[1], block_rows)
    for copy in copies:
        copy.start()
    waits = start_line_copies(own, ups, downs, x_scr, x_sems, scalars[0], rows)
    for copy in waits + copies:
        copy.wait()
    span = x_scr.shape[0]
    width = total // 3
    half = HEAD_DIM // 2
    lane = lax.broadcasted_iota(jnp.int32, (span, 128), 1)
    first_half = lax.rem(lane, HEAD_DIM) < half
    cosine, sine = cos_ref[...], sin_ref[...]
    for tile in range(0, total, 256):
        end = min(tile + 256, total)
        raw = jnp.dot(x_scr[...], w_scr[:, tile:end], preferred_element_type=jnp.float32)
        for at in range(tile, end, 128):
            stop = min(at + 128, end)
            part = raw[:, at - tile : stop - tile]
            if at < 2 * width:
                swapped = jnp.where(
                    first_half, pltpu.roll(part, 128 - half, 1), pltpu.roll(part, half, 1)
                )
                part = part * cosine + swapped * sine
                if stop <= width:
                    part = part * (HEAD_DIM**-0.5)
                elif at < width:
                    part = jnp.where(lane < width - at, part * (HEAD_DIM**-0.5), part)
            out_ref[:, at:stop] = part.astype(jnp.bfloat16)


def attend_block(q, k_new, v_new, k_old, v_old, limit_new, length):
    nt = (((1,), (1,)), ((), ()))
    s_new = lax.dot_general(q, k_new, nt, preferred_element_type=jnp.float32)
    s_old = lax.dot_general(q, k_old, nt, preferred_element_type=jnp.float32)
    pos_new = lax.broadcasted_iota(jnp.int32, s_new.shape, 1)
    pos_old = lax.broadcasted_iota(jnp.int32, s_old.shape, 1)
    s_new = jnp.where(pos_new < limit_new, s_new, -jnp.inf)
    s_old = jnp.where(pos_old < length, s_old, -jnp.inf)
    top = jnp.maximum(
        jnp.max(s_new, axis=1, keepdims=True), jnp.max(s_old, axis=1, keepdims=True)
    )
    e_new = jnp.exp(s_new - top)
    e_old = jnp.exp(s_old - top)
    total = jnp.sum(e_new, axis=1, keepdims=True) + jnp.sum(e_old, axis=1, keepdims=True)
    summed = jnp.dot(e_new.astype(jnp.bfloat16), v_new, preferred_element_type=jnp.float32)
    summed += jnp.dot(e_old.astype(jnp.bfloat16), v_old, preferred_element_type=jnp.float32)
    return summed / total


def attention_kernel(size, scalars, *refs):
    blocks = refs[:size]
    qkv_ref, keep_ref, send_ref, last_ref, k_old, v_old, att_scr, sems = refs[size:]
    rows = blocks[0].shape[0] // 2
    me_row, length, count = scalars[0], scalars[2], scalars[3]
    waits = []
    for mask in range(size):
        index = jnp.bitwise_xor(me_row, mask)
        for part, target in enumerate((k_old, v_old)):
            copy = pltpu.make_async_copy(
                blocks[mask].at[pl.ds(part * rows, rows), :],
                target.at[pl.ds(pl.multiple_of(index * rows, rows), rows), :],
                sems.at[part, mask],
            )
            copy.start()
            waits.append(copy)
    for copy in waits:
        copy.wait()
    span, total = qkv_ref.shape
    width = total // 3
    last = width - HEAD_DIM
    block = min(256, span)

    def attend(live):
        lane = lax.broadcasted_iota(jnp.int32, (block, 128), 1)
        left = lane < HEAD_DIM

        def heads(q_at, k_at, v_at, lo, wide):
            old_k, old_v = k_old[0:live, pl.ds(lo, wide)], v_old[0:live, pl.ds(lo, wide)]
            for begin in range(0, span, block):
                stop = begin + block
                q = qkv_ref[begin:stop, pl.ds(q_at, wide)]
                k_new = qkv_ref[0:stop, pl.ds(k_at, wide)]
                v_new = qkv_ref[0:stop, pl.ds(v_at, wide)]
                row = begin + lax.broadcasted_iota(jnp.int32, (block, 1), 0)
                limit = jnp.minimum(row + 1, count)
                if wide == 128:
                    zero = jnp.zeros_like(q)
                    both = jnp.where(
                        left,
                        attend_block(
                            jnp.where(left, q, zero), k_new, v_new, old_k, old_v, limit, length
                        ),
                        attend_block(
                            jnp.where(left, zero, q), k_new, v_new, old_k, old_v, limit, length
                        ),
                    )
                else:
                    both = attend_block(q, k_new, v_new, old_k, old_v, limit, length)
                att_scr[begin:stop, pl.ds(lo, wide)] = both.astype(jnp.bfloat16)

        @pl.loop(0, last // 128)
        def _(pair):
            lo = pl.multiple_of(pair * 128, 128)
            heads(lo, lo + width + HEAD_DIM, lo + 2 * width, lo, 128)

        heads(last, width, 2 * width + last, last, HEAD_DIM)

    @pl.when(length <= rows)
    def _():
        attend(rows)

    @pl.when(length > rows)
    def _():
        attend(size * rows)

    chunk = span // size
    for slot, ref in ((0, keep_ref), (1, send_ref), (2, keep_ref), (3, send_ref)):
        start = pl.multiple_of(jnp.bitwise_xor(me_row, slot) * chunk, chunk)
        at = slot // 2 * chunk
        ref[at : at + chunk, :] = att_scr[pl.ds(start, chunk), :]
    group = lax.div(count - 1, 16)
    rows16 = att_scr[pl.ds(pl.multiple_of(group * 16, 16), 16), :].astype(jnp.float32)
    at16 = lax.broadcasted_iota(jnp.int32, rows16.shape, 0) == count - 1 - group * 16
    row = jnp.sum(jnp.where(at16, rows16, 0.0), axis=0, keepdims=True)
    last_ref[...] = jnp.broadcast_to(row, last_ref.shape).astype(jnp.bfloat16)


NT = (((1,), (1,)), ((), ()))


def last_row_kernel(layout, block_rows, scalars, *refs):
    pieces = len(layout)
    weights = refs[:pieces]
    last_ref, in_ref, out_ref, w_scr, sems = refs[pieces:]
    columns = w_scr.shape[1]
    weights = [ref.at[:, 0:columns] for ref in weights]
    copies = weight_copies(weights, layout, w_scr, sems, scalars[1], block_rows)
    for copy in copies:
        copy.start()
    rows = in_ref.shape[0]
    local = scalars[3] - 1 - scalars[0] * rows
    group = jnp.clip(lax.div(local, 16), 0, rows // 16 - 1)
    rows16 = in_ref[pl.ds(pl.multiple_of(group * 16, 16), 16), :].astype(jnp.float32)
    at16 = lax.broadcasted_iota(jnp.int32, rows16.shape, 0) == local - group * 16
    residual = jnp.sum(jnp.where(at16, rows16, 0.0), axis=0, keepdims=True)
    for copy in copies:
        copy.wait()
    width = last_ref.shape[1]
    here = lax.broadcasted_iota(jnp.int32, (out_ref.shape[0], 256), 0) == scalars[1]
    for tile in range(0, out_ref.shape[1], 256):
        share = lax.dot_general(
            last_ref[...],
            w_scr[tile : tile + 256, 0:width],
            NT,
            preferred_element_type=jnp.float32,
        )
        row = share[0:1] + residual[:, tile : tile + 256]
        out_ref[:, tile : tile + 256] = jnp.where(here, row, 0.0)


def final_rows_kernel(*refs):
    shares, (gain_ref, table_ref) = refs[:-2], refs[-2:]
    rows = add_all(*[ref[...] for ref in shares]).astype(jnp.bfloat16).astype(jnp.float32)
    table_ref[...] = rms_scale(rows, gain_ref[...][None]).astype(jnp.bfloat16)


def merge_kernel(*refs):
    stats, out_ref = refs[:-1], refs[-1]
    out_ref[...] = merge_stats(*[ref[...] for ref in stats])


def logprobs_kernel(logits_ref, *refs):
    stats, out_ref = refs[:-1], refs[-1]
    merged = merge_stats(*[ref[...] for ref in stats])
    out_ref[...] = logits_ref[...] - merged[:, :1] - jnp.log(merged[:, 1:])


def project_kernel(layout, block_rows, scalars, *refs):
    pieces = len(layout)
    keep_ref, got_ref, in_ref, own_ref, mate_ref, w_scr, sems = refs[pieces:]
    copies = weight_copies(refs[:pieces], layout, w_scr, sems, scalars[1], block_rows)
    for copy in copies:
        copy.start()
    attended = jnp.concatenate([keep_ref[...], got_ref[...]], axis=1)
    for copy in copies:
        copy.wait()
    chunk = own_ref.shape[0]
    for tile in range(0, own_ref.shape[1], 256):
        to = tile + 256
        total = lax.dot_general(
            attended, w_scr[tile:to, :], NT, preferred_element_type=jnp.float32
        )
        own_ref[:, tile:to] = total[:chunk] + in_ref[:, tile:to].astype(jnp.float32)
        mate_ref[:, tile:to] = total[chunk:].astype(jnp.bfloat16)


def head_kernel(streams, *refs):
    tables, refs = refs[: -streams - 2], refs[-streams - 2 :]
    weights, (logits_ref, stats_ref) = refs[:-2], refs[-2:]
    table = add_all(*[ref[...] for ref in tables])
    step = pl.program_id(0)
    wide = weights[0].shape[1]
    for index, ref in enumerate(weights):
        start = pl.multiple_of((step * len(weights) + index) * wide, 128)
        logits_ref[:, pl.ds(start, wide)] = jnp.dot(
            table, ref[...], preferred_element_type=jnp.float32
        )

    @pl.when(step == pl.num_programs(0) - 1)
    def _():
        logits = logits_ref[...]
        top = jnp.max(logits, axis=1, keepdims=True)
        stats_ref[:, 0:1] = top
        stats_ref[:, 1:2] = jnp.sum(jnp.exp(logits - top), axis=1, keepdims=True)


def exchange_all(value, axis, size, bit, combine=None):
    values = [value]
    while bit < size:
        count = min(4, size // bit)
        if len(values) > 1:
            value = combine(*values)
        values = [value] + [
            lax.ppermute(value, axis, xor_pairs(size, bit * index)) for index in range(1, count)
        ]
        bit *= count
    return values


def add_all(*tables):
    return functools.reduce(jnp.add, tables)


def merge_stats(*stats):
    top = functools.reduce(jnp.maximum, [one[:, :1] for one in stats])
    total = add_all(*[one[:, 1:] * jnp.exp(one[:, :1] - top) for one in stats])
    return jnp.concatenate([top, total], axis=1)


def merge(*stats):
    return pl.pallas_call(
        merge_kernel,
        out_shape=jax.ShapeDtypeStruct(stats[0].shape, jnp.float32),
        compiler_params=params(4),
        cost_estimate=FREE,
        name="merge",
    )(*stats)


def on_device(
    n_req,
    n_row,
    hidden_in,
    cache_len,
    new_count,
    key_cache,
    value_cache,
    attn_gain,
    w_query,
    w_key,
    w_value,
    w_out,
    final_gain,
    head_weight,
):
    me_row = lax.axis_index("row")
    me_req = lax.axis_index("req")
    inputs = hidden_in[0]
    rows, model = inputs.shape
    span = rows * n_row
    block_rows, width = w_query.shape
    length, count = cache_len[0], new_count[0]
    scalars = jnp.stack([me_row, me_req, length, count]).astype(jnp.int32)

    normed = rms_scale(inputs.astype(jnp.float32), attn_gain).astype(jnp.bfloat16)
    last = width - HEAD_DIM
    joined = jnp.concatenate([w_query, w_key[:, last:], w_key[:, :last], w_value], axis=1)

    def cache_for(owner):
        return jnp.concatenate(
            [
                lax.dynamic_slice_in_dim(key_cache[0], owner * width, width, 1),
                lax.dynamic_slice_in_dim(value_cache[0], owner * width, width, 1),
            ],
            axis=0,
        )

    cached_rows = key_cache.shape[1]

    joined = after(joined, normed)
    out_own = w_out.T
    weights = Rows(joined, n_req)
    got = weights.neighbours()
    cosine, sine = rotary_tables(length + jnp.arange(span, dtype=jnp.int32))
    out_next = lax.ppermute(out_own, "row", xor_pairs(n_row, 1))
    out_both = jnp.concatenate([out_own, out_next], axis=1)
    cached = [cache_for(jnp.bitwise_xor(me_row, mask)) for mask in range(n_row)]
    x_ups, x_downs, scalars, cosine, sine, out_both, own_block, *cached = gather_line(
        normed, n_row, scalars, cosine, sine, out_both, *cached
    )
    got, own = together(got, [joined])
    diagonal = weights.diagonal(got)
    others = weights.cores([*own, *got, *diagonal])
    pieces = weights.pieces(got, diagonal, others)
    layout = tuple(piece[1:] for piece in pieces)

    across = lax.ppermute(cached[1], "row", xor_pairs(n_row, 2))
    beside, behind = after_all([cached[0], cached[2]], across, x_ups[-1], x_downs[-1])
    old_blocks = [
        lax.ppermute(beside, "row", xor_pairs(n_row, 1)),
        across,
        lax.ppermute(behind, "row", xor_pairs(n_row, 3)),
    ]
    out_rows = Rows(after(out_both, *diagonal), n_req)
    out_got = out_rows.neighbours()
    out_got, out_block = together(out_got, [out_rows.block])
    out_diagonal = out_rows.diagonal(out_got)
    qkv = pl.pallas_call(
        functools.partial(qkv_kernel, n_row, layout, block_rows),
        out_shape=jax.ShapeDtypeStruct((span, 3 * width), jnp.bfloat16),
        in_specs=[SMEM] + [HBM] * (2 * n_row - 1 + len(pieces)) + [VMEM] * 2,
        out_specs=VMEM,
        scratch_shapes=[
            pltpu.VMEM((span, model), jnp.bfloat16),
            pltpu.VMEM((model, 3 * width), jnp.bfloat16),
            pltpu.SemaphoreType.DMA((n_row,)),
            pltpu.SemaphoreType.DMA((len(pieces),)),
        ],
        compiler_params=params(17),
        cost_estimate=pl.CostEstimate(
            flops=6 * span * model * width, bytes_accessed=14 * 2**20, transcendentals=0
        ),
        name="qkv",
    )(scalars, normed, *x_ups, *x_downs, *[piece[0] for piece in pieces], cosine, sine)

    out_here, old_blocks, _ = together([*out_block, *out_got, *out_diagonal], old_blocks, [qkv])
    out_others = out_rows.cores(out_here)
    out_pieces = out_rows.pieces(out_got, out_diagonal, out_others)

    chunk = span // n_row
    keep, send, last_attended = pl.pallas_call(
        functools.partial(attention_kernel, n_row),
        out_shape=(
            jax.ShapeDtypeStruct((2 * chunk, width), jnp.bfloat16),
            jax.ShapeDtypeStruct((2 * chunk, width), jnp.bfloat16),
            jax.ShapeDtypeStruct((16, width), jnp.bfloat16),
        ),
        in_specs=[SMEM] + [HBM] * (1 + len(old_blocks)) + [VMEM],
        out_specs=(VMEM, VMEM, VMEM),
        scratch_shapes=[
            pltpu.VMEM((cached_rows * n_row, width), jnp.bfloat16),
            pltpu.VMEM((cached_rows * n_row, width), jnp.bfloat16),
            pltpu.VMEM((span, width), jnp.bfloat16),
            pltpu.SemaphoreType.DMA((2, n_row)),
        ],
        compiler_params=params(11),
        cost_estimate=pl.CostEstimate(
            flops=6 * span * span * width, bytes_accessed=4 * 2**20, transcendentals=0
        ),
        name="attention",
    )(scalars, own_block, *old_blocks, qkv)

    out_layout = tuple(piece[1:] for piece in out_pieces)
    out_weights = [piece[0] for piece in out_pieces]
    own_columns = -(-width // 128) * 128
    share = pl.pallas_call(
        functools.partial(last_row_kernel, out_layout, block_rows),
        out_shape=jax.ShapeDtypeStruct((n_req, model), jnp.float32),
        in_specs=[SMEM] + [HBM] * len(out_weights) + [VMEM] * 2,
        out_specs=VMEM,
        scratch_shapes=[
            pltpu.VMEM((model, own_columns), jnp.bfloat16),
            pltpu.SemaphoreType.DMA((len(out_weights),)),
        ],
        compiler_params=params(7),
        cost_estimate=FREE,
        name="last_row",
    )(scalars, *out_weights, last_attended, inputs)

    pair = lax.ppermute(share, "req", xor_pairs(n_req, 1))
    share = share + pair
    shares = [share] + [
        lax.ppermute(share, "row", xor_pairs(n_row, mask)) for mask in range(1, n_row)
    ]

    got = after(lax.ppermute(send, "row", xor_pairs(n_row, 1)), share)
    own_sum, mate_part = pl.pallas_call(
        functools.partial(project_kernel, out_layout, block_rows),
        out_shape=(
            jax.ShapeDtypeStruct((chunk, model), jnp.float32),
            jax.ShapeDtypeStruct((chunk, model), jnp.bfloat16),
        ),
        in_specs=[SMEM] + [HBM] * len(out_weights) + [VMEM] * 3,
        out_specs=(VMEM, VMEM),
        scratch_shapes=[
            pltpu.VMEM((model, 2 * width), jnp.bfloat16),
            pltpu.SemaphoreType.DMA((len(out_weights),)),
        ],
        compiler_params=params(11),
        cost_estimate=pl.CostEstimate(
            flops=2 * span * model * width, bytes_accessed=8 * 2**20, transcendentals=0
        ),
        name="project",
    )(scalars, *out_weights, keep, got, inputs)
    mate_part, *shares = lax.optimization_barrier((mate_part, *shares))
    others = lax.ppermute(mate_part, "row", xor_pairs(n_row, 2))
    layer_rows = (own_sum + others.astype(jnp.float32)).astype(jnp.bfloat16)

    table = pl.pallas_call(
        final_rows_kernel,
        out_shape=jax.ShapeDtypeStruct((n_req, model), jnp.bfloat16),
        compiler_params=params(4),
        cost_estimate=FREE,
        name="final_rows",
    )(*shares, final_gain)
    tables = exchange_all(table, "req", n_req, 2, add_all)
    vocab = head_weight.shape[1]
    wide, streams = 256, 5

    def columns(index):
        return pl.BlockSpec((model, wide), lambda step: (0, step * streams + index))

    logits, stats = pl.pallas_call(
        functools.partial(head_kernel, streams),
        grid=(vocab // (wide * streams),),
        out_shape=(
            jax.ShapeDtypeStruct((n_req, vocab), jnp.float32),
            jax.ShapeDtypeStruct((n_req, 2), jnp.float32),
        ),
        in_specs=[
            *[pl.BlockSpec((n_req, model), lambda step: (0, 0))] * len(tables),
            *[columns(index) for index in range(streams)],
        ],
        out_specs=(
            pl.BlockSpec((n_req, vocab), lambda step: (0, 0)),
            pl.BlockSpec((n_req, 2), lambda step: (0, 0)),
        ),
        compiler_params=params(48),
        cost_estimate=FREE,
        name="head",
    )(*tables, *[head_weight] * streams)
    stats = merge(*exchange_all(stats, "req", n_req, 2, merge))
    stats = merge(stats, lax.ppermute(stats, "req", xor_pairs(n_req, 1)))
    stats = exchange_all(after(stats, others), "row", n_row, 1, merge)
    logprobs = pl.pallas_call(
        logprobs_kernel,
        out_shape=jax.ShapeDtypeStruct(logits.shape, jnp.float32),
        compiler_params=params(4),
        cost_estimate=FREE,
        name="logprobs",
    )(logits, *stats)
    return (layer_rows[None], logprobs)


def solution(mesh):
    placed = (
        P("req", "row", None),
        P("req"),
        P("req"),
        P("req", "row", None),
        P("req", "row", None),
        P(),
        P("req", "row"),
        P("req", "row"),
        P("req", "row"),
        P("row", "req"),
        P(),
        P(None, ("req", "row")),
    )
    return jax.shard_map(
        functools.partial(on_device, mesh.shape["req"], mesh.shape["row"]),
        mesh=mesh,
        in_specs=placed,
        out_specs=(P("req", "row", None), P(None, ("req", "row"))),
        check_vma=False,
    )
```

```python
import functools

import jax
import jax.numpy as jnp
from jax import lax
from jax.experimental import pallas as pl
from jax.experimental.pallas import tpu as pltpu
from jax.sharding import PartitionSpec as P

HEAD_DIM = 64
EPSILON = 1e-05
HBM = pl.BlockSpec(memory_space=pltpu.HBM)
SMEM = pl.BlockSpec(memory_space=pltpu.SMEM)
VMEM = pl.BlockSpec(memory_space=pltpu.VMEM)


def params(mib):
    return pltpu.CompilerParams(vmem_limit_bytes=mib * 1024 * 1024)


FREE = pl.CostEstimate(flops=0, bytes_accessed=0, transcendentals=0)


def rms_scale(values, gain_vec):
    return (
        values * lax.rsqrt(jnp.mean(values * values, axis=-1, keepdims=True) + EPSILON) * gain_vec
    )


def rotary_tables(places):
    half_dim = HEAD_DIM // 2
    frequency = 10000.0 ** (-jnp.arange(half_dim).astype(jnp.float32) / half_dim)
    angles = places.astype(jnp.float32)[:, None] * frequency[None, :]
    cosine, sine = jnp.cos(angles), jnp.sin(angles)
    return (
        jnp.concatenate([cosine] * 4, axis=1),
        jnp.concatenate([-sine, sine, -sine, sine], axis=1),
    )


def up_pairs(size, hop, first=0):
    return [(i, i + hop) for i in range(first, size - hop)]


def down_pairs(size, hop, last=None):
    last = size - 1 if last is None else last
    return [(i, i - hop) for i in range(hop, last + 1)]


def xor_pairs(size, bit):
    return [(i, i ^ bit) for i in range(size)]


def after(value, *earlier):
    return lax.optimization_barrier((value, *earlier))[0]


class Rows:
    def __init__(self, block, size):
        self.block, self.size, self.rows = block, size, block.shape[0]
        self.half = self.rows // 2

    def send(self, array, mask):
        return lax.ppermute(array, "req", xor_pairs(self.size, mask))

    def neighbours(self):
        if self.size != 8:
            return [lax.all_gather(self.block, "req", axis=0, tiled=True)]
        return [self.send(self.block, 2), self.send(self.block, 4)]

    def diagonal(self, got):
        if self.size != 8:
            return []
        half_x, half_y = lax.optimization_barrier((got[0][self.half :], got[1][: self.half]))
        return [self.send(half_y, 2), self.send(half_x, 4)]

    def cores(self, arrays):
        return [self.send(array, 1) for array in arrays] if self.size == 8 else []

    def pieces(self, got, diagonal, others):
        if self.size != 8:
            return [(got[0], None, 0, self.rows * self.size)]
        places = [
            (0, 0, self.rows),
            (2, 0, self.rows),
            (4, 0, self.rows),
            (6, 0, self.half),
            (6, self.half, self.half),
        ]
        pieces = []
        for here, there, (mask, at, count) in zip(
            [self.block, *got, *diagonal], others, places, strict=True
        ):
            pieces += [(here, mask, at, count), (there, mask ^ 1, at, count)]
        return pieces


def after_all(values, *earlier):
    return list(lax.optimization_barrier((*values, *earlier)))[: len(values)]


def gather_line(block, size, *ready):
    ups, downs = [], []
    up, down = block, block
    for step in range(1, size):
        up = lax.ppermute(up, "row", up_pairs(size, 1, step - 1))
        down = lax.ppermute(down, "row", down_pairs(size, 1, size - step))
        if step == size - 2:
            up, down, *ready = lax.optimization_barrier((up, down, *ready))
        else:
            up, down = lax.optimization_barrier((up, down))
        ups.append(up)
        downs.append(down)
    return ups, downs, *ready


def together(*groups):
    flat = lax.optimization_barrier(tuple(array for group in groups for array in group))
    result, at = [], 0
    for group in groups:
        result.append(list(flat[at : at + len(group)]))
        at += len(group)
    return result


def weight_copies(refs, layout, target, sems, me_req, block_rows):
    copies = []
    for index, (ref, (mask, first, count)) in enumerate(zip(refs, layout)):
        if mask is None:
            start = 0
        else:
            start = pl.multiple_of(jnp.bitwise_xor(me_req, mask) * block_rows + first, 16)
        copies.append(pltpu.make_async_copy(ref, target.at[pl.ds(start, count), :], sems.at[index]))
    return copies


def start_line_copies(own, ups, downs, target, sems, me_row, rows):
    size = len(ups) + 1
    waits = []
    own_copy = pltpu.make_async_copy(own, target.at[pl.ds(me_row * rows, rows), :], sems.at[0])
    own_copy.start()
    waits.append(own_copy)
    for hop in range(1, size):
        index = lax.rem(me_row - hop + size, size)
        place = target.at[pl.ds(pl.multiple_of(index * rows, rows), rows), :]
        below = pltpu.make_async_copy(ups[hop - 1], place, sems.at[hop])
        above = pltpu.make_async_copy(downs[size - hop - 1], place, sems.at[hop])

        @pl.when(me_row >= hop)
        def _(below=below):
            below.start()

        @pl.when(me_row < hop)
        def _(above=above):
            above.start()

        waits.append(below)
    return waits


def qkv_kernel(size, layout, block_rows, scalars, *refs):
    pieces = len(layout)
    own, ups, downs = refs[0], refs[1:size], refs[size : 2 * size - 1]
    weights = refs[2 * size - 1 : 2 * size - 1 + pieces]
    cos_ref, sin_ref, out_ref, x_scr, w_scr, x_sems, w_sems = refs[2 * size - 1 + pieces :]
    rows = own.shape[0]
    total = out_ref.shape[1]
    copies = weight_copies(weights, layout, w_scr, w_sems, scalars[1], block_rows)
    for copy in copies:
        copy.start()
    waits = start_line_copies(own, ups, downs, x_scr, x_sems, scalars[0], rows)
    for copy in waits + copies:
        copy.wait()
    span = x_scr.shape[0]
    width = total // 3
    half = HEAD_DIM // 2
    lane = lax.broadcasted_iota(jnp.int32, (span, 128), 1)
    first_half = lax.rem(lane, HEAD_DIM) < half
    cosine, sine = cos_ref[...], sin_ref[...]
    for tile in range(0, total, 256):
        end = min(tile + 256, total)
        raw = jnp.dot(x_scr[...], w_scr[:, tile:end], preferred_element_type=jnp.float32)
        for at in range(tile, end, 128):
            stop = min(at + 128, end)
            part = raw[:, at - tile : stop - tile]
            if at < 2 * width:
                swapped = jnp.where(
                    first_half, pltpu.roll(part, 128 - half, 1), pltpu.roll(part, half, 1)
                )
                part = part * cosine + swapped * sine
                if stop <= width:
                    part = part * (HEAD_DIM**-0.5)
                elif at < width:
                    part = jnp.where(lane < width - at, part * (HEAD_DIM**-0.5), part)
            out_ref[:, at:stop] = part.astype(jnp.bfloat16)


def attend_block(q, k_new, v_new, k_old, v_old, limit_new, length):
    nt = (((1,), (1,)), ((), ()))
    s_new = lax.dot_general(q, k_new, nt, preferred_element_type=jnp.float32)
    s_old = lax.dot_general(q, k_old, nt, preferred_element_type=jnp.float32)
    pos_new = lax.broadcasted_iota(jnp.int32, s_new.shape, 1)
    pos_old = lax.broadcasted_iota(jnp.int32, s_old.shape, 1)
    s_new = jnp.where(pos_new < limit_new, s_new, -jnp.inf)
    s_old = jnp.where(pos_old < length, s_old, -jnp.inf)
    top = jnp.maximum(
        jnp.max(s_new, axis=1, keepdims=True), jnp.max(s_old, axis=1, keepdims=True)
    )
    e_new = jnp.exp(s_new - top)
    e_old = jnp.exp(s_old - top)
    total = jnp.sum(e_new, axis=1, keepdims=True) + jnp.sum(e_old, axis=1, keepdims=True)
    summed = jnp.dot(e_new.astype(jnp.bfloat16), v_new, preferred_element_type=jnp.float32)
    summed += jnp.dot(e_old.astype(jnp.bfloat16), v_old, preferred_element_type=jnp.float32)
    return summed / total


def attention_kernel(size, scalars, *refs):
    blocks = refs[:size]
    qkv_ref, keep_ref, send_ref, last_ref, k_old, v_old, att_scr, sems = refs[size:]
    rows = blocks[0].shape[0] // 2
    me_row, length, count = scalars[0], scalars[2], scalars[3]
    waits = []
    for mask in range(size):
        index = jnp.bitwise_xor(me_row, mask)
        for part, target in enumerate((k_old, v_old)):
            copy = pltpu.make_async_copy(
                blocks[mask].at[pl.ds(part * rows, rows), :],
                target.at[pl.ds(pl.multiple_of(index * rows, rows), rows), :],
                sems.at[part, mask],
            )
            copy.start()
            waits.append(copy)
    for copy in waits:
        copy.wait()
    span, total = qkv_ref.shape
    width = total // 3
    last = width - HEAD_DIM
    block = min(256, span)

    def attend(live):
        lane = lax.broadcasted_iota(jnp.int32, (block, 128), 1)
        left = lane < HEAD_DIM

        def heads(q_at, k_at, v_at, lo, wide):
            old_k, old_v = k_old[0:live, pl.ds(lo, wide)], v_old[0:live, pl.ds(lo, wide)]
            for begin in range(0, span, block):
                stop = begin + block
                q = qkv_ref[begin:stop, pl.ds(q_at, wide)]
                k_new = qkv_ref[0:stop, pl.ds(k_at, wide)]
                v_new = qkv_ref[0:stop, pl.ds(v_at, wide)]
                row = begin + lax.broadcasted_iota(jnp.int32, (block, 1), 0)
                limit = jnp.minimum(row + 1, count)
                if wide == 128:
                    zero = jnp.zeros_like(q)
                    stacked = jnp.concatenate(
                        [jnp.where(left, q, zero), jnp.where(left, zero, q)], axis=0
                    )
                    limits = jnp.concatenate([limit, limit], axis=0)
                    got = attend_block(stacked, k_new, v_new, old_k, old_v, limits, length)
                    both = jnp.where(left, got[:block], got[block:])
                else:
                    both = attend_block(q, k_new, v_new, old_k, old_v, limit, length)
                att_scr[begin:stop, pl.ds(lo, wide)] = both.astype(jnp.bfloat16)

        for lo in range(0, last, 128):
            heads(lo, lo + width + HEAD_DIM, lo + 2 * width, lo, 128)

        heads(last, width, 2 * width + last, last, HEAD_DIM)

    @pl.when(length <= rows)
    def _():
        attend(rows)

    @pl.when(length > rows)
    def _():
        attend(size * rows)

    chunk = span // size
    for slot, ref in ((0, keep_ref), (1, send_ref), (2, keep_ref), (3, send_ref)):
        start = pl.multiple_of(jnp.bitwise_xor(me_row, slot) * chunk, chunk)
        at = slot // 2 * chunk
        ref[at : at + chunk, :] = att_scr[pl.ds(start, chunk), :]
    group = lax.div(count - 1, 16)
    rows16 = att_scr[pl.ds(pl.multiple_of(group * 16, 16), 16), :].astype(jnp.float32)
    at16 = lax.broadcasted_iota(jnp.int32, rows16.shape, 0) == count - 1 - group * 16
    row = jnp.sum(jnp.where(at16, rows16, 0.0), axis=0, keepdims=True)
    last_ref[...] = jnp.broadcast_to(row, last_ref.shape).astype(jnp.bfloat16)


NT = (((1,), (1,)), ((), ()))


def last_row_kernel(layout, block_rows, scalars, *refs):
    pieces = len(layout)
    weights = refs[:pieces]
    last_ref, in_ref, out_ref, w_scr, sems = refs[pieces:]
    columns = w_scr.shape[1]
    weights = [ref.at[:, 0:columns] for ref in weights]
    copies = weight_copies(weights, layout, w_scr, sems, scalars[1], block_rows)
    for copy in copies:
        copy.start()
    rows = in_ref.shape[0]
    local = scalars[3] - 1 - scalars[0] * rows
    group = jnp.clip(lax.div(local, 16), 0, rows // 16 - 1)
    rows16 = in_ref[pl.ds(pl.multiple_of(group * 16, 16), 16), :].astype(jnp.float32)
    at16 = lax.broadcasted_iota(jnp.int32, rows16.shape, 0) == local - group * 16
    residual = jnp.sum(jnp.where(at16, rows16, 0.0), axis=0, keepdims=True)
    for copy in copies:
        copy.wait()
    width = last_ref.shape[1]
    here = lax.broadcasted_iota(jnp.int32, (out_ref.shape[0], 256), 0) == scalars[1]
    for tile in range(0, out_ref.shape[1], 256):
        share = lax.dot_general(
            last_ref[...],
            w_scr[tile : tile + 256, 0:width],
            NT,
            preferred_element_type=jnp.float32,
        )
        row = share[0:1] + residual[:, tile : tile + 256]
        out_ref[:, tile : tile + 256] = jnp.where(here, row, 0.0)


def final_rows_kernel(*refs):
    shares, (gain_ref, table_ref) = refs[:-2], refs[-2:]
    rows = add_all(*[ref[...] for ref in shares]).astype(jnp.bfloat16).astype(jnp.float32)
    table_ref[...] = rms_scale(rows, gain_ref[...][None]).astype(jnp.bfloat16)


def merge_kernel(*refs):
    stats, out_ref = refs[:-1], refs[-1]
    out_ref[...] = merge_stats(*[ref[...] for ref in stats])


def logprobs_kernel(logits_ref, *refs):
    stats, out_ref = refs[:-1], refs[-1]
    merged = merge_stats(*[ref[...] for ref in stats])
    out_ref[...] = logits_ref[...] - merged[:, :1] - jnp.log(merged[:, 1:])


def project_kernel(layout, block_rows, scalars, *refs):
    pieces = len(layout)
    keep_ref, got_ref, in_ref, own_ref, mate_ref, w_scr, sems = refs[pieces:]
    copies = weight_copies(refs[:pieces], layout, w_scr, sems, scalars[1], block_rows)
    for copy in copies:
        copy.start()
    attended = jnp.concatenate([keep_ref[...], got_ref[...]], axis=1)
    for copy in copies:
        copy.wait()
    chunk = own_ref.shape[0]
    for tile in range(0, own_ref.shape[1], 256):
        to = tile + 256
        total = lax.dot_general(
            attended, w_scr[tile:to, :], NT, preferred_element_type=jnp.float32
        )
        own_ref[:, tile:to] = total[:chunk] + in_ref[:, tile:to].astype(jnp.float32)
        mate_ref[:, tile:to] = total[chunk:].astype(jnp.bfloat16)


def head_kernel(streams, *refs):
    tables, refs = refs[: -streams - 2], refs[-streams - 2 :]
    weights, (logits_ref, stats_ref) = refs[:-2], refs[-2:]
    table = add_all(*[ref[...] for ref in tables])
    step = pl.program_id(0)
    wide = weights[0].shape[1]
    for index, ref in enumerate(weights):
        start = pl.multiple_of((step * len(weights) + index) * wide, 128)
        logits_ref[:, pl.ds(start, wide)] = jnp.dot(
            table, ref[...], preferred_element_type=jnp.float32
        )

    @pl.when(step == pl.num_programs(0) - 1)
    def _():
        logits = logits_ref[...]
        top = jnp.max(logits, axis=1, keepdims=True)
        stats_ref[:, 0:1] = top
        stats_ref[:, 1:2] = jnp.sum(jnp.exp(logits - top), axis=1, keepdims=True)


def exchange_all(value, axis, size, bit, combine=None):
    values = [value]
    while bit < size:
        count = min(4, size // bit)
        if len(values) > 1:
            value = combine(*values)
        values = [value] + [
            lax.ppermute(value, axis, xor_pairs(size, bit * index)) for index in range(1, count)
        ]
        bit *= count
    return values


def add_all(*tables):
    return functools.reduce(jnp.add, tables)


def merge_stats(*stats):
    top = functools.reduce(jnp.maximum, [one[:, :1] for one in stats])
    total = add_all(*[one[:, 1:] * jnp.exp(one[:, :1] - top) for one in stats])
    return jnp.concatenate([top, total], axis=1)


def merge(*stats):
    return pl.pallas_call(
        merge_kernel,
        out_shape=jax.ShapeDtypeStruct(stats[0].shape, jnp.float32),
        compiler_params=params(4),
        cost_estimate=FREE,
        name="merge",
    )(*stats)


def on_device(
    n_req,
    n_row,
    hidden_in,
    cache_len,
    new_count,
    key_cache,
    value_cache,
    attn_gain,
    w_query,
    w_key,
    w_value,
    w_out,
    final_gain,
    head_weight,
):
    me_row = lax.axis_index("row")
    me_req = lax.axis_index("req")
    inputs = hidden_in[0]
    rows, model = inputs.shape
    span = rows * n_row
    block_rows, width = w_query.shape
    length, count = cache_len[0], new_count[0]
    scalars = jnp.stack([me_row, me_req, length, count]).astype(jnp.int32)

    normed = rms_scale(inputs.astype(jnp.float32), attn_gain).astype(jnp.bfloat16)
    last = width - HEAD_DIM
    joined = jnp.concatenate([w_query, w_key[:, last:], w_key[:, :last], w_value], axis=1)

    def cache_for(owner):
        return jnp.concatenate(
            [
                lax.dynamic_slice_in_dim(key_cache[0], owner * width, width, 1),
                lax.dynamic_slice_in_dim(value_cache[0], owner * width, width, 1),
            ],
            axis=0,
        )

    cached_rows = key_cache.shape[1]

    joined = after(joined, normed)
    out_own = w_out.T
    weights = Rows(joined, n_req)
    got = weights.neighbours()
    cosine, sine = rotary_tables(length + jnp.arange(span, dtype=jnp.int32))
    out_next = lax.ppermute(out_own, "row", xor_pairs(n_row, 1))
    out_both = jnp.concatenate([out_own, out_next], axis=1)
    cached = [cache_for(jnp.bitwise_xor(me_row, mask)) for mask in range(n_row)]
    x_ups, x_downs, scalars, cosine, sine, out_both, own_block, *cached = gather_line(
        normed, n_row, scalars, cosine, sine, out_both, *cached
    )
    got, own = together(got, [joined])
    diagonal = weights.diagonal(got)
    others = weights.cores([*own, *got, *diagonal])
    pieces = weights.pieces(got, diagonal, others)
    layout = tuple(piece[1:] for piece in pieces)

    across = lax.ppermute(cached[1], "row", xor_pairs(n_row, 2))
    beside, behind = after_all([cached[0], cached[2]], across, x_ups[-1], x_downs[-1])
    old_blocks = [
        lax.ppermute(beside, "row", xor_pairs(n_row, 1)),
        across,
        lax.ppermute(behind, "row", xor_pairs(n_row, 3)),
    ]
    out_rows = Rows(after(out_both, *diagonal), n_req)
    out_got = out_rows.neighbours()
    out_got, out_block = together(out_got, [out_rows.block])
    out_diagonal = out_rows.diagonal(out_got)
    qkv = pl.pallas_call(
        functools.partial(qkv_kernel, n_row, layout, block_rows),
        out_shape=jax.ShapeDtypeStruct((span, 3 * width), jnp.bfloat16),
        in_specs=[SMEM] + [HBM] * (2 * n_row - 1 + len(pieces)) + [VMEM] * 2,
        out_specs=VMEM,
        scratch_shapes=[
            pltpu.VMEM((span, model), jnp.bfloat16),
            pltpu.VMEM((model, 3 * width), jnp.bfloat16),
            pltpu.SemaphoreType.DMA((n_row,)),
            pltpu.SemaphoreType.DMA((len(pieces),)),
        ],
        compiler_params=params(17),
        cost_estimate=pl.CostEstimate(
            flops=6 * span * model * width, bytes_accessed=14 * 2**20, transcendentals=0
        ),
        name="qkv",
    )(scalars, normed, *x_ups, *x_downs, *[piece[0] for piece in pieces], cosine, sine)

    out_here, old_blocks, _ = together([*out_block, *out_got, *out_diagonal], old_blocks, [qkv])
    out_others = out_rows.cores(out_here)
    out_pieces = out_rows.pieces(out_got, out_diagonal, out_others)

    chunk = span // n_row
    keep, send, last_attended = pl.pallas_call(
        functools.partial(attention_kernel, n_row),
        out_shape=(
            jax.ShapeDtypeStruct((2 * chunk, width), jnp.bfloat16),
            jax.ShapeDtypeStruct((2 * chunk, width), jnp.bfloat16),
            jax.ShapeDtypeStruct((16, width), jnp.bfloat16),
        ),
        in_specs=[SMEM] + [HBM] * (1 + len(old_blocks)) + [VMEM],
        out_specs=(VMEM, VMEM, VMEM),
        scratch_shapes=[
            pltpu.VMEM((cached_rows * n_row, width), jnp.bfloat16),
            pltpu.VMEM((cached_rows * n_row, width), jnp.bfloat16),
            pltpu.VMEM((span, width), jnp.bfloat16),
            pltpu.SemaphoreType.DMA((2, n_row)),
        ],
        compiler_params=params(18),
        cost_estimate=pl.CostEstimate(
            flops=6 * span * span * width, bytes_accessed=4 * 2**20, transcendentals=0
        ),
        name="attention",
    )(scalars, own_block, *old_blocks, qkv)

    out_layout = tuple(piece[1:] for piece in out_pieces)
    out_weights = [piece[0] for piece in out_pieces]
    own_columns = -(-width // 128) * 128
    share = pl.pallas_call(
        functools.partial(last_row_kernel, out_layout, block_rows),
        out_shape=jax.ShapeDtypeStruct((n_req, model), jnp.float32),
        in_specs=[SMEM] + [HBM] * len(out_weights) + [VMEM] * 2,
        out_specs=VMEM,
        scratch_shapes=[
            pltpu.VMEM((model, own_columns), jnp.bfloat16),
            pltpu.SemaphoreType.DMA((len(out_weights),)),
        ],
        compiler_params=params(7),
        cost_estimate=FREE,
        name="last_row",
    )(scalars, *out_weights, last_attended, inputs)

    pair = lax.ppermute(share, "req", xor_pairs(n_req, 1))
    share = share + pair
    shares = [share] + [
        lax.ppermute(share, "row", xor_pairs(n_row, mask)) for mask in range(1, n_row)
    ]

    got = after(lax.ppermute(send, "row", xor_pairs(n_row, 1)), share)
    own_sum, mate_part = pl.pallas_call(
        functools.partial(project_kernel, out_layout, block_rows),
        out_shape=(
            jax.ShapeDtypeStruct((chunk, model), jnp.float32),
            jax.ShapeDtypeStruct((chunk, model), jnp.bfloat16),
        ),
        in_specs=[SMEM] + [HBM] * len(out_weights) + [VMEM] * 3,
        out_specs=(VMEM, VMEM),
        scratch_shapes=[
            pltpu.VMEM((model, 2 * width), jnp.bfloat16),
            pltpu.SemaphoreType.DMA((len(out_weights),)),
        ],
        compiler_params=params(11),
        cost_estimate=pl.CostEstimate(
            flops=2 * span * model * width, bytes_accessed=8 * 2**20, transcendentals=0
        ),
        name="project",
    )(scalars, *out_weights, keep, got, inputs)
    mate_part, *shares = lax.optimization_barrier((mate_part, *shares))
    others = lax.ppermute(mate_part, "row", xor_pairs(n_row, 2))
    layer_rows = (own_sum + others.astype(jnp.float32)).astype(jnp.bfloat16)

    table = pl.pallas_call(
        final_rows_kernel,
        out_shape=jax.ShapeDtypeStruct((n_req, model), jnp.bfloat16),
        compiler_params=params(4),
        cost_estimate=FREE,
        name="final_rows",
    )(*shares, final_gain)
    tables = exchange_all(table, "req", n_req, 2, add_all)
    vocab = head_weight.shape[1]
    wide, streams = 256, 5

    def columns(index):
        return pl.BlockSpec((model, wide), lambda step: (0, step * streams + index))

    logits, stats = pl.pallas_call(
        functools.partial(head_kernel, streams),
        grid=(vocab // (wide * streams),),
        out_shape=(
            jax.ShapeDtypeStruct((n_req, vocab), jnp.float32),
            jax.ShapeDtypeStruct((n_req, 2), jnp.float32),
        ),
        in_specs=[
            *[pl.BlockSpec((n_req, model), lambda step: (0, 0))] * len(tables),
            *[columns(index) for index in range(streams)],
        ],
        out_specs=(
            pl.BlockSpec((n_req, vocab), lambda step: (0, 0)),
            pl.BlockSpec((n_req, 2), lambda step: (0, 0)),
        ),
        compiler_params=params(48),
        cost_estimate=FREE,
        name="head",
    )(*tables, *[head_weight] * streams)
    stats = merge(*exchange_all(stats, "req", n_req, 2, merge))
    stats = merge(stats, lax.ppermute(stats, "req", xor_pairs(n_req, 1)))
    stats = exchange_all(after(stats, others), "row", n_row, 1, merge)
    logprobs = pl.pallas_call(
        logprobs_kernel,
        out_shape=jax.ShapeDtypeStruct(logits.shape, jnp.float32),
        compiler_params=params(4),
        cost_estimate=FREE,
        name="logprobs",
    )(logits, *stats)
    return (layer_rows[None], logprobs)


def solution(mesh):
    placed = (
        P("req", "row", None),
        P("req"),
        P("req"),
        P("req", "row", None),
        P("req", "row", None),
        P(),
        P("req", "row"),
        P("req", "row"),
        P("req", "row"),
        P("row", "req"),
        P(),
        P(None, ("req", "row")),
    )
    return jax.shard_map(
        functools.partial(on_device, mesh.shape["req"], mesh.shape["row"]),
        mesh=mesh,
        in_specs=placed,
        out_specs=(P("req", "row", None), P(None, ("req", "row"))),
        check_vma=False,
    )
```

```python
import functools

import jax
import jax.numpy as jnp
from jax import lax
from jax.experimental import pallas as pl
from jax.experimental.pallas import tpu as pltpu
from jax.sharding import PartitionSpec as P

HEAD_DIM = 64
EPSILON = 1e-05
HBM = pl.BlockSpec(memory_space=pltpu.HBM)
SMEM = pl.BlockSpec(memory_space=pltpu.SMEM)
VMEM = pl.BlockSpec(memory_space=pltpu.VMEM)


def params(mib):
    return pltpu.CompilerParams(vmem_limit_bytes=mib * 1024 * 1024)


FREE = pl.CostEstimate(flops=0, bytes_accessed=0, transcendentals=0)


def rms_scale(values, gain_vec):
    return (
        values * lax.rsqrt(jnp.mean(values * values, axis=-1, keepdims=True) + EPSILON) * gain_vec
    )


def rotary_tables(places):
    half_dim = HEAD_DIM // 2
    frequency = 10000.0 ** (-jnp.arange(half_dim).astype(jnp.float32) / half_dim)
    angles = places.astype(jnp.float32)[:, None] * frequency[None, :]
    cosine, sine = jnp.cos(angles), jnp.sin(angles)
    return (
        jnp.concatenate([cosine] * 4, axis=1),
        jnp.concatenate([-sine, sine, -sine, sine], axis=1),
    )


def up_pairs(size, hop, first=0):
    return [(i, i + hop) for i in range(first, size - hop)]


def down_pairs(size, hop, last=None):
    last = size - 1 if last is None else last
    return [(i, i - hop) for i in range(hop, last + 1)]


def xor_pairs(size, bit):
    return [(i, i ^ bit) for i in range(size)]


def after(value, *earlier):
    return lax.optimization_barrier((value, *earlier))[0]


class Rows:
    def __init__(self, block, size):
        self.block, self.size, self.rows = block, size, block.shape[0]
        self.half = self.rows // 2

    def send(self, array, mask):
        return lax.ppermute(array, "req", xor_pairs(self.size, mask))

    def neighbours(self):
        if self.size != 8:
            return [lax.all_gather(self.block, "req", axis=0, tiled=True)]
        return [self.send(self.block, 2), self.send(self.block, 4)]

    def diagonal(self, got):
        if self.size != 8:
            return []
        half_x, half_y = lax.optimization_barrier((got[0][self.half :], got[1][: self.half]))
        return [self.send(half_y, 2), self.send(half_x, 4)]

    def cores(self, arrays):
        return [self.send(array, 1) for array in arrays] if self.size == 8 else []

    def pieces(self, got, diagonal, others):
        if self.size != 8:
            return [(got[0], None, 0, self.rows * self.size)]
        places = [
            (0, 0, self.rows),
            (2, 0, self.rows),
            (4, 0, self.rows),
            (6, 0, self.half),
            (6, self.half, self.half),
        ]
        pieces = []
        for here, there, (mask, at, count) in zip(
            [self.block, *got, *diagonal], others, places, strict=True
        ):
            pieces += [(here, mask, at, count), (there, mask ^ 1, at, count)]
        return pieces


def after_all(values, *earlier):
    return list(lax.optimization_barrier((*values, *earlier)))[: len(values)]


def gather_line(block, size, *ready):
    ups, downs = [], []
    up, down = block, block
    for step in range(1, size):
        up = lax.ppermute(up, "row", up_pairs(size, 1, step - 1))
        down = lax.ppermute(down, "row", down_pairs(size, 1, size - step))
        if step == size - 2:
            up, down, *ready = lax.optimization_barrier((up, down, *ready))
        else:
            up, down = lax.optimization_barrier((up, down))
        ups.append(up)
        downs.append(down)
    return ups, downs, *ready


def together(*groups):
    flat = lax.optimization_barrier(tuple(array for group in groups for array in group))
    result, at = [], 0
    for group in groups:
        result.append(list(flat[at : at + len(group)]))
        at += len(group)
    return result


def weight_copies(refs, layout, target, sems, me_req, block_rows):
    copies = []
    for index, (ref, (mask, first, count)) in enumerate(zip(refs, layout)):
        if mask is None:
            start = 0
        else:
            start = pl.multiple_of(jnp.bitwise_xor(me_req, mask) * block_rows + first, 16)
        copies.append(pltpu.make_async_copy(ref, target.at[pl.ds(start, count), :], sems.at[index]))
    return copies


def start_line_copies(own, ups, downs, target, sems, me_row, rows):
    size = len(ups) + 1
    waits = []
    own_copy = pltpu.make_async_copy(own, target.at[pl.ds(me_row * rows, rows), :], sems.at[0])
    own_copy.start()
    waits.append(own_copy)
    for hop in range(1, size):
        index = lax.rem(me_row - hop + size, size)
        place = target.at[pl.ds(pl.multiple_of(index * rows, rows), rows), :]
        below = pltpu.make_async_copy(ups[hop - 1], place, sems.at[hop])
        above = pltpu.make_async_copy(downs[size - hop - 1], place, sems.at[hop])

        @pl.when(me_row >= hop)
        def _(below=below):
            below.start()

        @pl.when(me_row < hop)
        def _(above=above):
            above.start()

        waits.append(below)
    return waits


def norm_kernel(in_ref, gain_ref, out_ref):
    rows = rms_scale(in_ref[...].astype(jnp.float32), gain_ref[...][None])
    out_ref[...] = rows.astype(jnp.bfloat16)


def qkv_kernel(size, layout, block_rows, scalars, *refs):
    pieces = len(layout)
    own, ups, downs = refs[0], refs[1:size], refs[size : 2 * size - 1]
    weights = refs[2 * size - 1 : 2 * size - 1 + pieces]
    cos_ref, sin_ref, out_ref, x_scr, w_scr, x_sems, w_sems = refs[2 * size - 1 + pieces :]
    rows = own.shape[0]
    total = out_ref.shape[1]
    copies = weight_copies(weights, layout, w_scr, w_sems, scalars[1], block_rows)
    for copy in copies:
        copy.start()
    waits = start_line_copies(own, ups, downs, x_scr, x_sems, scalars[0], rows)
    for copy in waits + copies:
        copy.wait()
    span = x_scr.shape[0]
    width = total // 3
    half = HEAD_DIM // 2
    lane = lax.broadcasted_iota(jnp.int32, (span, 128), 1)
    first_half = lax.rem(lane, HEAD_DIM) < half
    cosine, sine = cos_ref[...], sin_ref[...]
    for tile in range(0, total, 256):
        end = min(tile + 256, total)
        raw = jnp.dot(x_scr[...], w_scr[:, tile:end], preferred_element_type=jnp.float32)
        for at in range(tile, end, 128):
            stop = min(at + 128, end)
            part = raw[:, at - tile : stop - tile]
            if at < 2 * width:
                swapped = jnp.where(
                    first_half, pltpu.roll(part, 128 - half, 1), pltpu.roll(part, half, 1)
                )
                part = part * cosine + swapped * sine
                if stop <= width:
                    part = part * (HEAD_DIM**-0.5)
                elif at < width:
                    part = jnp.where(lane < width - at, part * (HEAD_DIM**-0.5), part)
            out_ref[:, at:stop] = part.astype(jnp.bfloat16)


def attend_block(q, k_new, v_new, k_old, v_old, limit_new, length):
    nt = (((1,), (1,)), ((), ()))
    s_new = lax.dot_general(q, k_new, nt, preferred_element_type=jnp.float32)
    s_old = lax.dot_general(q, k_old, nt, preferred_element_type=jnp.float32)
    pos_new = lax.broadcasted_iota(jnp.int32, s_new.shape, 1)
    pos_old = lax.broadcasted_iota(jnp.int32, s_old.shape, 1)
    s_new = jnp.where(pos_new < limit_new, s_new, -jnp.inf)
    s_old = jnp.where(pos_old < length, s_old, -jnp.inf)
    top = jnp.maximum(
        jnp.max(s_new, axis=1, keepdims=True), jnp.max(s_old, axis=1, keepdims=True)
    )
    e_new = jnp.exp(s_new - top)
    e_old = jnp.exp(s_old - top)
    total = jnp.sum(e_new, axis=1, keepdims=True) + jnp.sum(e_old, axis=1, keepdims=True)
    summed = jnp.dot(e_new.astype(jnp.bfloat16), v_new, preferred_element_type=jnp.float32)
    summed += jnp.dot(e_old.astype(jnp.bfloat16), v_old, preferred_element_type=jnp.float32)
    return summed / total


def attention_kernel(size, scalars, *refs):
    blocks = refs[:size]
    qkv_ref, keep_ref, send_ref, last_ref, k_old, v_old, att_scr, sems = refs[size:]
    rows = blocks[0].shape[0] // 2
    me_row, length, count = scalars[0], scalars[2], scalars[3]
    waits = []
    for mask in range(size):
        index = jnp.bitwise_xor(me_row, mask)
        for part, target in enumerate((k_old, v_old)):
            copy = pltpu.make_async_copy(
                blocks[mask].at[pl.ds(part * rows, rows), :],
                target.at[pl.ds(pl.multiple_of(index * rows, rows), rows), :],
                sems.at[part, mask],
            )
            copy.start()
            waits.append(copy)
    for copy in waits:
        copy.wait()
    span, total = qkv_ref.shape
    width = total // 3
    last = width - HEAD_DIM
    block = min(256, span)

    def attend(live):
        lane = lax.broadcasted_iota(jnp.int32, (block, 128), 1)
        left = lane < HEAD_DIM

        def heads(q_at, k_at, v_at, lo, wide):
            old_k, old_v = k_old[0:live, pl.ds(lo, wide)], v_old[0:live, pl.ds(lo, wide)]
            for begin in range(0, span, block):
                stop = begin + block
                q = qkv_ref[begin:stop, pl.ds(q_at, wide)]
                k_new = qkv_ref[0:stop, pl.ds(k_at, wide)]
                v_new = qkv_ref[0:stop, pl.ds(v_at, wide)]
                row = begin + lax.broadcasted_iota(jnp.int32, (block, 1), 0)
                limit = jnp.minimum(row + 1, count)
                if wide == 128:
                    zero = jnp.zeros_like(q)
                    stacked = jnp.concatenate(
                        [jnp.where(left, q, zero), jnp.where(left, zero, q)], axis=0
                    )
                    limits = jnp.concatenate([limit, limit], axis=0)
                    got = attend_block(stacked, k_new, v_new, old_k, old_v, limits, length)
                    both = jnp.where(left, got[:block], got[block:])
                else:
                    both = attend_block(q, k_new, v_new, old_k, old_v, limit, length)
                att_scr[begin:stop, pl.ds(lo, wide)] = both.astype(jnp.bfloat16)

        for lo in range(0, last, 128):
            heads(lo, lo + width + HEAD_DIM, lo + 2 * width, lo, 128)

        heads(last, width, 2 * width + last, last, HEAD_DIM)

    @pl.when(length <= rows)
    def _():
        attend(rows)

    @pl.when(length > rows)
    def _():
        attend(size * rows)

    chunk = span // size
    for slot, ref in ((0, keep_ref), (1, send_ref), (2, keep_ref), (3, send_ref)):
        start = pl.multiple_of(jnp.bitwise_xor(me_row, slot) * chunk, chunk)
        at = slot // 2 * chunk
        ref[at : at + chunk, :] = att_scr[pl.ds(start, chunk), :]
    group = lax.div(count - 1, 16)
    rows16 = att_scr[pl.ds(pl.multiple_of(group * 16, 16), 16), :].astype(jnp.float32)
    at16 = lax.broadcasted_iota(jnp.int32, rows16.shape, 0) == count - 1 - group * 16
    row = jnp.sum(jnp.where(at16, rows16, 0.0), axis=0, keepdims=True)
    last_ref[...] = jnp.broadcast_to(row, last_ref.shape).astype(jnp.bfloat16)


NT = (((1,), (1,)), ((), ()))


def last_row_kernel(layout, block_rows, scalars, *refs):
    pieces = len(layout)
    weights = refs[:pieces]
    last_ref, in_ref, out_ref, w_scr, sems = refs[pieces:]
    columns = w_scr.shape[1]
    weights = [ref.at[:, 0:columns] for ref in weights]
    copies = weight_copies(weights, layout, w_scr, sems, scalars[1], block_rows)
    for copy in copies:
        copy.start()
    rows = in_ref.shape[0]
    local = scalars[3] - 1 - scalars[0] * rows
    group = jnp.clip(lax.div(local, 16), 0, rows // 16 - 1)
    rows16 = in_ref[pl.ds(pl.multiple_of(group * 16, 16), 16), :].astype(jnp.float32)
    at16 = lax.broadcasted_iota(jnp.int32, rows16.shape, 0) == local - group * 16
    residual = jnp.sum(jnp.where(at16, rows16, 0.0), axis=0, keepdims=True)
    for copy in copies:
        copy.wait()
    width = last_ref.shape[1]
    here = lax.broadcasted_iota(jnp.int32, (out_ref.shape[0], 256), 0) == lax.rem(scalars[1], 2)
    for tile in range(0, out_ref.shape[1], 256):
        share = lax.dot_general(
            last_ref[...],
            w_scr[tile : tile + 256, 0:width],
            NT,
            preferred_element_type=jnp.float32,
        )
        row = share[0:1] + residual[:, tile : tile + 256]
        out_ref[:, tile : tile + 256] = jnp.where(here, row, 0.0)


def final_rows_kernel(scalars, *refs):
    shares, (gain_ref, table_ref) = refs[:-2], refs[-2:]
    rows = add_all(*[ref[...] for ref in shares]).astype(jnp.bfloat16).astype(jnp.float32)
    rows = rms_scale(rows, gain_ref[...][None]).astype(jnp.bfloat16).astype(jnp.float32)
    at = lax.broadcasted_iota(jnp.int32, table_ref.shape, 0) - lax.div(scalars[1], 2) * 2
    table = jnp.where(at == 0, rows[0:1], jnp.where(at == 1, rows[1:2], 0.0))
    table_ref[...] = table.astype(jnp.bfloat16)


def merge_kernel(*refs):
    stats, out_ref = refs[:-1], refs[-1]
    out_ref[...] = merge_stats(*[ref[...] for ref in stats])


def logprobs_kernel(logits_ref, *refs):
    stats, out_ref = refs[:-1], refs[-1]
    merged = merge_stats(*[ref[...] for ref in stats])
    out_ref[...] = logits_ref[...] - merged[:, :1] - jnp.log(merged[:, 1:])


def project_kernel(layout, block_rows, scalars, *refs):
    pieces = len(layout)
    keep_ref, got_ref, in_ref, own_ref, mate_ref, w_scr, sems = refs[pieces:]
    copies = weight_copies(refs[:pieces], layout, w_scr, sems, scalars[1], block_rows)
    for copy in copies:
        copy.start()
    attended = jnp.concatenate([keep_ref[...], got_ref[...]], axis=1)
    for copy in copies:
        copy.wait()
    chunk = own_ref.shape[0]
    for tile in range(0, own_ref.shape[1], 256):
        to = tile + 256
        total = lax.dot_general(
            attended, w_scr[tile:to, :], NT, preferred_element_type=jnp.float32
        )
        own_ref[:, tile:to] = total[:chunk] + in_ref[:, tile:to].astype(jnp.float32)
        mate_ref[:, tile:to] = total[chunk:].astype(jnp.bfloat16)


def head_kernel(streams, *refs):
    tables, refs = refs[: -streams - 2], refs[-streams - 2 :]
    weights, (logits_ref, stats_ref) = refs[:-2], refs[-2:]
    table = add_all(*[ref[...] for ref in tables])
    step = pl.program_id(0)
    wide = weights[0].shape[1]
    for index, ref in enumerate(weights):
        start = pl.multiple_of((step * len(weights) + index) * wide, 128)
        logits_ref[:, pl.ds(start, wide)] = jnp.dot(
            table, ref[...], preferred_element_type=jnp.float32
        )

    @pl.when(step == pl.num_programs(0) - 1)
    def _():
        logits = logits_ref[...]
        top = jnp.max(logits, axis=1, keepdims=True)
        stats_ref[:, 0:1] = top
        stats_ref[:, 1:2] = jnp.sum(jnp.exp(logits - top), axis=1, keepdims=True)


def exchange_all(value, axis, size, bit, combine=None):
    values = [value]
    while bit < size:
        count = min(4, size // bit)
        if len(values) > 1:
            value = combine(*values)
        values = [value] + [
            lax.ppermute(value, axis, xor_pairs(size, bit * index)) for index in range(1, count)
        ]
        bit *= count
    return values


def add_all(*tables):
    return functools.reduce(jnp.add, tables)


def merge_stats(*stats):
    top = functools.reduce(jnp.maximum, [one[:, :1] for one in stats])
    total = add_all(*[one[:, 1:] * jnp.exp(one[:, :1] - top) for one in stats])
    return jnp.concatenate([top, total], axis=1)


def merge(*stats):
    return pl.pallas_call(
        merge_kernel,
        out_shape=jax.ShapeDtypeStruct(stats[0].shape, jnp.float32),
        compiler_params=params(4),
        cost_estimate=FREE,
        name="merge",
    )(*stats)


def on_device(
    n_req,
    n_row,
    hidden_in,
    cache_len,
    new_count,
    key_cache,
    value_cache,
    attn_gain,
    w_query,
    w_key,
    w_value,
    w_out,
    final_gain,
    head_weight,
):
    me_row = lax.axis_index("row")
    me_req = lax.axis_index("req")
    inputs = hidden_in[0]
    rows, model = inputs.shape
    span = rows * n_row
    block_rows, width = w_query.shape
    length, count = cache_len[0], new_count[0]
    scalars = jnp.stack([me_row, me_req, length, count]).astype(jnp.int32)

    normed = pl.pallas_call(
        norm_kernel,
        out_shape=jax.ShapeDtypeStruct(inputs.shape, jnp.bfloat16),
        compiler_params=params(6),
        cost_estimate=FREE,
        name="norm",
    )(inputs, attn_gain)
    last = width - HEAD_DIM
    joined = jnp.concatenate([w_query, w_key[:, last:], w_key[:, :last], w_value], axis=1)

    def cache_for(owner):
        return jnp.concatenate(
            [
                lax.dynamic_slice_in_dim(key_cache[0], owner * width, width, 1),
                lax.dynamic_slice_in_dim(value_cache[0], owner * width, width, 1),
            ],
            axis=0,
        )

    cached_rows = key_cache.shape[1]

    joined = after(joined, normed)
    out_own = w_out.T
    weights = Rows(joined, n_req)
    got = weights.neighbours()
    cosine, sine = rotary_tables(length + jnp.arange(span, dtype=jnp.int32))
    out_next = lax.ppermute(out_own, "row", xor_pairs(n_row, 1))
    out_both = jnp.concatenate([out_own, out_next], axis=1)
    cached = [cache_for(jnp.bitwise_xor(me_row, mask)) for mask in range(n_row)]
    x_ups, x_downs, scalars, cosine, sine, out_both, own_block, *cached = gather_line(
        normed, n_row, scalars, cosine, sine, out_both, *cached
    )
    got, own = together(got, [joined])
    diagonal = weights.diagonal(got)
    others = weights.cores([*own, *got, *diagonal])
    pieces = weights.pieces(got, diagonal, others)
    layout = tuple(piece[1:] for piece in pieces)

    across = lax.ppermute(cached[1], "row", xor_pairs(n_row, 2))
    beside, behind = after_all([cached[0], cached[2]], across, x_ups[-1], x_downs[-1])
    old_blocks = [
        lax.ppermute(beside, "row", xor_pairs(n_row, 1)),
        across,
        lax.ppermute(behind, "row", xor_pairs(n_row, 3)),
    ]
    out_rows = Rows(after(out_both, *diagonal), n_req)
    out_got = out_rows.neighbours()
    out_got, out_block = together(out_got, [out_rows.block])
    out_diagonal = out_rows.diagonal(out_got)
    qkv = pl.pallas_call(
        functools.partial(qkv_kernel, n_row, layout, block_rows),
        out_shape=jax.ShapeDtypeStruct((span, 3 * width), jnp.bfloat16),
        in_specs=[SMEM] + [HBM] * (2 * n_row - 1 + len(pieces)) + [VMEM] * 2,
        out_specs=VMEM,
        scratch_shapes=[
            pltpu.VMEM((span, model), jnp.bfloat16),
            pltpu.VMEM((model, 3 * width), jnp.bfloat16),
            pltpu.SemaphoreType.DMA((n_row,)),
            pltpu.SemaphoreType.DMA((len(pieces),)),
        ],
        compiler_params=params(17),
        cost_estimate=pl.CostEstimate(
            flops=6 * span * model * width, bytes_accessed=14 * 2**20, transcendentals=0
        ),
        name="qkv",
    )(scalars, normed, *x_ups, *x_downs, *[piece[0] for piece in pieces], cosine, sine)

    out_here, old_blocks, _ = together([*out_block, *out_got, *out_diagonal], old_blocks, [qkv])
    out_others = out_rows.cores(out_here)
    out_pieces = out_rows.pieces(out_got, out_diagonal, out_others)

    chunk = span // n_row
    keep, send, last_attended = pl.pallas_call(
        functools.partial(attention_kernel, n_row),
        out_shape=(
            jax.ShapeDtypeStruct((2 * chunk, width), jnp.bfloat16),
            jax.ShapeDtypeStruct((2 * chunk, width), jnp.bfloat16),
            jax.ShapeDtypeStruct((16, width), jnp.bfloat16),
        ),
        in_specs=[SMEM] + [HBM] * (1 + len(old_blocks)) + [VMEM],
        out_specs=(VMEM, VMEM, VMEM),
        scratch_shapes=[
            pltpu.VMEM((cached_rows * n_row, width), jnp.bfloat16),
            pltpu.VMEM((cached_rows * n_row, width), jnp.bfloat16),
            pltpu.VMEM((span, width), jnp.bfloat16),
            pltpu.SemaphoreType.DMA((2, n_row)),
        ],
        compiler_params=params(18),
        cost_estimate=pl.CostEstimate(
            flops=6 * span * span * width, bytes_accessed=4 * 2**20, transcendentals=0
        ),
        name="attention",
    )(scalars, own_block, *old_blocks, qkv)

    out_layout = tuple(piece[1:] for piece in out_pieces)
    out_weights = [piece[0] for piece in out_pieces]
    own_columns = -(-width // 128) * 128
    share = pl.pallas_call(
        functools.partial(last_row_kernel, out_layout, block_rows),
        out_shape=jax.ShapeDtypeStruct((2, model), jnp.float32),
        in_specs=[SMEM] + [HBM] * len(out_weights) + [VMEM] * 2,
        out_specs=VMEM,
        scratch_shapes=[
            pltpu.VMEM((model, own_columns), jnp.bfloat16),
            pltpu.SemaphoreType.DMA((len(out_weights),)),
        ],
        compiler_params=params(7),
        cost_estimate=FREE,
        name="last_row",
    )(scalars, *out_weights, last_attended, inputs)

    pair = lax.ppermute(share, "req", xor_pairs(n_req, 1))
    share = share + pair
    shares = [share] + [
        lax.ppermute(share, "row", xor_pairs(n_row, mask)) for mask in range(1, n_row)
    ]

    got = after(lax.ppermute(send, "row", xor_pairs(n_row, 1)), share)
    own_sum, mate_part = pl.pallas_call(
        functools.partial(project_kernel, out_layout, block_rows),
        out_shape=(
            jax.ShapeDtypeStruct((chunk, model), jnp.float32),
            jax.ShapeDtypeStruct((chunk, model), jnp.bfloat16),
        ),
        in_specs=[SMEM] + [HBM] * len(out_weights) + [VMEM] * 3,
        out_specs=(VMEM, VMEM),
        scratch_shapes=[
            pltpu.VMEM((model, 2 * width), jnp.bfloat16),
            pltpu.SemaphoreType.DMA((len(out_weights),)),
        ],
        compiler_params=params(11),
        cost_estimate=pl.CostEstimate(
            flops=2 * span * model * width, bytes_accessed=8 * 2**20, transcendentals=0
        ),
        name="project",
    )(scalars, *out_weights, keep, got, inputs)
    mate_part, *shares = lax.optimization_barrier((mate_part, *shares))
    others = lax.ppermute(mate_part, "row", xor_pairs(n_row, 2))
    layer_rows = (own_sum + others.astype(jnp.float32)).astype(jnp.bfloat16)

    table = pl.pallas_call(
        final_rows_kernel,
        out_shape=jax.ShapeDtypeStruct((n_req, model), jnp.bfloat16),
        in_specs=[SMEM] + [VMEM] * (n_row + 1),
        out_specs=VMEM,
        compiler_params=params(4),
        cost_estimate=FREE,
        name="final_rows",
    )(scalars, *shares, final_gain)
    tables = exchange_all(table, "req", n_req, 2, add_all)
    vocab = head_weight.shape[1]
    wide, streams = 256, 5

    def columns(index):
        return pl.BlockSpec((model, wide), lambda step: (0, step * streams + index))

    logits, stats = pl.pallas_call(
        functools.partial(head_kernel, streams),
        grid=(vocab // (wide * streams),),
        out_shape=(
            jax.ShapeDtypeStruct((n_req, vocab), jnp.float32),
            jax.ShapeDtypeStruct((n_req, 2), jnp.float32),
        ),
        in_specs=[
            *[pl.BlockSpec((n_req, model), lambda step: (0, 0))] * len(tables),
            *[columns(index) for index in range(streams)],
        ],
        out_specs=(
            pl.BlockSpec((n_req, vocab), lambda step: (0, 0)),
            pl.BlockSpec((n_req, 2), lambda step: (0, 0)),
        ),
        compiler_params=params(48),
        cost_estimate=FREE,
        name="head",
    )(*tables, *[head_weight] * streams)
    stats = merge(*exchange_all(stats, "req", n_req, 2, merge))
    stats = merge(stats, lax.ppermute(stats, "req", xor_pairs(n_req, 1)))
    stats = exchange_all(after(stats, others), "row", n_row, 1, merge)
    logprobs = pl.pallas_call(
        logprobs_kernel,
        out_shape=jax.ShapeDtypeStruct(logits.shape, jnp.float32),
        compiler_params=params(4),
        cost_estimate=FREE,
        name="logprobs",
    )(logits, *stats)
    return (layer_rows[None], logprobs)


def solution(mesh):
    placed = (
        P("req", "row", None),
        P("req"),
        P("req"),
        P("req", "row", None),
        P("req", "row", None),
        P(),
        P("req", "row"),
        P("req", "row"),
        P("req", "row"),
        P("row", "req"),
        P(),
        P(None, ("req", "row")),
    )
    return jax.shard_map(
        functools.partial(on_device, mesh.shape["req"], mesh.shape["row"]),
        mesh=mesh,
        in_specs=placed,
        out_specs=(P("req", "row", None), P(None, ("req", "row"))),
        check_vma=False,
    )
```

```python
import functools

import jax
import jax.numpy as jnp
from jax import lax
from jax.experimental import pallas as pl
from jax.experimental.pallas import tpu as pltpu
from jax.sharding import PartitionSpec as P

HEAD_DIM = 64
EPSILON = 1e-05
HBM = pl.BlockSpec(memory_space=pltpu.HBM)
SMEM = pl.BlockSpec(memory_space=pltpu.SMEM)
VMEM = pl.BlockSpec(memory_space=pltpu.VMEM)


def params(mib):
    return pltpu.CompilerParams(vmem_limit_bytes=mib * 1024 * 1024)


FREE = pl.CostEstimate(flops=0, bytes_accessed=0, transcendentals=0)


def rms_scale(values, gain_vec):
    return (
        values * lax.rsqrt(jnp.mean(values * values, axis=-1, keepdims=True) + EPSILON) * gain_vec
    )


def rotary_tables(places):
    half_dim = HEAD_DIM // 2
    frequency = 10000.0 ** (-jnp.arange(half_dim).astype(jnp.float32) / half_dim)
    angles = places.astype(jnp.float32)[:, None] * frequency[None, :]
    cosine, sine = jnp.cos(angles), jnp.sin(angles)
    return (
        jnp.concatenate([cosine] * 4, axis=1),
        jnp.concatenate([-sine, sine, -sine, sine], axis=1),
    )


def up_pairs(size, hop, first=0):
    return [(i, i + hop) for i in range(first, size - hop)]


def down_pairs(size, hop, last=None):
    last = size - 1 if last is None else last
    return [(i, i - hop) for i in range(hop, last + 1)]


def xor_pairs(size, bit):
    return [(i, i ^ bit) for i in range(size)]


def after(value, *earlier):
    return lax.optimization_barrier((value, *earlier))[0]


class Rows:
    def __init__(self, block, size):
        self.block, self.size, self.rows = block, size, block.shape[0]
        self.half = self.rows // 2

    def send(self, array, mask):
        return lax.ppermute(array, "req", xor_pairs(self.size, mask))

    def neighbours(self):
        if self.size != 8:
            return [lax.all_gather(self.block, "req", axis=0, tiled=True)]
        return [self.send(self.block, 2), self.send(self.block, 4)]

    def diagonal(self, got):
        if self.size != 8:
            return []
        half_x, half_y = lax.optimization_barrier((got[0][self.half :], got[1][: self.half]))
        return [self.send(half_y, 2), self.send(half_x, 4)]

    def cores(self, arrays):
        return [self.send(array, 1) for array in arrays] if self.size == 8 else []

    def pieces(self, got, diagonal, others):
        if self.size != 8:
            return [(got[0], None, 0, self.rows * self.size)]
        places = [
            (0, 0, self.rows),
            (2, 0, self.rows),
            (4, 0, self.rows),
            (6, 0, self.half),
            (6, self.half, self.half),
        ]
        pieces = []
        for here, there, (mask, at, count) in zip(
            [self.block, *got, *diagonal], others, places, strict=True
        ):
            pieces += [(here, mask, at, count), (there, mask ^ 1, at, count)]
        return pieces


def after_all(values, *earlier):
    return list(lax.optimization_barrier((*values, *earlier)))[: len(values)]


def gather_line(block, size, *ready):
    ups, downs = [], []
    up, down = block, block
    for step in range(1, size):
        up = lax.ppermute(up, "row", up_pairs(size, 1, step - 1))
        down = lax.ppermute(down, "row", down_pairs(size, 1, size - step))
        if step == size - 2:
            up, down, *ready = lax.optimization_barrier((up, down, *ready))
        else:
            up, down = lax.optimization_barrier((up, down))
        ups.append(up)
        downs.append(down)
    return ups, downs, *ready


def together(*groups):
    flat = lax.optimization_barrier(tuple(array for group in groups for array in group))
    result, at = [], 0
    for group in groups:
        result.append(list(flat[at : at + len(group)]))
        at += len(group)
    return result


def weight_copies(refs, layout, target, sems, me_req, block_rows):
    copies = []
    for index, (ref, (mask, first, count)) in enumerate(zip(refs, layout)):
        if mask is None:
            start = 0
        else:
            start = pl.multiple_of(jnp.bitwise_xor(me_req, mask) * block_rows + first, 16)
        copies.append(pltpu.make_async_copy(ref, target.at[pl.ds(start, count), :], sems.at[index]))
    return copies


def start_line_copies(own, ups, downs, target, sems, me_row, rows):
    size = len(ups) + 1
    waits = []
    own_copy = pltpu.make_async_copy(own, target.at[pl.ds(me_row * rows, rows), :], sems.at[0])
    own_copy.start()
    waits.append(own_copy)
    for hop in range(1, size):
        index = lax.rem(me_row - hop + size, size)
        place = target.at[pl.ds(pl.multiple_of(index * rows, rows), rows), :]
        below = pltpu.make_async_copy(ups[hop - 1], place, sems.at[hop])
        above = pltpu.make_async_copy(downs[size - hop - 1], place, sems.at[hop])

        @pl.when(me_row >= hop)
        def _(below=below):
            below.start()

        @pl.when(me_row < hop)
        def _(above=above):
            above.start()

        waits.append(below)
    return waits


def norm_kernel(in_ref, gain_ref, out_ref):
    rows = rms_scale(in_ref[...].astype(jnp.float32), gain_ref[...][None])
    out_ref[...] = rows.astype(jnp.bfloat16)


def qkv_kernel(size, layout, block_rows, scalars, *refs):
    pieces = len(layout)
    own, ups, downs = refs[0], refs[1:size], refs[size : 2 * size - 1]
    weights = refs[2 * size - 1 : 2 * size - 1 + pieces]
    cos_ref, sin_ref, out_ref, x_scr, w_scr, x_sems, w_sems = refs[2 * size - 1 + pieces :]
    rows = own.shape[0]
    total = out_ref.shape[1]
    copies = weight_copies(weights, layout, w_scr, w_sems, scalars[1], block_rows)
    for copy in copies:
        copy.start()
    waits = start_line_copies(own, ups, downs, x_scr, x_sems, scalars[0], rows)
    for copy in waits + copies:
        copy.wait()
    span = x_scr.shape[0]
    width = total // 3
    half = HEAD_DIM // 2
    lane = lax.broadcasted_iota(jnp.int32, (span, 128), 1)
    first_half = lax.rem(lane, HEAD_DIM) < half
    cosine, sine = cos_ref[...], sin_ref[...]
    for tile in range(0, total, 256):
        end = min(tile + 256, total)
        raw = jnp.dot(x_scr[...], w_scr[:, tile:end], preferred_element_type=jnp.float32)
        for at in range(tile, end, 128):
            stop = min(at + 128, end)
            part = raw[:, at - tile : stop - tile]
            if at < 2 * width:
                swapped = jnp.where(
                    first_half, pltpu.roll(part, 128 - half, 1), pltpu.roll(part, half, 1)
                )
                part = part * cosine + swapped * sine
                if stop <= width:
                    part = part * (HEAD_DIM**-0.5)
                elif at < width:
                    part = jnp.where(lane < width - at, part * (HEAD_DIM**-0.5), part)
            out_ref[:, at:stop] = part.astype(jnp.bfloat16)


def attend_block(q, k_new, v_new, k_old, v_old, limit_new, length):
    nt = (((1,), (1,)), ((), ()))
    s_new = lax.dot_general(q, k_new, nt, preferred_element_type=jnp.float32)
    s_old = lax.dot_general(q, k_old, nt, preferred_element_type=jnp.float32)
    pos_new = lax.broadcasted_iota(jnp.int32, s_new.shape, 1)
    pos_old = lax.broadcasted_iota(jnp.int32, s_old.shape, 1)
    s_new = jnp.where(pos_new < limit_new, s_new, -jnp.inf)
    s_old = jnp.where(pos_old < length, s_old, -jnp.inf)
    top = jnp.maximum(
        jnp.max(s_new, axis=1, keepdims=True), jnp.max(s_old, axis=1, keepdims=True)
    )
    e_new = jnp.exp(s_new - top)
    e_old = jnp.exp(s_old - top)
    total = jnp.sum(e_new, axis=1, keepdims=True) + jnp.sum(e_old, axis=1, keepdims=True)
    summed = jnp.dot(e_new.astype(jnp.bfloat16), v_new, preferred_element_type=jnp.float32)
    summed += jnp.dot(e_old.astype(jnp.bfloat16), v_old, preferred_element_type=jnp.float32)
    return summed / total


def attention_kernel(size, scalars, *refs):
    blocks = refs[:size]
    qkv_ref, keep_ref, send_ref, last_ref, k_old, v_old, att_scr, sems = refs[size:]
    rows = blocks[0].shape[0] // 2
    me_row, length, count = scalars[0], scalars[2], scalars[3]
    waits = []
    for mask in range(size):
        index = jnp.bitwise_xor(me_row, mask)
        for part, target in enumerate((k_old, v_old)):
            copy = pltpu.make_async_copy(
                blocks[mask].at[pl.ds(part * rows, rows), :],
                target.at[pl.ds(pl.multiple_of(index * rows, rows), rows), :],
                sems.at[part, mask],
            )
            copy.start()
            waits.append(copy)
    for copy in waits:
        copy.wait()
    span, total = qkv_ref.shape
    width = total // 3
    last = width - HEAD_DIM
    block = min(256, span)

    def attend(live):
        lane = lax.broadcasted_iota(jnp.int32, (block, 128), 1)
        left = lane < HEAD_DIM

        def heads(q_at, k_at, v_at, lo, wide):
            old_k, old_v = k_old[0:live, pl.ds(lo, wide)], v_old[0:live, pl.ds(lo, wide)]
            for begin in range(0, span, block):
                stop = begin + block
                q = qkv_ref[begin:stop, pl.ds(q_at, wide)]
                k_new = qkv_ref[0:stop, pl.ds(k_at, wide)]
                v_new = qkv_ref[0:stop, pl.ds(v_at, wide)]
                row = begin + lax.broadcasted_iota(jnp.int32, (block, 1), 0)
                limit = jnp.minimum(row + 1, count)
                if wide == 128:
                    zero = jnp.zeros_like(q)
                    stacked = jnp.concatenate(
                        [jnp.where(left, q, zero), jnp.where(left, zero, q)], axis=0
                    )
                    limits = jnp.concatenate([limit, limit], axis=0)
                    got = attend_block(stacked, k_new, v_new, old_k, old_v, limits, length)
                    both = jnp.where(left, got[:block], got[block:])
                else:
                    both = attend_block(q, k_new, v_new, old_k, old_v, limit, length)
                att_scr[begin:stop, pl.ds(lo, wide)] = both.astype(jnp.bfloat16)

        for lo in range(0, last, 128):
            heads(lo, lo + width + HEAD_DIM, lo + 2 * width, lo, 128)

        heads(last, width, 2 * width + last, last, HEAD_DIM)

    @pl.when(length <= rows)
    def _():
        attend(rows)

    @pl.when(length > rows)
    def _():
        attend(size * rows)

    chunk = span // size
    for slot, ref in ((0, keep_ref), (1, send_ref), (2, keep_ref), (3, send_ref)):
        start = pl.multiple_of(jnp.bitwise_xor(me_row, slot) * chunk, chunk)
        at = slot // 2 * chunk
        ref[at : at + chunk, :] = att_scr[pl.ds(start, chunk), :]
    group = lax.div(count - 1, 16)
    rows16 = att_scr[pl.ds(pl.multiple_of(group * 16, 16), 16), :].astype(jnp.float32)
    at16 = lax.broadcasted_iota(jnp.int32, rows16.shape, 0) == count - 1 - group * 16
    row = jnp.sum(jnp.where(at16, rows16, 0.0), axis=0, keepdims=True)
    last_ref[...] = jnp.broadcast_to(row, last_ref.shape).astype(jnp.bfloat16)


NT = (((1,), (1,)), ((), ()))


def last_row_kernel(layout, block_rows, scalars, *refs):
    pieces = len(layout)
    weights = refs[:pieces]
    last_ref, in_ref, out_ref, w_scr, sems = refs[pieces:]
    columns = w_scr.shape[1]
    weights = [ref.at[:, 0:columns] for ref in weights]
    copies = weight_copies(weights, layout, w_scr, sems, scalars[1], block_rows)
    for copy in copies:
        copy.start()
    rows = in_ref.shape[0]
    local = scalars[3] - 1 - scalars[0] * rows
    group = jnp.clip(lax.div(local, 16), 0, rows // 16 - 1)
    rows16 = in_ref[pl.ds(pl.multiple_of(group * 16, 16), 16), :].astype(jnp.float32)
    at16 = lax.broadcasted_iota(jnp.int32, rows16.shape, 0) == local - group * 16
    residual = jnp.sum(jnp.where(at16, rows16, 0.0), axis=0, keepdims=True)
    for copy in copies:
        copy.wait()
    width = last_ref.shape[1]
    here = lax.broadcasted_iota(jnp.int32, (out_ref.shape[0], 256), 0) == lax.rem(scalars[1], 2)
    for tile in range(0, out_ref.shape[1], 256):
        share = lax.dot_general(
            last_ref[...],
            w_scr[tile : tile + 256, 0:width],
            NT,
            preferred_element_type=jnp.float32,
        )
        row = share[0:1] + residual[:, tile : tile + 256]
        out_ref[:, tile : tile + 256] = jnp.where(here, row, 0.0)


def final_rows_kernel(scalars, *refs):
    shares, (gain_ref, table_ref) = refs[:-2], refs[-2:]
    rows = add_all(*[ref[...] for ref in shares]).astype(jnp.bfloat16).astype(jnp.float32)
    rows = rms_scale(rows, gain_ref[...][None]).astype(jnp.bfloat16).astype(jnp.float32)
    at = lax.broadcasted_iota(jnp.int32, table_ref.shape, 0) - lax.div(scalars[1], 2) * 2
    table = jnp.where(at == 0, rows[0:1], jnp.where(at == 1, rows[1:2], 0.0))
    table_ref[...] = table.astype(jnp.bfloat16)


def merge_kernel(*refs):
    stats, out_ref = refs[:-1], refs[-1]
    out_ref[...] = merge_stats(*[ref[...] for ref in stats])


def logprobs_kernel(logits_ref, *refs):
    stats, out_ref = refs[:-1], refs[-1]
    merged = merge_stats(*[ref[...] for ref in stats])
    out_ref[...] = logits_ref[...] - merged[:, :1] - jnp.log(merged[:, 1:])


def project_kernel(layout, block_rows, scalars, *refs):
    pieces = len(layout)
    keep_ref, got_ref, in_ref, own_ref, mate_ref, w_scr, sems = refs[pieces:]
    copies = weight_copies(refs[:pieces], layout, w_scr, sems, scalars[1], block_rows)
    for copy in copies:
        copy.start()
    attended = jnp.concatenate([keep_ref[...], got_ref[...]], axis=1)
    for copy in copies:
        copy.wait()
    chunk = own_ref.shape[0]
    for tile in range(0, own_ref.shape[1], 256):
        to = tile + 256
        total = lax.dot_general(
            attended, w_scr[tile:to, :], NT, preferred_element_type=jnp.float32
        )
        own_ref[:, tile:to] = total[:chunk] + in_ref[:, tile:to].astype(jnp.float32)
        mate_ref[:, tile:to] = total[chunk:].astype(jnp.bfloat16)


def head_kernel(streams, *refs):
    tables, refs = refs[: -streams - 2], refs[-streams - 2 :]
    weights, (logits_ref, stats_ref) = refs[:-2], refs[-2:]
    table = add_all(*[ref[...] for ref in tables])
    step = pl.program_id(0)
    wide = weights[0].shape[1]
    for index, ref in enumerate(weights):
        part = jnp.dot(table, ref[...], preferred_element_type=jnp.float32)
        if wide == logits_ref.shape[1]:
            logits_ref[...] = part
        else:
            start = pl.multiple_of((step * len(weights) + index) * wide, 128)
            logits_ref[:, pl.ds(start, wide)] = part

    @pl.when(step == pl.num_programs(0) - 1)
    def _():
        logits = logits_ref[...]
        top = jnp.max(logits, axis=1, keepdims=True)
        stats_ref[:, 0:1] = top
        stats_ref[:, 1:2] = jnp.sum(jnp.exp(logits - top), axis=1, keepdims=True)


def exchange_all(value, axis, size, bit, combine=None):
    values = [value]
    while bit < size:
        count = min(4, size // bit)
        if len(values) > 1:
            value = combine(*values)
        values = [value] + [
            lax.ppermute(value, axis, xor_pairs(size, bit * index)) for index in range(1, count)
        ]
        bit *= count
    return values


def add_all(*tables):
    return functools.reduce(jnp.add, tables)


def merge_stats(*stats):
    top = functools.reduce(jnp.maximum, [one[:, :1] for one in stats])
    total = add_all(*[one[:, 1:] * jnp.exp(one[:, :1] - top) for one in stats])
    return jnp.concatenate([top, total], axis=1)


def merge(*stats):
    return pl.pallas_call(
        merge_kernel,
        out_shape=jax.ShapeDtypeStruct(stats[0].shape, jnp.float32),
        compiler_params=params(4),
        cost_estimate=FREE,
        name="merge",
    )(*stats)


def on_device(
    n_req,
    n_row,
    hidden_in,
    cache_len,
    new_count,
    key_cache,
    value_cache,
    attn_gain,
    w_query,
    w_key,
    w_value,
    w_out,
    final_gain,
    head_weight,
):
    me_row = lax.axis_index("row")
    me_req = lax.axis_index("req")
    inputs = hidden_in[0]
    rows, model = inputs.shape
    span = rows * n_row
    block_rows, width = w_query.shape
    length, count = cache_len[0], new_count[0]
    scalars = jnp.stack([me_row, me_req, length, count]).astype(jnp.int32)

    normed = pl.pallas_call(
        norm_kernel,
        out_shape=jax.ShapeDtypeStruct(inputs.shape, jnp.bfloat16),
        compiler_params=params(6),
        cost_estimate=FREE,
        name="norm",
    )(inputs, attn_gain)
    last = width - HEAD_DIM
    joined = jnp.concatenate([w_query, w_key[:, last:], w_key[:, :last], w_value], axis=1)

    def cache_for(owner):
        return jnp.concatenate(
            [
                lax.dynamic_slice_in_dim(key_cache[0], owner * width, width, 1),
                lax.dynamic_slice_in_dim(value_cache[0], owner * width, width, 1),
            ],
            axis=0,
        )

    cached_rows = key_cache.shape[1]

    joined = after(joined, normed)
    out_own = w_out.T
    weights = Rows(joined, n_req)
    got = weights.neighbours()
    cosine, sine = rotary_tables(length + jnp.arange(span, dtype=jnp.int32))
    out_next = lax.ppermute(out_own, "row", xor_pairs(n_row, 1))
    out_both = jnp.concatenate([out_own, out_next], axis=1)
    cached = [cache_for(jnp.bitwise_xor(me_row, mask)) for mask in range(n_row)]
    x_ups, x_downs, scalars, cosine, sine, out_both, own_block, *cached = gather_line(
        normed, n_row, scalars, cosine, sine, out_both, *cached
    )
    got, own = together(got, [joined])
    diagonal = weights.diagonal(got)
    others = weights.cores([*own, *got, *diagonal])
    pieces = weights.pieces(got, diagonal, others)
    layout = tuple(piece[1:] for piece in pieces)

    across = lax.ppermute(cached[1], "row", xor_pairs(n_row, 2))
    beside, behind = after_all([cached[0], cached[2]], across, x_ups[-1], x_downs[-1])
    old_blocks = [
        lax.ppermute(beside, "row", xor_pairs(n_row, 1)),
        across,
        lax.ppermute(behind, "row", xor_pairs(n_row, 3)),
    ]
    out_rows = Rows(after(out_both, *diagonal), n_req)
    out_got = out_rows.neighbours()
    out_got, out_block = together(out_got, [out_rows.block])
    out_diagonal = out_rows.diagonal(out_got)
    qkv = pl.pallas_call(
        functools.partial(qkv_kernel, n_row, layout, block_rows),
        out_shape=jax.ShapeDtypeStruct((span, 3 * width), jnp.bfloat16),
        in_specs=[SMEM] + [HBM] * (2 * n_row - 1 + len(pieces)) + [VMEM] * 2,
        out_specs=VMEM,
        scratch_shapes=[
            pltpu.VMEM((span, model), jnp.bfloat16),
            pltpu.VMEM((model, 3 * width), jnp.bfloat16),
            pltpu.SemaphoreType.DMA((n_row,)),
            pltpu.SemaphoreType.DMA((len(pieces),)),
        ],
        compiler_params=params(17),
        cost_estimate=pl.CostEstimate(
            flops=6 * span * model * width, bytes_accessed=14 * 2**20, transcendentals=0
        ),
        name="qkv",
    )(scalars, normed, *x_ups, *x_downs, *[piece[0] for piece in pieces], cosine, sine)

    out_here, old_blocks, _ = together([*out_block, *out_got, *out_diagonal], old_blocks, [qkv])
    out_others = out_rows.cores(out_here)
    out_pieces = out_rows.pieces(out_got, out_diagonal, out_others)

    chunk = span // n_row
    keep, send, last_attended = pl.pallas_call(
        functools.partial(attention_kernel, n_row),
        out_shape=(
            jax.ShapeDtypeStruct((2 * chunk, width), jnp.bfloat16),
            jax.ShapeDtypeStruct((2 * chunk, width), jnp.bfloat16),
            jax.ShapeDtypeStruct((16, width), jnp.bfloat16),
        ),
        in_specs=[SMEM] + [HBM] * (1 + len(old_blocks)) + [VMEM],
        out_specs=(VMEM, VMEM, VMEM),
        scratch_shapes=[
            pltpu.VMEM((cached_rows * n_row, width), jnp.bfloat16),
            pltpu.VMEM((cached_rows * n_row, width), jnp.bfloat16),
            pltpu.VMEM((span, width), jnp.bfloat16),
            pltpu.SemaphoreType.DMA((2, n_row)),
        ],
        compiler_params=params(18),
        cost_estimate=pl.CostEstimate(
            flops=6 * span * span * width, bytes_accessed=4 * 2**20, transcendentals=0
        ),
        name="attention",
    )(scalars, own_block, *old_blocks, qkv)

    out_layout = tuple(piece[1:] for piece in out_pieces)
    out_weights = [piece[0] for piece in out_pieces]
    own_columns = -(-width // 128) * 128
    share = pl.pallas_call(
        functools.partial(last_row_kernel, out_layout, block_rows),
        out_shape=jax.ShapeDtypeStruct((2, model), jnp.float32),
        in_specs=[SMEM] + [HBM] * len(out_weights) + [VMEM] * 2,
        out_specs=VMEM,
        scratch_shapes=[
            pltpu.VMEM((model, own_columns), jnp.bfloat16),
            pltpu.SemaphoreType.DMA((len(out_weights),)),
        ],
        compiler_params=params(7),
        cost_estimate=FREE,
        name="last_row",
    )(scalars, *out_weights, last_attended, inputs)

    pair = lax.ppermute(share, "req", xor_pairs(n_req, 1))
    share = share + pair
    shares = [share] + [
        lax.ppermute(share, "row", xor_pairs(n_row, mask)) for mask in range(1, n_row)
    ]

    got = after(lax.ppermute(send, "row", xor_pairs(n_row, 1)), share)
    own_sum, mate_part = pl.pallas_call(
        functools.partial(project_kernel, out_layout, block_rows),
        out_shape=(
            jax.ShapeDtypeStruct((chunk, model), jnp.float32),
            jax.ShapeDtypeStruct((chunk, model), jnp.bfloat16),
        ),
        in_specs=[SMEM] + [HBM] * len(out_weights) + [VMEM] * 3,
        out_specs=(VMEM, VMEM),
        scratch_shapes=[
            pltpu.VMEM((model, 2 * width), jnp.bfloat16),
            pltpu.SemaphoreType.DMA((len(out_weights),)),
        ],
        compiler_params=params(11),
        cost_estimate=pl.CostEstimate(
            flops=2 * span * model * width, bytes_accessed=8 * 2**20, transcendentals=0
        ),
        name="project",
    )(scalars, *out_weights, keep, got, inputs)
    mate_part, *shares = lax.optimization_barrier((mate_part, *shares))
    others = lax.ppermute(mate_part, "row", xor_pairs(n_row, 2))
    layer_rows = (own_sum + others.astype(jnp.float32)).astype(jnp.bfloat16)

    table = pl.pallas_call(
        final_rows_kernel,
        out_shape=jax.ShapeDtypeStruct((n_req, model), jnp.bfloat16),
        in_specs=[SMEM] + [VMEM] * (n_row + 1),
        out_specs=VMEM,
        compiler_params=params(4),
        cost_estimate=FREE,
        name="final_rows",
    )(scalars, *shares, final_gain)
    tables = exchange_all(table, "req", n_req, 2, add_all)
    vocab = head_weight.shape[1]
    wide, streams = 256, 5
    if vocab % (wide * streams):
        wide, streams = vocab, 1

    def columns(index):
        return pl.BlockSpec((model, wide), lambda step: (0, step * streams + index))

    logits, stats = pl.pallas_call(
        functools.partial(head_kernel, streams),
        grid=(vocab // (wide * streams),),
        out_shape=(
            jax.ShapeDtypeStruct((n_req, vocab), jnp.float32),
            jax.ShapeDtypeStruct((n_req, 2), jnp.float32),
        ),
        in_specs=[
            *[pl.BlockSpec((n_req, model), lambda step: (0, 0))] * len(tables),
            *[columns(index) for index in range(streams)],
        ],
        out_specs=(
            pl.BlockSpec((n_req, vocab), lambda step: (0, 0)),
            pl.BlockSpec((n_req, 2), lambda step: (0, 0)),
        ),
        compiler_params=params(48),
        cost_estimate=FREE,
        name="head",
    )(*tables, *[head_weight] * streams)
    stats = merge(*exchange_all(stats, "req", n_req, 2, merge))
    stats = merge(stats, lax.ppermute(stats, "req", xor_pairs(n_req, 1)))
    stats = exchange_all(after(stats, others), "row", n_row, 1, merge)
    logprobs = pl.pallas_call(
        logprobs_kernel,
        out_shape=jax.ShapeDtypeStruct(logits.shape, jnp.float32),
        compiler_params=params(4),
        cost_estimate=FREE,
        name="logprobs",
    )(logits, *stats)
    return (layer_rows[None], logprobs)


def solution(mesh):
    placed = (
        P("req", "row", None),
        P("req"),
        P("req"),
        P("req", "row", None),
        P("req", "row", None),
        P(),
        P("req", "row"),
        P("req", "row"),
        P("req", "row"),
        P("row", "req"),
        P(),
        P(None, ("req", "row")),
    )
    return jax.shard_map(
        functools.partial(on_device, mesh.shape["req"], mesh.shape["row"]),
        mesh=mesh,
        in_specs=placed,
        out_specs=(P("req", "row", None), P(None, ("req", "row"))),
        check_vma=False,
    )
```

```python
import functools

import jax
import jax.numpy as jnp
from jax import lax
from jax.experimental import pallas as pl
from jax.experimental.pallas import tpu as pltpu
from jax.sharding import PartitionSpec as P

HEAD_DIM = 64
EPSILON = 1e-05
HBM = pl.BlockSpec(memory_space=pltpu.HBM)
SMEM = pl.BlockSpec(memory_space=pltpu.SMEM)
VMEM = pl.BlockSpec(memory_space=pltpu.VMEM)


def params(mib):
    return pltpu.CompilerParams(vmem_limit_bytes=mib * 1024 * 1024)


FREE = pl.CostEstimate(flops=0, bytes_accessed=0, transcendentals=0)


def rms_scale(values, gain_vec):
    return (
        values * lax.rsqrt(jnp.mean(values * values, axis=-1, keepdims=True) + EPSILON) * gain_vec
    )


def rotary_tables(places):
    half_dim = HEAD_DIM // 2
    frequency = 10000.0 ** (-jnp.arange(half_dim).astype(jnp.float32) / half_dim)
    angles = places.astype(jnp.float32)[:, None] * frequency[None, :]
    cosine, sine = jnp.cos(angles), jnp.sin(angles)
    return (
        jnp.concatenate([cosine] * 4, axis=1),
        jnp.concatenate([-sine, sine, -sine, sine], axis=1),
    )


def up_pairs(size, hop, first=0):
    return [(i, i + hop) for i in range(first, size - hop)]


def down_pairs(size, hop, last=None):
    last = size - 1 if last is None else last
    return [(i, i - hop) for i in range(hop, last + 1)]


def xor_pairs(size, bit):
    return [(i, i ^ bit) for i in range(size)]


def after(value, *earlier):
    return lax.optimization_barrier((value, *earlier))[0]


class Rows:
    def __init__(self, block, size):
        self.block, self.size, self.rows = block, size, block.shape[0]
        self.half = self.rows // 2

    def send(self, array, mask):
        return lax.ppermute(array, "req", xor_pairs(self.size, mask))

    def neighbours(self):
        if self.size != 8:
            return [lax.all_gather(self.block, "req", axis=0, tiled=True)]
        return [self.send(self.block, 2), self.send(self.block, 4)]

    def diagonal(self, got):
        if self.size != 8:
            return []
        half_x, half_y = lax.optimization_barrier((got[0][self.half :], got[1][: self.half]))
        return [self.send(half_y, 2), self.send(half_x, 4)]

    def cores(self, arrays):
        return [self.send(array, 1) for array in arrays] if self.size == 8 else []

    def pieces(self, got, diagonal, others):
        if self.size != 8:
            return [(got[0], None, 0, self.rows * self.size)]
        places = [
            (0, 0, self.rows),
            (2, 0, self.rows),
            (4, 0, self.rows),
            (6, 0, self.half),
            (6, self.half, self.half),
        ]
        pieces = []
        for here, there, (mask, at, count) in zip(
            [self.block, *got, *diagonal], others, places, strict=True
        ):
            pieces += [(here, mask, at, count), (there, mask ^ 1, at, count)]
        return pieces


def after_all(values, *earlier):
    return list(lax.optimization_barrier((*values, *earlier)))[: len(values)]


def gather_line(block, size, *ready):
    ups, downs = [], []
    up, down = block, block
    for step in range(1, size):
        up = lax.ppermute(up, "row", up_pairs(size, 1, step - 1))
        down = lax.ppermute(down, "row", down_pairs(size, 1, size - step))
        if step == size - 2:
            up, down, *ready = lax.optimization_barrier((up, down, *ready))
        else:
            up, down = lax.optimization_barrier((up, down))
        ups.append(up)
        downs.append(down)
    return ups, downs, *ready


def together(*groups):
    flat = lax.optimization_barrier(tuple(array for group in groups for array in group))
    result, at = [], 0
    for group in groups:
        result.append(list(flat[at : at + len(group)]))
        at += len(group)
    return result


def weight_copies(refs, layout, target, sems, me_req, block_rows):
    copies = []
    for index, (ref, (mask, first, count)) in enumerate(zip(refs, layout)):
        if mask is None:
            start = 0
        else:
            start = pl.multiple_of(jnp.bitwise_xor(me_req, mask) * block_rows + first, 16)
        copies.append(pltpu.make_async_copy(ref, target.at[pl.ds(start, count), :], sems.at[index]))
    return copies


def start_line_copies(own, ups, downs, target, sems, me_row, rows):
    size = len(ups) + 1
    waits = []
    own_copy = pltpu.make_async_copy(own, target.at[pl.ds(me_row * rows, rows), :], sems.at[0])
    own_copy.start()
    waits.append(own_copy)
    for hop in range(1, size):
        index = lax.rem(me_row - hop + size, size)
        place = target.at[pl.ds(pl.multiple_of(index * rows, rows), rows), :]
        below = pltpu.make_async_copy(ups[hop - 1], place, sems.at[hop])
        above = pltpu.make_async_copy(downs[size - hop - 1], place, sems.at[hop])

        @pl.when(me_row >= hop)
        def _(below=below):
            below.start()

        @pl.when(me_row < hop)
        def _(above=above):
            above.start()

        waits.append(below)
    return waits


def norm_kernel(in_ref, gain_ref, out_ref):
    rows = rms_scale(in_ref[...].astype(jnp.float32), gain_ref[...][None])
    out_ref[...] = rows.astype(jnp.bfloat16)


def qkv_kernel(size, layout, block_rows, scalars, *refs):
    pieces = len(layout)
    own, ups, downs = refs[0], refs[1:size], refs[size : 2 * size - 1]
    weights = refs[2 * size - 1 : 2 * size - 1 + pieces]
    cos_ref, sin_ref, out_ref, x_scr, w_scr, x_sems, w_sems = refs[2 * size - 1 + pieces :]
    rows = own.shape[0]
    total = out_ref.shape[1]
    copies = weight_copies(weights, layout, w_scr, w_sems, scalars[1], block_rows)
    for copy in copies:
        copy.start()
    waits = start_line_copies(own, ups, downs, x_scr, x_sems, scalars[0], rows)
    for copy in waits + copies:
        copy.wait()
    span = x_scr.shape[0]
    width = total // 3
    half = HEAD_DIM // 2
    lane = lax.broadcasted_iota(jnp.int32, (span, 128), 1)
    first_half = lax.rem(lane, HEAD_DIM) < half
    cosine, sine = cos_ref[...], sin_ref[...]
    for tile in range(0, total, 256):
        end = min(tile + 256, total)
        raw = jnp.dot(x_scr[...], w_scr[:, tile:end], preferred_element_type=jnp.float32)
        for at in range(tile, end, 128):
            stop = min(at + 128, end)
            part = raw[:, at - tile : stop - tile]
            if at < 2 * width:
                swapped = jnp.where(
                    first_half, pltpu.roll(part, 128 - half, 1), pltpu.roll(part, half, 1)
                )
                part = part * cosine + swapped * sine
                if stop <= width:
                    part = part * (HEAD_DIM**-0.5)
                elif at < width:
                    part = jnp.where(lane < width - at, part * (HEAD_DIM**-0.5), part)
            out_ref[:, at:stop] = part.astype(jnp.bfloat16)


def attend_block(q, k_new, v_new, k_old, v_old, limit_new, length):
    nt = (((1,), (1,)), ((), ()))
    s_new = lax.dot_general(q, k_new, nt, preferred_element_type=jnp.float32)
    s_old = lax.dot_general(q, k_old, nt, preferred_element_type=jnp.float32)
    pos_new = lax.broadcasted_iota(jnp.int32, s_new.shape, 1)
    pos_old = lax.broadcasted_iota(jnp.int32, s_old.shape, 1)
    s_new = jnp.where(pos_new < limit_new, s_new, -jnp.inf)
    s_old = jnp.where(pos_old < length, s_old, -jnp.inf)
    top = jnp.maximum(
        jnp.max(s_new, axis=1, keepdims=True), jnp.max(s_old, axis=1, keepdims=True)
    )
    e_new = jnp.exp(s_new - top)
    e_old = jnp.exp(s_old - top)
    total = jnp.sum(e_new, axis=1, keepdims=True) + jnp.sum(e_old, axis=1, keepdims=True)
    summed = jnp.dot(e_new.astype(jnp.bfloat16), v_new, preferred_element_type=jnp.float32)
    summed += jnp.dot(e_old.astype(jnp.bfloat16), v_old, preferred_element_type=jnp.float32)
    return summed / total


def attention_kernel(size, scalars, *refs):
    blocks = refs[:size]
    qkv_ref, keep_ref, send_ref, last_ref, k_old, v_old, att_scr, sems = refs[size:]
    rows = blocks[0].shape[0] // 2
    me_row, length, count = scalars[0], scalars[2], scalars[3]
    waits = []
    for mask in range(size):
        index = jnp.bitwise_xor(me_row, mask)
        for part, target in enumerate((k_old, v_old)):
            copy = pltpu.make_async_copy(
                blocks[mask].at[pl.ds(part * rows, rows), :],
                target.at[pl.ds(pl.multiple_of(index * rows, rows), rows), :],
                sems.at[part, mask],
            )
            copy.start()
            waits.append(copy)
    for copy in waits:
        copy.wait()
    span, total = qkv_ref.shape
    width = total // 3
    last = width - HEAD_DIM
    block = min(256, span)

    def attend(live):
        lane = lax.broadcasted_iota(jnp.int32, (block, 128), 1)
        left = lane < HEAD_DIM

        def heads(q_at, k_at, v_at, lo, wide):
            old_k, old_v = k_old[0:live, pl.ds(lo, wide)], v_old[0:live, pl.ds(lo, wide)]
            for begin in range(0, span, block):
                stop = begin + block
                q = qkv_ref[begin:stop, pl.ds(q_at, wide)]
                k_new = qkv_ref[0:stop, pl.ds(k_at, wide)]
                v_new = qkv_ref[0:stop, pl.ds(v_at, wide)]
                row = begin + lax.broadcasted_iota(jnp.int32, (block, 1), 0)
                limit = jnp.minimum(row + 1, count)
                if wide == 128:
                    zero = jnp.zeros_like(q)
                    stacked = jnp.concatenate(
                        [jnp.where(left, q, zero), jnp.where(left, zero, q)], axis=0
                    )
                    limits = jnp.concatenate([limit, limit], axis=0)
                    got = attend_block(stacked, k_new, v_new, old_k, old_v, limits, length)
                    both = jnp.where(left, got[:block], got[block:])
                else:
                    both = attend_block(q, k_new, v_new, old_k, old_v, limit, length)
                att_scr[begin:stop, pl.ds(lo, wide)] = both.astype(jnp.bfloat16)

        for lo in range(0, last, 128):
            heads(lo, lo + width + HEAD_DIM, lo + 2 * width, lo, 128)

        heads(last, width, 2 * width + last, last, HEAD_DIM)

    @pl.when(length <= rows)
    def _():
        attend(rows)

    @pl.when(length > rows)
    def _():
        attend(size * rows)

    chunk = span // size
    for slot, ref in ((0, keep_ref), (1, send_ref), (2, keep_ref), (3, send_ref)):
        start = pl.multiple_of(jnp.bitwise_xor(me_row, slot) * chunk, chunk)
        at = slot // 2 * chunk
        ref[at : at + chunk, :] = att_scr[pl.ds(start, chunk), :]
    group = lax.div(count - 1, 16)
    rows16 = att_scr[pl.ds(pl.multiple_of(group * 16, 16), 16), :].astype(jnp.float32)
    at16 = lax.broadcasted_iota(jnp.int32, rows16.shape, 0) == count - 1 - group * 16
    row = jnp.sum(jnp.where(at16, rows16, 0.0), axis=0, keepdims=True)
    last_ref[...] = jnp.broadcast_to(row, last_ref.shape).astype(jnp.bfloat16)


NT = (((1,), (1,)), ((), ()))


def last_row_kernel(layout, block_rows, scalars, *refs):
    pieces = len(layout)
    weights = refs[:pieces]
    last_ref, in_ref, out_ref, w_scr, sems = refs[pieces:]
    columns = w_scr.shape[1]
    weights = [ref.at[:, 0:columns] for ref in weights]
    copies = weight_copies(weights, layout, w_scr, sems, scalars[1], block_rows)
    for copy in copies:
        copy.start()
    rows = in_ref.shape[0]
    local = scalars[3] - 1 - scalars[0] * rows
    group = jnp.clip(lax.div(local, 16), 0, rows // 16 - 1)
    rows16 = in_ref[pl.ds(pl.multiple_of(group * 16, 16), 16), :].astype(jnp.float32)
    at16 = lax.broadcasted_iota(jnp.int32, rows16.shape, 0) == local - group * 16
    residual = jnp.sum(jnp.where(at16, rows16, 0.0), axis=0, keepdims=True)
    for copy in copies:
        copy.wait()
    width = last_ref.shape[1]
    here = lax.broadcasted_iota(jnp.int32, (out_ref.shape[0], 256), 0) == lax.rem(scalars[1], 2)
    for tile in range(0, out_ref.shape[1], 256):
        share = lax.dot_general(
            last_ref[...],
            w_scr[tile : tile + 256, 0:width],
            NT,
            preferred_element_type=jnp.float32,
        )
        row = share[0:1] + residual[:, tile : tile + 256]
        out_ref[:, tile : tile + 256] = jnp.where(here, row, 0.0)


def final_rows_kernel(scalars, *refs):
    shares, (gain_ref, table_ref) = refs[:-2], refs[-2:]
    rows = add_all(*[ref[...] for ref in shares]).astype(jnp.bfloat16).astype(jnp.float32)
    rows = rms_scale(rows, gain_ref[...][None]).astype(jnp.bfloat16).astype(jnp.float32)
    at = lax.broadcasted_iota(jnp.int32, table_ref.shape, 0) - lax.div(scalars[1], 2) * 2
    table = jnp.where(at == 0, rows[0:1], jnp.where(at == 1, rows[1:2], 0.0))
    table_ref[...] = table.astype(jnp.bfloat16)


def merge_kernel(*refs):
    stats, out_ref = refs[:-1], refs[-1]
    out_ref[...] = merge_stats(*[ref[...] for ref in stats])


def logprobs_kernel(logits_ref, *refs):
    stats, out_ref = refs[:-1], refs[-1]
    merged = merge_stats(*[ref[...] for ref in stats])
    out_ref[...] = logits_ref[...] - merged[:, :1] - jnp.log(merged[:, 1:])


def project_kernel(layout, block_rows, scalars, *refs):
    pieces = len(layout)
    keep_ref, got_ref, in_ref, own_ref, mate_ref, w_scr, sems = refs[pieces:]
    copies = weight_copies(refs[:pieces], layout, w_scr, sems, scalars[1], block_rows)
    for copy in copies:
        copy.start()
    attended = jnp.concatenate([keep_ref[...], got_ref[...]], axis=1)
    for copy in copies:
        copy.wait()
    chunk = own_ref.shape[0]
    for tile in range(0, own_ref.shape[1], 256):
        to = tile + 256
        total = lax.dot_general(
            attended, w_scr[tile:to, :], NT, preferred_element_type=jnp.float32
        )
        own_ref[:, tile:to] = total[:chunk] + in_ref[:, tile:to].astype(jnp.float32)
        mate_ref[:, tile:to] = total[chunk:].astype(jnp.bfloat16)


def head_kernel(streams, *refs):
    tables, refs = refs[: -streams - 2], refs[-streams - 2 :]
    weights, (logits_ref, stats_ref) = refs[:-2], refs[-2:]
    table = add_all(*[ref[...] for ref in tables])
    step = pl.program_id(0)
    wide = weights[0].shape[1]
    for index, ref in enumerate(weights):
        part = jnp.dot(table, ref[...], preferred_element_type=jnp.float32)
        if wide == logits_ref.shape[1]:
            logits_ref[...] = part
        else:
            start = pl.multiple_of((step * len(weights) + index) * wide, 128)
            logits_ref[:, pl.ds(start, wide)] = part

    @pl.when(step == pl.num_programs(0) - 1)
    def _():
        logits = logits_ref[...]
        top = jnp.max(logits, axis=1, keepdims=True)
        stats_ref[:, 0:1] = top
        stats_ref[:, 1:2] = jnp.sum(jnp.exp(logits - top), axis=1, keepdims=True)


def exchange_all(value, axis, size, bit, combine=None):
    values = [value]
    while bit < size:
        count = min(4, size // bit)
        if len(values) > 1:
            value = combine(*values)
        values = [value] + [
            lax.ppermute(value, axis, xor_pairs(size, bit * index)) for index in range(1, count)
        ]
        bit *= count
    return values


def add_all(*tables):
    return functools.reduce(jnp.add, tables)


def merge_stats(*stats):
    top = functools.reduce(jnp.maximum, [one[:, :1] for one in stats])
    total = add_all(*[one[:, 1:] * jnp.exp(one[:, :1] - top) for one in stats])
    return jnp.concatenate([top, total], axis=1)


def merge(*stats):
    return pl.pallas_call(
        merge_kernel,
        out_shape=jax.ShapeDtypeStruct(stats[0].shape, jnp.float32),
        compiler_params=params(4),
        cost_estimate=FREE,
        name="merge",
    )(*stats)


def on_device(
    n_req,
    n_row,
    hidden_in,
    cache_len,
    new_count,
    key_cache,
    value_cache,
    attn_gain,
    w_query,
    w_key,
    w_value,
    w_out,
    final_gain,
    head_weight,
):
    me_row = lax.axis_index("row")
    me_req = lax.axis_index("req")
    inputs = hidden_in[0]
    rows, model = inputs.shape
    span = rows * n_row
    block_rows, width = w_query.shape
    length, count = cache_len[0], new_count[0]
    scalars = jnp.stack([me_row, me_req, length, count]).astype(jnp.int32)

    normed = pl.pallas_call(
        norm_kernel,
        out_shape=jax.ShapeDtypeStruct(inputs.shape, jnp.bfloat16),
        compiler_params=params(6),
        cost_estimate=FREE,
        name="norm",
    )(inputs, attn_gain)
    last = width - HEAD_DIM
    joined = jnp.concatenate([w_query, w_key[:, last:], w_key[:, :last], w_value], axis=1)

    def cache_for(owner):
        return jnp.concatenate(
            [
                lax.dynamic_slice_in_dim(key_cache[0], owner * width, width, 1),
                lax.dynamic_slice_in_dim(value_cache[0], owner * width, width, 1),
            ],
            axis=0,
        )

    cached_rows = key_cache.shape[1]

    joined = after(joined, normed)
    out_own = w_out.T
    weights = Rows(joined, n_req)
    got = weights.neighbours()
    cosine, sine = rotary_tables(length + jnp.arange(span, dtype=jnp.int32))
    out_next = lax.ppermute(out_own, "row", xor_pairs(n_row, 1))
    out_both = jnp.concatenate([out_own, out_next], axis=1)
    cached = [cache_for(jnp.bitwise_xor(me_row, mask)) for mask in range(n_row)]
    x_ups, x_downs, scalars, cosine, sine, out_both, own_block, *cached = gather_line(
        normed, n_row, scalars, cosine, sine, out_both, *cached
    )
    got, own = together(got, [joined])
    diagonal = weights.diagonal(got)
    others = weights.cores([*own, *got, *diagonal])
    pieces = weights.pieces(got, diagonal, others)
    layout = tuple(piece[1:] for piece in pieces)

    across = lax.ppermute(cached[1], "row", xor_pairs(n_row, 2))
    beside, behind = after_all([cached[0], cached[2]], across, x_ups[-1], x_downs[-1])
    old_blocks = [
        lax.ppermute(beside, "row", xor_pairs(n_row, 1)),
        across,
        lax.ppermute(behind, "row", xor_pairs(n_row, 3)),
    ]
    out_rows = Rows(after(out_both, *diagonal), n_req)
    out_got = out_rows.neighbours()
    out_got, out_block = together(out_got, [out_rows.block])
    out_diagonal = out_rows.diagonal(out_got)
    qkv = pl.pallas_call(
        functools.partial(qkv_kernel, n_row, layout, block_rows),
        out_shape=jax.ShapeDtypeStruct((span, 3 * width), jnp.bfloat16),
        in_specs=[SMEM] + [HBM] * (2 * n_row - 1 + len(pieces)) + [VMEM] * 2,
        out_specs=VMEM,
        scratch_shapes=[
            pltpu.VMEM((span, model), jnp.bfloat16),
            pltpu.VMEM((model, 3 * width), jnp.bfloat16),
            pltpu.SemaphoreType.DMA((n_row,)),
            pltpu.SemaphoreType.DMA((len(pieces),)),
        ],
        compiler_params=params(17),
        cost_estimate=pl.CostEstimate(
            flops=6 * span * model * width, bytes_accessed=14 * 2**20, transcendentals=0
        ),
        name="qkv",
    )(scalars, normed, *x_ups, *x_downs, *[piece[0] for piece in pieces], cosine, sine)

    out_here, old_blocks, _ = together([*out_block, *out_got, *out_diagonal], old_blocks, [qkv])
    out_others = out_rows.cores(out_here)
    out_pieces = out_rows.pieces(out_got, out_diagonal, out_others)

    chunk = span // n_row
    keep, send, last_attended = pl.pallas_call(
        functools.partial(attention_kernel, n_row),
        out_shape=(
            jax.ShapeDtypeStruct((2 * chunk, width), jnp.bfloat16),
            jax.ShapeDtypeStruct((2 * chunk, width), jnp.bfloat16),
            jax.ShapeDtypeStruct((16, width), jnp.bfloat16),
        ),
        in_specs=[SMEM] + [HBM] * (1 + len(old_blocks)) + [VMEM],
        out_specs=(VMEM, VMEM, VMEM),
        scratch_shapes=[
            pltpu.VMEM((cached_rows * n_row, width), jnp.bfloat16),
            pltpu.VMEM((cached_rows * n_row, width), jnp.bfloat16),
            pltpu.VMEM((span, width), jnp.bfloat16),
            pltpu.SemaphoreType.DMA((2, n_row)),
        ],
        compiler_params=params(18),
        cost_estimate=pl.CostEstimate(
            flops=6 * span * span * width, bytes_accessed=4 * 2**20, transcendentals=0
        ),
        name="attention",
    )(scalars, own_block, *old_blocks, qkv)

    out_layout = tuple(piece[1:] for piece in out_pieces)
    out_weights = [piece[0] for piece in out_pieces]
    own_columns = -(-width // 128) * 128
    share = pl.pallas_call(
        functools.partial(last_row_kernel, out_layout, block_rows),
        out_shape=jax.ShapeDtypeStruct((2, model), jnp.float32),
        in_specs=[SMEM] + [HBM] * len(out_weights) + [VMEM] * 2,
        out_specs=VMEM,
        scratch_shapes=[
            pltpu.VMEM((model, own_columns), jnp.bfloat16),
            pltpu.SemaphoreType.DMA((len(out_weights),)),
        ],
        compiler_params=params(7),
        cost_estimate=FREE,
        name="last_row",
    )(scalars, *out_weights, last_attended, inputs)

    pair = lax.ppermute(share, "req", xor_pairs(n_req, 1))
    share = share + pair
    shares = [share] + [
        lax.ppermute(share, "row", xor_pairs(n_row, mask)) for mask in range(1, n_row)
    ]

    got = after(lax.ppermute(send, "row", xor_pairs(n_row, 1)), share)
    own_sum, mate_part = pl.pallas_call(
        functools.partial(project_kernel, out_layout, block_rows),
        out_shape=(
            jax.ShapeDtypeStruct((chunk, model), jnp.float32),
            jax.ShapeDtypeStruct((chunk, model), jnp.bfloat16),
        ),
        in_specs=[SMEM] + [HBM] * len(out_weights) + [VMEM] * 3,
        out_specs=(VMEM, VMEM),
        scratch_shapes=[
            pltpu.VMEM((model, 2 * width), jnp.bfloat16),
            pltpu.SemaphoreType.DMA((len(out_weights),)),
        ],
        compiler_params=params(11),
        cost_estimate=pl.CostEstimate(
            flops=2 * span * model * width, bytes_accessed=8 * 2**20, transcendentals=0
        ),
        name="project",
    )(scalars, *out_weights, keep, got, inputs)
    mate_part, *shares = lax.optimization_barrier((mate_part, *shares))
    others = lax.ppermute(mate_part, "row", xor_pairs(n_row, 2))
    layer_rows = (own_sum + others.astype(jnp.float32)).astype(jnp.bfloat16)

    table = pl.pallas_call(
        final_rows_kernel,
        out_shape=jax.ShapeDtypeStruct((n_req, model), jnp.bfloat16),
        in_specs=[SMEM] + [VMEM] * (n_row + 1),
        out_specs=VMEM,
        compiler_params=params(4),
        cost_estimate=FREE,
        name="final_rows",
    )(scalars, *shares, final_gain)
    tables = exchange_all(table, "req", n_req, 2, add_all)
    vocab = head_weight.shape[1]
    wide, streams = 256, 5
    if vocab % (wide * streams):
        wide, streams = vocab, 1

    def columns(index):
        return pl.BlockSpec((model, wide), lambda step: (0, step * streams + index))

    logits, stats = pl.pallas_call(
        functools.partial(head_kernel, streams),
        grid=(vocab // (wide * streams),),
        out_shape=(
            jax.ShapeDtypeStruct((n_req, vocab), jnp.float32),
            jax.ShapeDtypeStruct((n_req, 2), jnp.float32),
        ),
        in_specs=[
            *[pl.BlockSpec((n_req, model), lambda step: (0, 0))] * len(tables),
            *[columns(index) for index in range(streams)],
        ],
        out_specs=(
            pl.BlockSpec((n_req, vocab), lambda step: (0, 0)),
            pl.BlockSpec((n_req, 2), lambda step: (0, 0)),
        ),
        compiler_params=params(48),
        cost_estimate=FREE,
        name="head",
    )(*tables, *[head_weight] * streams)
    stats = merge(*exchange_all(stats, "req", n_req, 2, merge))
    stats = merge(stats, lax.ppermute(stats, "req", xor_pairs(n_req, 1)))
    later = after(stats, others)
    stats = [stats, lax.ppermute(stats, "row", xor_pairs(n_row, 1))] + [
        lax.ppermute(later, "row", xor_pairs(n_row, mask)) for mask in range(2, n_row)
    ]
    logprobs = pl.pallas_call(
        logprobs_kernel,
        out_shape=jax.ShapeDtypeStruct(logits.shape, jnp.float32),
        compiler_params=params(4),
        cost_estimate=FREE,
        name="logprobs",
    )(logits, *stats)
    return (layer_rows[None], logprobs)


def solution(mesh):
    placed = (
        P("req", "row", None),
        P("req"),
        P("req"),
        P("req", "row", None),
        P("req", "row", None),
        P(),
        P("req", "row"),
        P("req", "row"),
        P("req", "row"),
        P("row", "req"),
        P(),
        P(None, ("req", "row")),
    )
    return jax.shard_map(
        functools.partial(on_device, mesh.shape["req"], mesh.shape["row"]),
        mesh=mesh,
        in_specs=placed,
        out_specs=(P("req", "row", None), P(None, ("req", "row"))),
        check_vma=False,
    )
```
